128 devices in a mesh: section: 2 (over z_hi), dp: 64 (over y, z_lo, x, core).
Axes of the slice: x: 4, y: 4, z: 4 (z_hi: 2, z_lo: 2; z = z_hi * 2 + z_lo), core: 2. Of those that a mesh axis runs over, the one named last changes fastest.
Arguments:
- tokens: bfloat16 [128, 256, 512], P('dp'), may hold values from -6 to 6
- segments: int32 [128, 256], P('dp'), may hold values from 0 to 7, never falling along the last dimension, each value on 1 to 128 neighbouring positions
- cotangent: bfloat16 [128, 256, 512], P('dp'), may hold values from -6 to 6
- w_query: bfloat16 [2, 512, 512], P('section'), may hold values from -0.25 to 0.25
- q_bias: float32 [2, 512], P('section'), may hold values from -1.5 to 1.5
- w_key: bfloat16 [2, 512, 512], P('section'), may hold values from -0.25 to 0.25
- w_value: bfloat16 [2, 512, 512], P('section'), may hold values from -0.25 to 0.25
- v_bias: float32 [2, 512], P('section'), may hold values from -1.5 to 1.5
- w_out: bfloat16 [2, 512, 512], P('section'), may hold values from -0.5 to 0.5
- out_bias: float32 [2, 512], P('section'), may hold values from -1.5 to 1.5
- ln1_gain: float32 [2, 512], P('section'), may hold values from 0.1 to 1.9
- ln1_shift: float32 [2, 512], P('section'), may hold values from -1.5 to 1.5
- w_up: bfloat16 [2, 512, 2048], P('section'), may hold values from -0.25 to 0.25
- up_bias: float32 [2, 2048], P('section'), may hold values from -1.5 to 1.5
- w_down: bfloat16 [2, 2048, 512], P('section'), may hold values from -0.125 to 0.125
- down_bias: float32 [2, 512], P('section'), may hold values from -1.5 to 1.5
- ln2_gain: float32 [2, 512], P('section'), may hold values from 0.1 to 1.9
- ln2_shift: float32 [2, 512], P('section'), may hold values from -1.5 to 1.5
Outputs:
- layer_outputs: bfloat16 [2, 128, 256, 512], P('section', 'dp')
- input_grads: float32 [2, 128, 256, 512], P('section', 'dp')
- g_query: float32 [2, 512, 512], P('section')
- g_qbias: float32 [2, 512], P('section')
- g_key: float32 [2, 512, 512], P('section')
- g_value: float32 [2, 512, 512], P('section')
- g_vbias: float32 [2, 512], P('section')
- g_out: float32 [2, 512, 512], P('section')
- g_outbias: float32 [2, 512], P('section')
- g_ln1gain: float32 [2, 512], P('section')
- g_ln1shift: float32 [2, 512], P('section')
- g_up: float32 [2, 512, 2048], P('section')
- g_upbias: float32 [2, 2048], P('section')
- g_down: float32 [2, 2048, 512], P('section')
- g_downbias: float32 [2, 512], P('section')
- g_ln2gain: float32 [2, 512], P('section')
- g_ln2shift: float32 [2, 512], P('section')
The draws below stay inside these ranges and needn't reach their ends.
Inputs may be any that keep to these rules, and one draw needn't show every extreme that they name: `segments`: segment numbers never fall along a row; each sentence has 1 to 128 tokens.
All inputs are finite; a program needn't handle non-finite values.
Results may differ from the reference program's by a relative error of at most 0.02.
Values may be sent and summed in bfloat16 or wider, within the bound.
No kernel may reach another device: no remote copies, remote signals or barrier semaphores. Data moves between devices by JAX's collectives and lax.ppermute only.
A program may use at most 128 MiB of HBM per device.

```python
import math
import jax
import jax.numpy as jnp
import numpy as np
from jax import lax

D = 512
HEADS = 8
HEAD = 64
FF = 2048
ROW_LEN = 256
SENTS = 8
ROWS = 128


def levels(key, extent, cuts, low, high):
    factor_of = 1.0
    for axis_at, parts in cuts:
        draws = jax.random.uniform(jax.random.fold_in(jax.random.fold_in(key, 6), axis_at), (parts,), jnp.float32, low / len(cuts), high / len(cuts))
        factor_of = factor_of * jnp.repeat(jnp.exp(draws), extent[axis_at] // parts).reshape((-1,) + (1,) * (len(extent) - 1 - axis_at))
    return factor_of


def profile(number_of, total, bound, lean):
    loads = [(1 << 20) // math.isqrt(rank ** lean) + 1 for rank in range(2, number_of + 1)]
    spare, given = total - bound - (number_of - 1), [1] * (number_of - 1)
    while spare > 0:
        movable = [i for i in range(number_of - 1) if given[i] < bound]
        whole, remaining = sum([loads[i] for i in movable]), spare
        for i in movable:
            extra = min(bound - given[i], max(1, remaining * loads[i] // whole), spare)
            given[i] = given[i] + extra
            spare = spare - extra
    return np.array([bound] + given)


def ragged_sizes(own_key, count, total, reach, slope):
    if count == 2:
        one = jax.random.randint(own_key, (), max(1, total - reach), min(reach, total - 1) + 1)
        return jnp.stack([one, total - one])
    sizes = jnp.asarray(profile(count, total, reach, slope), jnp.int32)
    pairs = (count - 1) // 2
    giver, taker = sizes[1:1 + 2 * pairs:2], sizes[2:2 + 2 * pairs:2]
    slack = jnp.minimum(giver - 1, reach - taker)
    moved = jax.random.randint(jax.random.fold_in(own_key, 1), (pairs,), 0, 1 << 20) % (slack + 1)
    sizes = sizes.at[1:1 + 2 * pairs:2].set(giver - moved).at[2:2 + 2 * pairs:2].set(taker + moved)
    return sizes[jax.random.permutation(jax.random.fold_in(own_key, 2), count)]


def scatter_about(rng, extent, scale, limit, pieces=(), dtype=jnp.bfloat16):
    entries = jax.random.normal(rng, extent, jnp.float32) * scale
    if len(pieces) > 0:
        entries = levels(rng, extent, pieces, -0.22, 0.18) * entries
    return jnp.clip(entries, min=-limit, max=limit).astype(dtype)


def setup_inputs(seed: int = 0) -> dict:
    streams_of = jax.random.split(jax.random.key(seed), 19)
    tokens = scatter_about(streams_of[0], (ROWS, ROW_LEN, D), 1.0, 6.0, ((0, 64),))
    segments = jax.vmap(lambda own: jnp.searchsorted(jnp.cumsum(ragged_sizes(own, SENTS, ROW_LEN, ROW_LEN // 2, 0)), jnp.arange(ROW_LEN), side="right"))(jax.random.split(streams_of[1], ROWS)).reshape((ROWS, ROW_LEN)).astype(jnp.int32)
    cotangent = scatter_about(streams_of[2], (ROWS, ROW_LEN, D), 1.0, 6.0, ((0, 64),))
    w_query = scatter_about(streams_of[3], (2, D, D), D ** -0.5, 0.25, ((0, 2),))
    q_bias = scatter_about(streams_of[4], (2, D), 0.3, 1.5, ((0, 2),), jnp.float32)
    w_key = scatter_about(streams_of[5], (2, D, D), D ** -0.5, 0.25, ((0, 2),))
    w_value = scatter_about(streams_of[6], (2, D, D), D ** -0.5, 0.25, ((0, 2),))
    v_bias = scatter_about(streams_of[7], (2, D), 0.3, 1.5, ((0, 2),), jnp.float32)
    w_out = scatter_about(streams_of[8], (2, D, D), (D // 4) ** -0.5, 0.5, ((0, 2),))
    out_bias = scatter_about(streams_of[9], (2, D), 0.3, 1.5, ((0, 2),), jnp.float32)
    ln1_gain = jnp.clip(1.0 + 0.18 * jax.random.normal(streams_of[10], (2, D), jnp.float32), 0.1, 1.9)
    ln1_shift = scatter_about(streams_of[11], (2, D), 0.3, 1.5, ((0, 2),), jnp.float32)
    w_up = scatter_about(streams_of[12], (2, D, FF), D ** -0.5, 0.25, ((0, 2),))
    up_bias = scatter_about(streams_of[13], (2, FF), 0.3, 1.5, ((0, 2),), jnp.float32)
    w_down = scatter_about(streams_of[14], (2, FF, D), FF ** -0.5, 0.125, ((0, 2),))
    down_bias = scatter_about(streams_of[15], (2, D), 0.3, 1.5, ((0, 2),), jnp.float32)
    ln2_gain = jnp.clip(1.0 + 0.18 * jax.random.normal(streams_of[16], (2, D), jnp.float32), 0.1, 1.9)
    ln2_shift = scatter_about(streams_of[17], (2, D), 0.3, 1.5, ((0, 2),), jnp.float32)
    return {"tokens": tokens, "segments": segments, "cotangent": cotangent, "w_query": w_query, "q_bias": q_bias, "w_key": w_key, "w_value": w_value, "v_bias": v_bias, "w_out": w_out, "out_bias": out_bias, "ln1_gain": ln1_gain, "ln1_shift": ln1_shift, "w_up": w_up, "up_bias": up_bias, "w_down": w_down, "down_bias": down_bias, "ln2_gain": ln2_gain, "ln2_shift": ln2_shift}


@jax.custom_vjp
def low(v):
    return lax.optimization_barrier(v.astype(jnp.bfloat16)).astype(jnp.float32)

@jax.custom_vjp
def low_back(v):
    return v

def low_keep(v):
    return (low(v), None)

def low_pass(kept, grad):
    return (grad,)

def back_keep(v):
    return (v, None)

def back_low(kept, grad):
    return (low(grad),)
low.defvjp(low_keep, low_pass)
low_back.defvjp(back_keep, back_low)

def matmul(a, b):
    return jnp.dot(a, b, precision=lax.Precision.HIGHEST, preferred_element_type=jnp.float32)

def layer_norm(value, gain, shift):
    centre = value - lax.optimization_barrier(jnp.mean(value, -1, keepdims=True))
    spread = lax.optimization_barrier(jnp.mean(centre * centre, -1, keepdims=True))
    return centre * lax.rsqrt(spread + 1e-05) * gain + shift

def layer(hidden, same, params):
    wq, bq, wk, wv, bv, wo, bo, g1, s1, w1, c1, w2, c2, g2, s2 = params
    group = hidden.shape[0]

    def split_heads(value):
        return value.reshape(group, ROW_LEN, HEADS, HEAD)
    query = low_back(low(matmul(hidden, wq) + bq))
    keys = low_back(low(matmul(hidden, wk)))
    values = low_back(low(matmul(hidden, wv) + bv))
    scores = jnp.einsum('gqhe,gkhe->ghqk', split_heads(query), split_heads(keys), precision=lax.Precision.HIGHEST) * HEAD ** (-0.5)
    scores = low_back(jnp.where(same[:, None], scores, -1000000000.0))
    probs = jax.nn.softmax(scores, axis=-1)
    mixed = jnp.einsum('ghqk,gkhe->gqhe', low(probs), split_heads(values), precision=lax.Precision.HIGHEST)
    mixed = low_back(low(mixed.reshape(group, ROW_LEN, D)))
    resid = hidden + low_back(matmul(mixed, wo) + bo)
    normed = layer_norm(resid, g1, s1)
    inner = low_back(matmul(low(normed), w1) + c1)
    branch = low_back(matmul(low(jax.nn.gelu(inner, approximate=True)), w2) + c2)
    return layer_norm(normed + branch, g2, s2)

def reference(tokens, segments, cotangent, w_query, q_bias, w_key, w_value, v_bias, w_out, out_bias, ln1_gain, ln1_shift, w_up, up_bias, w_down, down_bias, ln2_gain, ln2_shift):
    params = [a.astype(jnp.float32) for a in (w_query, q_bias, w_key, w_value, v_bias, w_out, out_bias, ln1_gain, ln1_shift, w_up, up_bias, w_down, down_bias, ln2_gain, ln2_shift)]
    first = tuple((a[0] for a in params))
    second = tuple((a[1] for a in params))
    rows = tokens.shape[0]
    group = math.gcd(rows, max(1, 4096 // ROW_LEN))
    count = rows // group
    inputs = tokens.astype(jnp.float32).reshape(count, group, ROW_LEN, D)
    segs = segments.reshape(count, group, ROW_LEN)
    cots = cotangent.astype(jnp.float32).reshape(count, group, ROW_LEN, D)

    def step(total, block):
        source, seg, cot = block
        same = seg[:, :, None] == seg[:, None, :]

        def forward(source, probe, one, two):
            middle = layer(source, same, one)
            sent = low_back(low(middle)) + probe
            return (layer(sent, same, two), low(middle))
        final, pull, middle = jax.vjp(forward, source, jnp.zeros_like(source), first, second, has_aux=True)
        dsource, dprobe, gone, gtwo = pull(cot)
        total = jax.tree.map(lambda a, b: a + b, total, (gone, gtwo))
        return (total, (middle, final, dsource, dprobe))
    start = jax.tree.map(jnp.zeros_like, (first, second))
    total, outs = lax.scan(step, start, (inputs, segs, cots))
    middle, final, dsource, dprobe = [a.reshape(rows, ROW_LEN, D) for a in outs]
    layer_outputs = jnp.stack([middle, final]).astype(jnp.bfloat16)
    input_grads = jnp.stack([dsource, dprobe]).astype(jnp.float32)
    grads = tuple((jnp.stack([a, b]) for a, b in zip(total[0], total[1])))
    return (layer_outputs, input_grads) + grads
```

```python
import functools

import jax
import jax.numpy as jnp
from jax import lax
from jax.experimental import pallas as pl
from jax.experimental.pallas import tpu as pltpu
from jax.sharding import PartitionSpec as P

BF, F32 = jnp.bfloat16, jnp.float32
ROWS, L, D, FF, HEADS, HEAD = 2, 256, 512, 2048, 8, 64
BLK = 512
NBLK = FF // BLK
VEC = 16
MiB = 1 << 20
SCALE = HEAD ** (-0.5)
BQ, BV, BO, G1, S1, C2, G2, S2, C1 = 0, 1, 2, 3, 4, 5, 6, 7, 8
SEC, CORE, FIRST, SECOND = 0, 1, 2, 3


def nn(a, b):
    return jnp.dot(a, b, preferred_element_type=F32)


def nt(a, b):
    return lax.dot_general(a, b, (((1,), (1,)), ((), ())), preferred_element_type=F32)


def tn(a, b):
    return lax.dot_general(a, b, (((0,), (0,)), ((), ())), preferred_element_type=F32)


class Moves:
    def __init__(self, sems):
        self.sems, self.count, self.left = sems, 0, []

    def start(self, source, target):
        copy = pltpu.make_async_copy(source, target, self.sems.at[self.count])
        self.count += 1
        copy.start()
        return copy

    def out(self, source, target):
        self.left.append(self.start(source, target))

    def drain(self):
        for copy in self.left:
            copy.wait()
        self.left = []


def call(body, name, place, ins, outs, scratch, aliases=None, vmem=48, flops=0, nbytes=0, vmem_outs=()):
    any_spec = pl.BlockSpec(memory_space=pl.ANY)
    vm_spec = pl.BlockSpec(memory_space=pltpu.VMEM)
    return pl.pallas_call(
        body,
        out_shape=[jax.ShapeDtypeStruct(s, t) for s, t in outs],
        in_specs=[pl.BlockSpec(memory_space=pltpu.SMEM)] + [any_spec] * len(ins),
        out_specs=[vm_spec if i in vmem_outs else any_spec for i in range(len(outs))],
        scratch_shapes=[pltpu.VMEM(s, t) for s, t in scratch] + [pltpu.SemaphoreType.DMA((56,))],
        input_output_aliases=aliases or {},
        compiler_params=pltpu.CompilerParams(vmem_limit_bytes=vmem * MiB),
        cost_estimate=pl.CostEstimate(flops=flops, bytes_accessed=nbytes, transcendentals=0),
        name=name,
    )(place, *ins)


def norm_forward(resid, gain, shift):
    centre = resid - jnp.mean(resid, -1, keepdims=True)
    rstd = lax.rsqrt(jnp.mean(centre * centre, -1, keepdims=True) + 1e-05)
    unit = centre * rstd
    return unit, rstd, unit * gain + shift


def norm_backward(grad, unit, rstd, gain):
    scaled = grad * gain
    inner = scaled - jnp.mean(scaled, -1, keepdims=True)
    return rstd * (inner - unit * jnp.mean(scaled * unit, -1, keepdims=True))


def lane_masks():
    lane = lax.broadcasted_iota(jnp.int32, (L, 128), 1)
    low = (lane < HEAD).astype(F32)
    return low.astype(BF), (1.0 - low).astype(BF), lane < HEAD


FSCR = dict(
    vec=((VEC, D), F32),
    seg=((ROWS, L), jnp.int32),
    h=((L, D), BF),
    wq=((D, D), BF),
    wk=((D, D), BF),
    wv=((D, D), BF),
    wo=((D, D), BF),
    w1=((D, FF), BF),
    w2=((FF, D), BF),
    q=((L, D), BF),
    k=((L, D), BF),
    v=((L, D), BF),
    p=((HEADS * L, L), BF),
    o=((L, D), BF),
    u=((L, D), BF),
    a=((L, FF), BF),
    gp=((L, FF), BF),
    x1=((L, D), F32),
    x2=((L, D), F32),
    rs=((L, 256), F32),
    y=((L, D), BF),
)


def forward(s, need, emit, row):
    for name in ("h", "vec", "seg", "wq"):
        need(name)
    hidden = s["h"][...]

    def vec(i):
        return s["vec"][i : i + 1, :]

    s["q"][...] = (nn(hidden, s["wq"][...]) + vec(BQ)).astype(BF)
    emit("q")
    need("wk")
    s["k"][...] = nn(hidden, s["wk"][...]).astype(BF)
    emit("k")
    need("wv")
    s["v"][...] = (nn(hidden, s["wv"][...]) + vec(BV)).astype(BF)
    emit("v")
    seg = jnp.broadcast_to(s["seg"][row : row + 1, :].astype(F32), (L, L))
    same = seg == seg.T
    low, high, is_low = lane_masks()
    for pair in range(HEADS // 2):
        cols = slice(pair * 128, pair * 128 + 128)
        query, keys, values = s["q"][:, cols], s["k"][:, cols], s["v"][:, cols]
        got = []
        for half, mask in enumerate((low, high)):
            at = (2 * pair + half) * L
            scores = jnp.where(same, nt(query * mask, keys) * SCALE, -1000000000.0)
            weight = jnp.exp(scores - jnp.max(scores, -1, keepdims=True))
            probs = (weight * (1.0 / jnp.sum(weight, -1, keepdims=True))).astype(BF)
            s["p"][at : at + L, :] = probs
            got.append(nn(probs, values))
        s["o"][:, cols] = jnp.where(is_low, got[0], got[1]).astype(BF)
    emit("p")
    emit("o")
    need("wo")
    resid = hidden.astype(F32) + nn(s["o"][...], s["wo"][...]) + vec(BO)
    unit, rstd, normed = norm_forward(resid, vec(G1), vec(S1))
    s["x1"][...] = unit
    emit("x1")
    s["rs"][:, :128] = jnp.broadcast_to(rstd, (L, 128))
    s["u"][...] = normed.astype(BF)
    emit("u")
    need("w1")
    need("w2")
    total = normed + vec(C2)
    for j in range(NBLK):
        cols = slice(j * BLK, j * BLK + BLK)
        z = nn(s["u"][...], s["w1"][:, cols]) + vec(C1 + j)
        square = z * z
        tanh = jnp.tanh(0.7978845608028654 * z * (1.0 + 0.044715 * square))
        half = 0.5 * (1.0 + tanh)
        active = (z * half).astype(BF)
        s["a"][:, cols] = active
        slope = half + (z * half) * (1.0 - tanh) * (0.7978845608028654 * (1.0 + 0.134145 * square))
        s["gp"][:, cols] = slope.astype(BF)
        total = total + nn(active, s["w2"][cols, :])
    emit("a")
    emit("gp")
    unit, rstd, out = norm_forward(total, vec(G2), vec(S2))
    s["y"][...] = out.astype(BF)
    emit("y")
    s["x2"][...] = unit
    emit("x2")
    s["rs"][:, 128:] = jnp.broadcast_to(rstd, (L, 128))
    emit("rs")


B1SCR = dict(
    dy=((L, D), BF),
    e2=((L, D), BF),
    e1=((L, FF), BF),
    e0=((L, D), BF),
    r1=((L, D), F32),
    ln=((8, D), F32),
)
B2SCR = dict(
    qt=((D, L), BF),
    dot=((D, L), BF),
    do=((L, D), BF),
    dq=((L, D), BF),
    dkt=((D, L), F32),
    dvt=((D, L), F32),
    dk=((L, D), BF),
    dv=((L, D), BF),
    dh=((L, D), F32),
    ds=((L, D), BF),
)


def backward_feed(s, need, emit):
    need("dy")
    need("vec")
    need("x2")
    need("rs")
    gain1, gain2 = s["vec"][G1 : G1 + 1, :], s["vec"][G2 : G2 + 1, :]
    dout = s["dy"][...].astype(F32)
    unit = s["x2"][...]
    g_gain2 = jnp.sum(dout * unit, 0, keepdims=True)
    g_shift2 = jnp.sum(dout, 0, keepdims=True)
    dsecond = norm_backward(dout, unit, s["rs"][:, 128:129], gain2)
    s["e2"][...] = dsecond.astype(BF)
    emit("e2")
    need("w2")
    need("gp")
    need("w1")
    total = dsecond
    for j in range(NBLK):
        cols = slice(j * BLK, j * BLK + BLK)
        dactive = nt(s["e2"][...], s["w2"][cols, :])
        dinner = (s["gp"][:, cols].astype(F32) * dactive).astype(BF)
        s["e1"][:, cols] = dinner
        total = total + nt(dinner, s["w1"][:, cols])
    emit("e1")
    need("x1")
    unit = s["x1"][...]
    g_gain1 = jnp.sum(total * unit, 0, keepdims=True)
    g_shift1 = jnp.sum(total, 0, keepdims=True)
    dresid = norm_backward(total, unit, s["rs"][:, 0:1], gain1)
    s["r1"][...] = dresid
    s["e0"][...] = dresid.astype(BF)
    emit("r1")
    emit("e0")
    s["ln"][...] = jnp.concatenate([g_gain2, g_shift2, g_gain1, g_shift1, jnp.zeros((4, D), F32)], 0)
    emit("ln")


def backward_attention(s, need, emit):
    need("e0")
    need("wo")
    dmixed = nt(s["e0"][...], s["wo"][...]).astype(BF)
    s["do"][...] = dmixed
    s["dot"][...] = dmixed.T
    need("q")
    s["qt"][...] = s["q"][...].T
    need("k")
    need("v")
    need("p")
    low, high, is_low = lane_masks()
    for pair in range(HEADS // 2):
        cols = slice(pair * 128, pair * 128 + 128)
        grad, keys, values = s["do"][:, cols], s["k"][:, cols], s["v"][:, cols]
        got = []
        for half, mask in enumerate((low, high)):
            head = 2 * pair + half
            probs = s["p"][head * L : head * L + L, :]
            dprobs = nt(grad * mask, values)
            wide = probs.astype(F32)
            product = wide * dprobs
            dscores = (product - wide * jnp.sum(product, -1, keepdims=True)).astype(BF)
            got.append(nn(dscores, keys))
            lanes = slice(head * HEAD, head * HEAD + HEAD)
            s["dkt"][lanes, :] = nn(s["qt"][lanes, :], dscores)
            s["dvt"][lanes, :] = nn(s["dot"][lanes, :], probs)
        s["dq"][:, cols] = (jnp.where(is_low, got[0], got[1]) * SCALE).astype(BF)
    emit("dq")
    s["dk"][...] = (s["dkt"][...] * SCALE).T.astype(BF)
    emit("dk")
    s["dv"][...] = s["dvt"][...].T.astype(BF)
    emit("dv")
    for name in ("r1", "wq", "wk", "wv"):
        need(name)
    grad = s["r1"][...] + nt(s["dq"][...], s["wq"][...])
    grad = grad + nt(s["dk"][...], s["wk"][...]) + nt(s["dv"][...], s["wv"][...])
    s["ds"][...] = grad.astype(BF)
    emit("ds")
    s["dh"][...] = grad
    emit("dh")


WEIGHTS = ("wq", "wk", "wv", "wo", "w1", "w2")
SAVED = ("q", "k", "v", "p", "x1", "rs", "gp", "x2")
OPER_F = ("h", "o", "u", "a")
OPER_B = ("e2", "e1", "e0", "dq", "dk", "dv")


def run(refs_in, refs_out, scr, sems, order, body):
    moves = Moves(sems)
    coming = {name: moves.start(source, scr[name]) for name, source in ((n, refs_in[n]) for n in order)}

    def need(name):
        if name in coming:
            coming.pop(name).wait()

    def emit(name):
        for target in refs_out.get(name, ()):
            moves.out(scr[name], target)

    body(need, emit)
    for name in list(coming):
        need(name)
    moves.drain()


def stacked(names, scr):
    return [((ROWS,) + scr[n][0], scr[n][1]) for n in names]


def first_forward(row, place, tokens, segments, vecs, weights, state):
    keep = ("y",) + OPER_F + SAVED
    names = list(FSCR)
    order = ("h", "vec", "seg") + WEIGHTS

    def body(pos, *refs):
        ins, rest = refs[: 9 + (0 if state is None else len(keep))], refs[9 + (0 if state is None else len(keep)) :]
        outs, rest = rest[: len(keep) + 1], rest[len(keep) + 1 :]
        scr = dict(zip(names, rest[:-1]))

        @pl.when(pos[SEC] == 0)
        def _():
            src = dict(zip(("h", "seg", "vec") + WEIGHTS, ins))
            src["h"] = src["h"].at[row]
            for n in WEIGHTS:
                src[n] = src[n].at[0]
            dst = {n: [outs[i].at[row]] for i, n in enumerate(keep)}
            dst["y"] = [outs[-1]] + dst["y"]

            def whole(need, emit):
                need("h")
                emit("h")
                forward(scr, need, emit, row)

            run(src, dst, scr, rest[-1], order, whole)

    ins = [tokens, segments, vecs, *weights] + (list(state) if state is not None else [])
    outs = stacked(keep, FSCR) + [((L, D), BF)]
    aliases = {10 + i: i for i in range(len(keep))} if state is not None else None
    got = call(body, f"first_forward_{row}", place, ins, outs, list(FSCR.values()), aliases, flops=2 * 10**9, nbytes=16 * 10**6)
    return got[:-1], got[-1]


def second_both(row, place, arrived, segments, vecs, cotangent, weights, state, full):
    fwd, bwd = ("y",) + OPER_F, OPER_B + ("ln", "dh")
    scratch = {**FSCR, **B1SCR, **B2SCR}
    names = list(scratch)
    order = ("h", "vec", "seg", "wq", "wk", "wv", "wo", "w1", "w2", "dy")
    n_in = 10 + len(fwd) + (0 if full is None else len(bwd))

    def body(pos, *refs):
        ins, rest = refs[:n_in], refs[n_in:]
        outs, rest = rest[: len(fwd) + len(bwd) + 1], rest[len(fwd) + len(bwd) + 1 :]
        scr = dict(zip(names, rest[:-1]))

        @pl.when(pos[SEC] == 1)
        def _():
            src = dict(zip(("h", "seg", "vec", "dy") + WEIGHTS, ins))
            src["dy"] = src["dy"].at[row]
            for n in WEIGHTS:
                src[n] = src[n].at[0]
            dst = {n: [outs[i].at[row]] for i, n in enumerate(fwd + bwd)}
            dst["ds"] = [outs[-1]]

            def both(need, emit):
                emit("h")
                forward(scr, need, emit, row)
                backward_feed(scr, need, emit)
                backward_attention(scr, need, emit)

            def whole(need, emit):
                need("h")
                both(need, emit)

            run(src, dst, scr, rest[-1], order, whole)

    ins = [arrived, segments, vecs, cotangent, *weights, *state] + (list(full) if full is not None else [])
    outs = stacked(fwd + bwd, scratch) + [((L, D), BF)]
    aliases = {11 + i: i for i in range(len(fwd) + (0 if full is None else len(bwd)))}
    got = call(body, f"second_both_{row}", place, ins, outs, list(scratch.values()), aliases, flops=5 * 10**9, nbytes=20 * 10**6)
    return got[: len(fwd)], got[len(fwd) : -1], got[-1]


def first_feed(row, place, arrived, vecs, weights, saved, bufs):
    keep = ("e2", "e1", "e0", "ln")
    scratch = {**{n: FSCR[n] for n in ("vec", "w1", "w2", "x1", "rs", "gp", "x2")}, **B1SCR}
    names = list(scratch)
    order = ("dy", "vec", "x2", "rs", "w2", "gp", "w1", "x1")

    def body(pos, *refs):
        ins, rest = refs[: 8 + len(keep)], refs[8 + len(keep) :]
        outs, rest = rest[: len(keep) + 1], rest[len(keep) + 1 :]
        scr = dict(zip(names, rest[:-1]))

        @pl.when(pos[SEC] == 0)
        def _():
            src = dict(zip(("dy", "vec", "w1", "w2", "x1", "rs", "gp", "x2"), ins))
            for n in ("w1", "w2"):
                src[n] = src[n].at[0]
            for n in ("x1", "rs", "gp", "x2"):
                src[n] = src[n].at[row]
            dst = {n: [outs[i].at[row]] for i, n in enumerate(keep)}
            dst["r1"] = [outs[-1]]
            run(src, dst, scr, rest[-1], order, lambda need, emit: backward_feed(scr, need, emit))

    ins = [arrived, vecs, weights[4], weights[5], *[saved[n] for n in ("x1", "rs", "gp", "x2")], *bufs]
    outs = stacked(keep, scratch) + [((L, D), F32)]
    aliases = {9 + i: i for i in range(len(keep))}
    got = call(body, f"first_feed_{row}", place, ins, outs, list(scratch.values()), aliases, flops=10**9, nbytes=8 * 10**6)
    return got[:-1], got[-1]


def first_attention(row, place, dresid, e0, weights, saved, bufs):
    keep = ("dq", "dk", "dv", "dh")
    scratch = {**{n: FSCR[n] for n in ("wq", "wk", "wv", "wo", "q", "k", "v", "p")}, "e0": B1SCR["e0"], "r1": B1SCR["r1"], **B2SCR}
    names = list(scratch)
    order = ("e0", "wo", "q", "k", "v", "p", "r1", "wq", "wk", "wv")

    def body(pos, *refs):
        ins, rest = refs[: 10 + len(keep)], refs[10 + len(keep) :]
        outs, rest = rest[: len(keep)], rest[len(keep) :]
        scr = dict(zip(names, rest[:-1]))

        @pl.when(pos[SEC] == 0)
        def _():
            src = dict(zip(("r1", "e0", "wq", "wk", "wv", "wo", "q", "k", "v", "p"), ins))
            for n in ("wq", "wk", "wv", "wo"):
                src[n] = src[n].at[0]
            for n in ("e0", "q", "k", "v", "p"):
                src[n] = src[n].at[row]
            dst = {n: [outs[i].at[row]] for i, n in enumerate(keep)}
            run(src, dst, scr, rest[-1], order, lambda need, emit: backward_attention(scr, need, emit))

    ins = [dresid, e0, *weights[:4], *[saved[n] for n in ("q", "k", "v", "p")], *bufs]
    outs = stacked(keep, scratch)
    aliases = {11 + i: i for i in range(len(keep))}
    return call(body, f"first_attention_{row}", place, ins, outs, list(scratch.values()), aliases, flops=10**9, nbytes=8 * 10**6)


T2 = ROWS * L


def feed_product(want_up, ins, moves, lhs, rhs, store):
    u, a, e1, e2 = ins
    if want_up:
        one = moves.start(u, lhs.at[:, :D])
        many = [moves.start(e1.at[:, pl.ds(j * BLK, BLK)], rhs.at[:, pl.ds(j * BLK, BLK)]) for j in range(NBLK)]
        one.wait()
        left = lhs[:, :D].T
        for j in range(NBLK):
            many[j].wait()
            store(j, nn(left, rhs[:, j * BLK : j * BLK + BLK]))
    else:
        one = moves.start(e2, rhs.at[:, :D])
        many = [moves.start(a.at[:, pl.ds(j * BLK, BLK)], lhs.at[:, pl.ds(j * BLK, BLK)]) for j in range(NBLK)]
        one.wait()
        for j in range(NBLK):
            many[j].wait()
            store(j, tn(lhs[:, j * BLK : j * BLK + BLK], rhs[:, :D]))


def feed_send(place, ops):
    def body(pos, u, a, e1, e2, out, lhs, rhs, acc, sems):
        for core in range(2):

            @pl.when(pos[CORE] == core)
            def _():
                moves = Moves(sems)

                def store(j, value):
                    rows = slice(j * BLK, j * BLK + BLK)
                    acc[rows, :] = value.astype(BF)
                    moves.out(acc.at[rows, :], out.at[rows, :])

                feed_product(core == 0, (u, a, e1, e2), moves, lhs, rhs, store)
                moves.drain()

    scratch = [((T2, FF), BF), ((T2, FF), BF), ((FF, D), BF)]
    return call(body, "feed_send", place, ops, [((FF, D), BF)], scratch, flops=10**9, nbytes=6 * 10**6)[0]


def feed_keep(place, ops, got):
    def body(pos, u, a, e1, e2, recv, p1, p2, p3, p0, lhs, rhs, more, acc, sems):
        first = pos[FIRST]
        for core in range(2):

            @pl.when(pos[CORE] == core)
            def _():
                moves = Moves(sems)
                arrived = moves.start(recv, more)
                waiting = [arrived]

                def store(j, value):
                    if waiting:
                        waiting.pop().wait()
                    rows = slice(j * BLK, j * BLK + BLK)
                    acc[rows, :] = (value + more[rows, :].astype(F32)).astype(BF)

                feed_product(core == 1, (u, a, e1, e2), moves, lhs, rhs, store)
                for k, target in ((1, p1), (3, p3), (2, p2), (0, p0)):
                    at = pl.multiple_of(lax.rem(first + k, 4) * BLK, BLK)
                    moves.out(acc.at[pl.ds(at, BLK), :], target)
                moves.drain()

    scratch = [((T2, FF), BF), ((T2, FF), BF), ((FF, D), BF), ((FF, D), BF)]
    outs = [((BLK, D), BF)] * 4
    return call(body, "feed_keep", place, [*ops, got], outs, scratch, flops=10**9, nbytes=8 * 10**6)


ATT = 2 * D


def attention_product(want_out, ins, moves, left, right, store):
    o, h, e0, dq, dk, dv = ins
    pairs = ((o, e0), (h, dq)) if want_out else ((h, dk), (h, dv))
    loads = [(moves.start(x, left.at[i]), moves.start(y, right.at[i])) for i, (x, y) in enumerate(pairs)]
    for i in range(2):
        for load in loads[i]:
            load.wait()
        store(i, tn(left[i], right[i]))


def attention_send(place, ops, ln, feeds):
    def body(pos, o, h, e0, dq, dk, dv, lns, e1, e2, out, vec_out, left, right, acc, ones, wide, vecs, lnv, sems):
        moves = Moves(sems)
        loads = [moves.start(e1, wide), moves.start(e2, right.at[2]), moves.start(e0, right.at[3])]
        loads += [moves.start(dq, right.at[4]), moves.start(dv, right.at[5]), moves.start(lns, lnv)]
        ones[...] = jnp.ones_like(ones)
        for load in loads:
            load.wait()

        def total(value):
            return nn(ones[...], value)[0:1, :]

        lnt = lnv[0] + lnv[1]
        rows = [total(right[4]), total(right[5]), total(right[3]), lnt[2:3], lnt[3:4], total(right[2]), lnt[0:1], lnt[1:2]]
        rows += [total(wide[:, j * BLK : j * BLK + BLK]) for j in range(NBLK)]
        vecs[...] = jnp.concatenate(rows + [jnp.zeros((VEC - len(rows), D), F32)], 0).astype(BF)
        moves.out(vecs, out.at[pl.ds(ATT, VEC), :])
        moves.out(vecs, vec_out)
        done = moves.count
        for core in range(2):

            @pl.when(pos[CORE] == core)
            def _():
                own = Moves(sems)
                own.count = done

                def store(i, value):
                    rows = slice(i * D, i * D + D)
                    acc[rows, :] = value.astype(BF)
                    own.out(acc.at[rows, :], out.at[rows, :])

                attention_product(core == 1, (o, h, e0, dq, dk, dv), own, left, right, store)
                own.drain()

        moves.drain()

    scratch = [((2, T2, D), BF), ((6, T2, D), BF), ((ATT, D), BF), ((8, T2), BF), ((T2, FF), BF), ((VEC, D), BF), ((ROWS, 8, D), F32)]
    outs = [((ATT + VEC, D), BF), ((VEC, D), BF)]
    return call(body, "attention_send", place, [*ops, ln, *feeds], outs, scratch, flops=10**9, nbytes=8 * 10**6)


AQ = ATT // 4


def attention_keep(place, ops, vec, got):
    def body(pos, o, h, e0, dq, dk, dv, own_vec, recv, p1, p2, p3, p0, left, right, more, acc, vecs, sems):
        first = pos[FIRST]
        for core in range(2):

            @pl.when(pos[CORE] == core)
            def _():
                moves = Moves(sems)
                arrived = [moves.start(recv, more), moves.start(own_vec, vecs)]

                def store(i, value):
                    while arrived:
                        arrived.pop().wait()
                    rows = slice(i * D, i * D + D)
                    acc[rows, :] = (value + more[rows, :].astype(F32)).astype(BF)

                attention_product(core == 0, (o, h, e0, dq, dk, dv), moves, left, right, store)
                vecs[...] = (vecs[...].astype(F32) + more[ATT:, :].astype(F32)).astype(BF)
                for k, target in ((1, p1), (3, p3), (2, p2), (0, p0)):
                    at = pl.multiple_of(lax.rem(first + k, 4) * AQ, AQ)
                    moves.out(acc.at[pl.ds(at, AQ), :], target.at[pl.ds(0, AQ), :])
                    moves.out(vecs, target.at[pl.ds(AQ, VEC), :])
                moves.drain()

    scratch = [((2, T2, D), BF), ((2, T2, D), BF), ((ATT + VEC, D), BF), ((ATT, D), BF), ((VEC, D), BF)]
    outs = [((AQ + VEC, D), BF)] * 4
    return call(body, "attention_keep", place, [*ops, vec, got], outs, scratch, flops=10**9, nbytes=8 * 10**6)


def sum_split(place, own, got, extra, name):
    main = own.shape[0] - extra
    quarter = main // 4

    def body(pos, a, r1, r2, r3, p1, p2, p3, p0, parts, acc, sems):
        moves = Moves(sems)
        loads = [moves.start(x, parts.at[i]) for i, x in enumerate((a, r1, r2, r3))]
        for load in loads:
            load.wait()
        wide = [parts[i].astype(F32) for i in range(4)]
        acc[...] = ((wide[0] + wide[2]) + (wide[1] + wide[3])).astype(BF)
        for k, target in ((1, p1), (3, p3), (2, p2), (0, p0)):
            at = pl.multiple_of(lax.rem(pos[SECOND] + k, 4) * quarter, quarter)
            moves.out(acc.at[pl.ds(at, quarter), :], target.at[pl.ds(0, quarter), :])
            if extra:
                moves.out(acc.at[pl.ds(main, extra), :], target.at[pl.ds(quarter, extra), :])
        moves.drain()

    outs = [((quarter + extra, D), BF)] * 4
    return call(body, name, place, [own, *got], outs, [((4, main + extra, D), BF), ((main + extra, D), BF)], nbytes=4 * 10**6)


def sum_four(place, own, got, name):
    def body(pos, a, r1, r2, r3, out, parts, acc, sems):
        moves = Moves(sems)
        loads = [moves.start(x, parts.at[i]) for i, x in enumerate((a, r1, r2, r3))]
        for load in loads:
            load.wait()
        wide = [parts[i].astype(F32) for i in range(4)]
        acc[...] = ((wide[0] + wide[2]) + (wide[1] + wide[3])).astype(BF)
        moves.out(acc, out)
        moves.drain()

    return call(body, name, place, [own, *got], [(own.shape, BF)], [((4,) + own.shape, BF), (own.shape, BF)], nbytes=10**6)[0]


def sum_two(place, own, got, extra, name):
    main = own.shape[0] - extra

    def body(pos, a, b, *refs):
        outs, (parts, acc, sems) = refs[:-3], refs[-3:]
        moves = Moves(sems)
        loads = [moves.start(x, parts.at[i]) for i, x in enumerate((a, b))]
        for load in loads:
            load.wait()
        acc[...] = (parts[0].astype(F32) + parts[1].astype(F32)).astype(BF)
        moves.out(acc.at[pl.ds(0, main), :], outs[0])
        if extra:
            moves.out(acc.at[pl.ds(main, extra), :], outs[1])
        moves.drain()

    outs = [((main, D), BF)] + ([((extra, D), BF)] if extra else [])
    return call(body, name, place, [own, got], outs, [((2,) + own.shape, BF), (own.shape, BF)], nbytes=10**6)


def join(place, own, got, name):
    rows = own.shape[0]

    def body(pos, a, r1, r2, r3, out, sems):
        moves = Moves(sems)
        for k, x in enumerate((a, r1, r2, r3)):
            at = pl.multiple_of(lax.rem(pos[SECOND] + (4 - k), 4) * rows, rows)
            moves.out(x, out.at[pl.ds(at, rows), :])
        moves.drain()

    return call(body, name, place, [own, *got], [((4 * rows, D), BF)], [], nbytes=10**6)[0]


def feed_finish(place, mine, other):
    def body(pos, *refs):
        ins, (up, down), (narrow, wide, sems) = refs[:8], refs[8:10], refs[10:]
        moves = Moves(sems)
        loads = [moves.start(x, narrow.at[i]) for i, x in enumerate(ins)]
        for i in range(8):
            loads[i].wait()
            wide[i] = narrow[i].astype(F32)
            base = pos[FIRST] if i < 4 else pos[SECOND]
            at = pl.multiple_of(lax.rem(base + (4 - i % 4), 4) * BLK, BLK)
            first = moves.count
            for core in range(2):

                @pl.when(pos[CORE] == core)
                def _():
                    if (core == 0) == (i < 4):
                        target = down.at[0, pl.ds(at, BLK), :]
                    else:
                        target = up.at[0, :, pl.ds(at, BLK)]
                    pltpu.make_async_copy(wide.at[i], target, sems.at[first]).start()

            moves.count = first + 1
        for i in range(8):
            pltpu.make_async_copy(wide.at[i], down.at[0, pl.ds(0, BLK), :], sems.at[8 + i]).wait()

    outs = [((1, D, FF), F32), ((1, FF, D), F32)]
    scratch = [((8, BLK, D), BF), ((8, BLK, D), F32)]
    return call(body, "feed_finish", place, [*mine, *other], outs, scratch, nbytes=12 * 10**6)


VECTOR_ROWS = (BQ, BV, BO, G1, S1, C2, G2, S2)


def attention_finish(place, mine, other, vec_mine, vec_other):
    def body(pos, *refs):
        ins, vec_a, vec_b, outs = refs[:8], refs[8], refs[9], refs[10:14]
        vec_outs, up_out = refs[14:22], refs[22]
        narrow, wide, vecs, sems = refs[23:]
        moves = Moves(sems)
        loads = [moves.start(x, narrow.at[i]) for i, x in enumerate(ins)]
        first = moves.count
        for core, source in ((0, vec_a), (1, vec_b)):

            @pl.when(pos[CORE] == core)
            def _():
                pltpu.make_async_copy(source, vecs, sems.at[first]).start()

        moves.count = first + 1
        for i in range(8):
            loads[i].wait()
            wide[i] = narrow[i].astype(F32)
            base = pos[FIRST] if i < 4 else pos[SECOND]
            piece = lax.rem(base + (4 - i % 4), 4)
            at = pl.multiple_of(lax.rem(piece, 2) * AQ, AQ)
            kind = jnp.where((pos[CORE] == 0) == (i < 4), 0, 2) + lax.div(piece, 2)
            for which in range(4):

                @pl.when(kind == which)
                def _():
                    pltpu.make_async_copy(wide.at[i], outs[which].at[0, pl.ds(at, AQ), :], sems.at[first + 1 + i]).start()

        pltpu.make_async_copy(vec_a, vecs, sems.at[first]).wait()
        values = vecs[...].astype(F32)
        for row, target in zip(VECTOR_ROWS, vec_outs):
            target[...] = values[row : row + 1, :]
        for j in range(NBLK):
            up_out[:, j * BLK : j * BLK + BLK] = values[C1 + j : C1 + j + 1, :]
        for i in range(8):
            pltpu.make_async_copy(wide.at[i], outs[0].at[0, pl.ds(0, AQ), :], sems.at[first + 1 + i]).wait()

    outs = [((1, D, D), F32)] * 4 + [((1, D), F32)] * 8 + [((1, FF), F32)]
    scratch = [((8, AQ, D), BF), ((8, AQ, D), F32), ((VEC, D), BF)]
    return call(body, "attention_finish", place, [*mine, *other, vec_mine, vec_other], outs, scratch, nbytes=6 * 10**6, vmem_outs=range(4, 13))


def spot(y, z, x, core):
    return ((y * 2 + z) * 4 + x) * 2 + core


def everywhere(move):
    route = []
    for y in range(4):
        for z in range(2):
            for x in range(4):
                for core in range(2):
                    route.append((spot(y, z, x, core), spot(*move(y, z, x, core))))
    return route


def along(stage, distance):
    def move(y, z, x, core):
        if (core == 0) == (stage == 0):
            return y, z, (x + distance) % 4, core
        return (y + distance) % 4, z, x, core

    return everywhere(move)


def send(value, route):
    return lax.ppermute(value, "dp", route)


def to_core(value):
    return send(value, everywhere(lambda y, z, x, core: (y, z, x, 1 - core)))


def to_z(value):
    return send(value, everywhere(lambda y, z, x, core: (y, 1 - z, x, core)))


def spread(pieces, stage):
    sent = {k: send(pieces[k - 1], along(stage, k)) for k in (1, 3, 2)}
    return [sent[k] for k in (1, 2, 3)]


def reduce_over_dp(place, pieces, extra, name):
    got = spread(pieces[:3], 0)
    pieces = sum_split(place, pieces[3], got, extra, name + "_first")
    got = spread(pieces[:3], 1)
    mine = sum_four(place, pieces[3], got, name + "_second")
    whole = sum_two(place, mine, to_z(mine), extra, name + "_third")
    shard = whole[0]
    block = join(place, shard, spread([shard] * 3, 1), name + "_join")
    blocks = [block] + spread([block] * 3, 0)
    return blocks, [to_core(b) for b in blocks], whole[1:]


def shards(tokens, segments, cotangent, w_query, q_bias, w_key, w_value, v_bias, w_out, out_bias, ln1_gain, ln1_shift, w_up, up_bias, w_down, down_bias, ln2_gain, ln2_shift):
    here = lax.axis_index("dp")
    core, x, y = here % 2, (here // 2) % 4, here // 16
    first, second = jnp.where(core == 0, x, y), jnp.where(core == 0, y, x)
    place = jnp.stack([lax.axis_index("section"), core, first, second]).astype(jnp.int32)
    vecs = jnp.concatenate(
        [q_bias, v_bias, out_bias, ln1_gain, ln1_shift, down_bias, ln2_gain, ln2_shift, up_bias.reshape(NBLK, BLK), jnp.zeros((4, D), F32)], 0
    )
    weights = (w_query, w_key, w_value, w_out, w_up, w_down)

    def forth(value):
        return lax.ppermute(value, "section", [(0, 1)])

    def back(value):
        return lax.ppermute(value, "section", [(1, 0)])

    state, sent0 = first_forward(0, place, tokens, segments, vecs, weights, None)
    came0 = forth(sent0)
    state, sent1 = first_forward(1, place, tokens, segments, vecs, weights, state)
    came1 = forth(sent1)
    n = 1 + len(OPER_F)
    fwd, saved = state[:n], dict(zip(SAVED, state[n:]))
    fwd, full, dsent0 = second_both(0, place, came0, segments, vecs, cotangent, weights, fwd, None)
    dcame0 = back(dsent0)
    fwd, full, dsent1 = second_both(1, place, came1, segments, vecs, cotangent, weights, fwd, full)
    dcame1 = back(dsent1)
    outputs, ops_f = fwd[0], dict(zip(OPER_F, fwd[1:]))
    back_bufs = dict(zip(OPER_B + ("ln", "dh"), full))

    def flat(value):
        return value.reshape((T2, value.shape[-1]))

    for row, came in ((0, dcame0), (1, dcame1)):
        got, dresid = first_feed(row, place, came, vecs, weights, saved, [back_bufs[n] for n in ("e2", "e1", "e0", "ln")])
        back_bufs.update(zip(("e2", "e1", "e0", "ln"), got))
        if row == 1:
            feed_ops = [flat(ops_f["u"]), flat(ops_f["a"]), flat(back_bufs["e1"]), flat(back_bufs["e2"])]
            feed_out = feed_send(place, feed_ops)
            feed_in = to_core(feed_out)
        got = first_attention(row, place, dresid, back_bufs["e0"], weights, saved, [back_bufs[n] for n in ("dq", "dk", "dv", "dh")])
        back_bufs.update(zip(("dq", "dk", "dv", "dh"), got))
    att_ops = [flat(v) for v in (ops_f["o"], ops_f["h"], back_bufs["e0"], back_bufs["dq"], back_bufs["dk"], back_bufs["dv"])]
    att_out, att_vec = attention_send(place, att_ops, back_bufs["ln"], (feed_ops[2], feed_ops[3]))
    att_in = to_core(att_out)
    feed_pieces = feed_keep(place, feed_ops, feed_in)
    att_pieces = attention_keep(place, att_ops, att_vec, att_in)
    mine_f, other_f, _ = reduce_over_dp(place, feed_pieces, 0, "feed")
    mine_a, other_a, vec = reduce_over_dp(place, att_pieces, VEC, "attention")
    g_up, g_down = feed_finish(place, mine_f, other_f)
    finished = attention_finish(place, mine_a, other_a, vec[0], to_core(vec[0]))
    g_out, g_query, g_key, g_value = finished[:4]
    g = dict(zip(VECTOR_ROWS, finished[4:12]))
    g_upbias = finished[12]
    return (
        outputs[None],
        back_bufs["dh"][None],
        g_query,
        g[BQ],
        g_key,
        g_value,
        g[BV],
        g_out,
        g[BO],
        g[G1],
        g[S1],
        g_up,
        g_upbias,
        g_down,
        g[C2],
        g[G2],
        g[S2],
    )


def solution(mesh):
    row, matrix, vector = P("dp", None, None), P("section", None, None), P("section", None)
    in_specs = (row, P("dp", None), row, matrix, vector, matrix, matrix, vector, matrix, vector, vector, vector, matrix, vector, matrix, vector, vector, vector)
    big = P("section", "dp", None, None)
    out_specs = (big, big, matrix, vector, matrix, matrix, vector, matrix, vector, vector, vector, matrix, vector, matrix, vector, vector, vector)
    return jax.shard_map(shards, mesh=mesh, in_specs=in_specs, out_specs=out_specs, check_vma=False)
```

```python
import functools

import jax
import jax.numpy as jnp
from jax import lax
from jax.experimental import pallas as pl
from jax.experimental.pallas import tpu as pltpu
from jax.sharding import PartitionSpec as P

BF, F32 = jnp.bfloat16, jnp.float32
ROWS, L, D, FF, HEADS, HEAD = 2, 256, 512, 2048, 8, 64
BLK = 512
NBLK = FF // BLK
VEC = 16
MiB = 1 << 20
SCALE = HEAD ** (-0.5)
BQ, BV, BO, G1, S1, C2, G2, S2, C1 = 0, 1, 2, 3, 4, 5, 6, 7, 8
SEC, CORE, FIRST, SECOND = 0, 1, 2, 3


def nn(a, b):
    return jnp.dot(a, b, preferred_element_type=F32)


def nt(a, b):
    return lax.dot_general(a, b, (((1,), (1,)), ((), ())), preferred_element_type=F32)


def tn(a, b):
    return lax.dot_general(a, b, (((0,), (0,)), ((), ())), preferred_element_type=F32)


def kernel(name, body, reads, updates, news, scratch=None, sems=0, outside=(), free=(), vmem=12, flops=0, nbytes=0):
    scratch = scratch or {}
    outs = {**updates, **news}
    names = list(reads) + list(updates)

    def spec(n):
        if n in outside:
            return pl.BlockSpec(memory_space=pltpu.HBM)
        if n in ("pos", "here"):
            return pl.BlockSpec(memory_space=pltpu.SMEM)
        return pl.BlockSpec(memory_space=pltpu.VMEM)

    def shape(n):
        if n == "pos":
            return pltpu.SMEM(*news[n])
        space = pltpu.HBM if n in outside else jax.ShapeDtypeStruct if n in free else pltpu.VMEM
        return space(*news[n]) if n in news else space(updates[n].shape, updates[n].dtype)

    reads = {n: pltpu.with_memory_space_constraint(v, pltpu.HBM) if n in outside else v for n, v in reads.items()}

    def whole(*refs):
        s = dict(zip(reads, refs))
        rest = refs[len(names) :]
        s.update(zip(outs, rest))
        s.update(zip(list(scratch) + ["sems"], rest[len(outs) :]))
        body(s)

    got = pl.pallas_call(
        whole,
        out_shape=[shape(n) for n in outs],
        in_specs=[spec(n) for n in names],
        out_specs=[spec(n) for n in outs],
        scratch_shapes=[pltpu.VMEM(*v) for v in scratch.values()] + ([pltpu.SemaphoreType.DMA((sems,))] if sems else []),
        input_output_aliases={len(reads) + i: i for i in range(len(updates))},
        compiler_params=pltpu.CompilerParams(vmem_limit_bytes=vmem * MiB),
        cost_estimate=pl.CostEstimate(flops=flops, bytes_accessed=nbytes, transcendentals=0),
        name=name,
    )(*reads.values(), *updates.values())
    return dict(zip(outs, got))


def norm_forward(resid, gain, shift):
    centre = resid - jnp.mean(resid, -1, keepdims=True)
    rstd = lax.rsqrt(jnp.mean(centre * centre, -1, keepdims=True) + 1e-05)
    unit = centre * rstd
    return unit, rstd, unit * gain + shift


def norm_backward(grad, unit, rstd, gain):
    scaled = grad * gain
    inner = scaled - jnp.mean(scaled, -1, keepdims=True)
    return rstd * (inner - unit * jnp.mean(scaled * unit, -1, keepdims=True))


def lane_masks():
    lane = lax.broadcasted_iota(jnp.int32, (L, 128), 1)
    low = (lane < HEAD).astype(F32)
    return low.astype(BF), (1.0 - low).astype(BF), lane < HEAD


ROW = dict(
    h=((L, D), BF),
    y=((L, D), BF),
    o=((L, D), BF),
    u=((L, D), BF),
    a=((L, FF), BF),
    q=((L, D), BF),
    k=((L, D), BF),
    v=((L, D), BF),
    p=((HEADS * L, L), BF),
    gp=((L, FF), BF),
    x1=((L, D), F32),
    x2=((L, D), F32),
    rs=((L, 256), F32),
    e2=((L, D), BF),
    e1=((L, FF), BF),
    e0=((L, D), BF),
    dq=((L, D), BF),
    dk=((L, D), BF),
    dv=((L, D), BF),
    ln=((8, D), F32),
    dh=((L, D), F32),
)
FORWARD = ("h", "y", "o", "u", "a", "q", "k", "v", "p", "gp", "x1", "x2", "rs")
BACKWARD = ("e2", "e1", "e0", "dq", "dk", "dv", "ln", "dh")
WEIGHTS = dict(wq=((D, D), BF), wk=((D, D), BF), wv=((D, D), BF), wo=((D, D), BF), w1=((D, FF), BF), w2=((FF, D), BF))


def both_rows(names):
    return {n: ((ROWS,) + ROW[n][0], ROW[n][1]) for n in names}


def of_row(s, row, names):
    return {**s, **{n: s[n].at[row] for n in names}}


def forward(s, need, row):
    need("wq")
    hidden = s["h"][...]

    def vec(i):
        return s["vec"][i : i + 1, :]

    s["q"][...] = (nn(hidden, s["wq"][...]) + vec(BQ)).astype(BF)
    need("wk")
    s["k"][...] = nn(hidden, s["wk"][...]).astype(BF)
    need("wv")
    s["v"][...] = (nn(hidden, s["wv"][...]) + vec(BV)).astype(BF)
    seg = jnp.broadcast_to(s["seg"][row : row + 1, :].astype(F32), (L, L))
    same = seg == seg.T
    low, high, is_low = lane_masks()
    for pair in range(HEADS // 2):
        cols = slice(pair * 128, pair * 128 + 128)
        query, keys, values = s["q"][:, cols], s["k"][:, cols], s["v"][:, cols]
        got = []
        for half, mask in enumerate((low, high)):
            at = (2 * pair + half) * L
            scores = jnp.where(same, nt(query * mask, keys) * SCALE, -1000000000.0)
            weight = jnp.exp(scores - jnp.max(scores, -1, keepdims=True))
            probs = (weight * (1.0 / jnp.sum(weight, -1, keepdims=True))).astype(BF)
            s["p"][at : at + L, :] = probs
            got.append(nn(probs, values))
        s["o"][:, cols] = jnp.where(is_low, got[0], got[1]).astype(BF)
    need("wo")
    resid = hidden.astype(F32) + nn(s["o"][...], s["wo"][...]) + vec(BO)
    unit, rstd, normed = norm_forward(resid, vec(G1), vec(S1))
    s["x1"][...] = unit
    s["rs"][:, :128] = jnp.broadcast_to(rstd, (L, 128))
    s["u"][...] = normed.astype(BF)
    need("w1")
    need("w2")
    total = normed + vec(C2)
    for j in range(NBLK):
        cols = slice(j * BLK, j * BLK + BLK)
        z = nn(s["u"][...], s["w1"][:, cols]) + vec(C1 + j)
        square = z * z
        tanh = jnp.tanh(0.7978845608028654 * z * (1.0 + 0.044715 * square))
        half = 0.5 * (1.0 + tanh)
        active = (z * half).astype(BF)
        s["a"][:, cols] = active
        slope = half + (z * half) * (1.0 - tanh) * (0.7978845608028654 * (1.0 + 0.134145 * square))
        s["gp"][:, cols] = slope.astype(BF)
        total = total + nn(active, s["w2"][cols, :])
    unit, rstd, out = norm_forward(total, vec(G2), vec(S2))
    s["y"][...] = out.astype(BF)
    s["x2"][...] = unit
    s["rs"][:, 128:] = jnp.broadcast_to(rstd, (L, 128))


BACK = dict(qt=((D, L), BF), dot=((D, L), BF), do=((L, D), BF), dkt=((D, L), F32), dvt=((D, L), F32))


def backward_feed(s):
    gain1, gain2 = s["vec"][G1 : G1 + 1, :], s["vec"][G2 : G2 + 1, :]
    dout = s["dy"][...].astype(F32)
    unit = s["x2"][...]
    g_gain2 = jnp.sum(dout * unit, 0, keepdims=True)
    g_shift2 = jnp.sum(dout, 0, keepdims=True)
    dsecond = norm_backward(dout, unit, s["rs"][:, 128:129], gain2)
    s["e2"][...] = dsecond.astype(BF)
    total = dsecond
    for j in range(NBLK):
        cols = slice(j * BLK, j * BLK + BLK)
        dactive = nt(s["e2"][...], s["w2"][cols, :])
        dinner = (s["gp"][:, cols].astype(F32) * dactive).astype(BF)
        s["e1"][:, cols] = dinner
        total = total + nt(dinner, s["w1"][:, cols])
    unit = s["x1"][...]
    g_gain1 = jnp.sum(total * unit, 0, keepdims=True)
    g_shift1 = jnp.sum(total, 0, keepdims=True)
    dresid = norm_backward(total, unit, s["rs"][:, 0:1], gain1)
    s["r1"][...] = dresid
    s["e0"][...] = dresid.astype(BF)
    s["ln"][...] = jnp.concatenate([g_gain2, g_shift2, g_gain1, g_shift1, jnp.zeros((4, D), F32)], 0)


def backward_attention(s):
    dmixed = nt(s["e0"][...], s["wo"][...]).astype(BF)
    s["do"][...] = dmixed
    s["dot"][...] = dmixed.T
    s["qt"][...] = s["q"][...].T
    low, high, is_low = lane_masks()
    for pair in range(HEADS // 2):
        cols = slice(pair * 128, pair * 128 + 128)
        grad, keys, values = s["do"][:, cols], s["k"][:, cols], s["v"][:, cols]
        got = []
        for half, mask in enumerate((low, high)):
            head = 2 * pair + half
            probs = s["p"][head * L : head * L + L, :]
            dprobs = nt(grad * mask, values)
            wide = probs.astype(F32)
            product = wide * dprobs
            dscores = (product - wide * jnp.sum(product, -1, keepdims=True)).astype(BF)
            got.append(nn(dscores, keys))
            lanes = slice(head * HEAD, head * HEAD + HEAD)
            s["dkt"][lanes, :] = nn(s["qt"][lanes, :], dscores)
            s["dvt"][lanes, :] = nn(s["dot"][lanes, :], probs)
        s["dq"][:, cols] = (jnp.where(is_low, got[0], got[1]) * SCALE).astype(BF)
    s["dk"][...] = (s["dkt"][...] * SCALE).T.astype(BF)
    s["dv"][...] = s["dvt"][...].T.astype(BF)
    grad = s["r1"][...] + nt(s["dq"][...], s["wq"][...])
    grad = grad + nt(s["dk"][...], s["wk"][...]) + nt(s["dv"][...], s["wv"][...])
    s["ds"][...] = grad.astype(BF)
    s["dh"][...] = grad


VECTORS = (BQ, BV, BO, G1, S1, C2, G2, S2)


def first_forward(row, outside, state):
    if row == 0:
        reads, updates = outside, {}
        news = {**WEIGHTS, "vec": ((VEC, D), F32), "seg": ((ROWS, L), jnp.int32), "cot": ((ROWS, L, D), BF), "pos": ((4,), jnp.int32)}
        news.update(both_rows(FORWARD))
    else:
        keep = ("vec", "seg", "pos", *WEIGHTS)
        reads, updates = {n: state[n] for n in keep}, {n: state[n] for n in FORWARD}
        news = {}
    news["sent"] = ROW["y"]

    def body(s):
        copies = {}

        def start(n, source, target):
            copies[n] = pltpu.make_async_copy(source, target, s["sems"].at[len(copies)])
            copies[n].start()

        def need(n):
            if n in copies:
                copies.pop(n).wait()

        if row == 0:
            start("h", s["in_h"], s["h"])
            start("seg", s["in_seg"], s["seg"])
            start("wq", s["in_wq"].at[0], s["wq"])
            for i in VECTORS:
                start(i, s[f"in_{i}"], s["vec"].at[pl.ds(i, 1), :])
            for j in range(NBLK):
                start(C1 + j, s[f"in_{C1}"].at[:, pl.ds(j * BLK, BLK)], s["vec"].at[pl.ds(C1 + j, 1), :])
            for n in list(WEIGHTS)[1:]:
                start(n, s["in_" + n].at[0], s[n])
            start("cot", s["in_cot"], s["cot"])
            for i in range(4):
                s["pos"][i] = s["here"][i]
            for n in ("h", "seg", *VECTORS, *range(C1, C1 + NBLK)):
                need(n)
        r = of_row(s, row, FORWARD)
        waits = dict(copies)

        @pl.when(s["pos" if row else "here"][SEC] == 0)
        def _():
            forward(r, need, row)
            s["sent"][...] = r["y"][...]
            for n in list(copies):
                need(n)

        if row == 0:

            @pl.when(s["here"][SEC] != 0)
            def _():
                for copy in waits.values():
                    copy.wait()

    got = kernel(f"first_forward_{row}", body, reads, updates, news, sems=32 * (row == 0), outside=[n for n in reads if n.startswith("in_")], flops=3 * 10**9, nbytes=8 * 10**6)
    return got.pop("sent"), {**state, **got}


def second_both(row, arrived, state):
    reads = {n: state[n] for n in ("vec", "seg", "pos", "cot", *WEIGHTS)}
    reads["arrived"] = arrived
    updates = {n: state[n] for n in FORWARD}
    news = {"ds": ROW["y"]}
    if row == 0:
        news.update(both_rows(BACKWARD))
    else:
        updates.update({n: state[n] for n in BACKWARD})

    def body(s):
        r = of_row(s, row, FORWARD + BACKWARD)
        r["dy"] = s["cot"].at[row]

        @pl.when(s["pos"][SEC] == 1)
        def _():
            r["h"][...] = s["arrived"][...]
            forward(r, lambda n: None, row)
            backward_feed(r)
            backward_attention(r)

    got = kernel(f"second_both_{row}", body, reads, updates, news, {**BACK, "r1": ROW["dh"]}, flops=6 * 10**9, nbytes=8 * 10**6)
    return got.pop("ds"), {**state, **got}


def first_feed(row, arrived, state):
    reads = {n: state[n] for n in ("vec", "pos", "w1", "w2", "x1", "x2", "rs", "gp")}
    reads["dy"] = arrived
    keep = ("e2", "e1", "e0", "ln")

    def body(s):
        @pl.when(s["pos"][SEC] == 0)
        def _():
            backward_feed(of_row(s, row, ("x1", "x2", "rs", "gp", *keep)))

    got = kernel(f"first_feed_{row}", body, reads, {n: state[n] for n in keep}, {"r1": ROW["dh"]}, flops=10**9, nbytes=8 * 10**6)
    return got.pop("r1"), {**state, **got}


def first_attention(row, dresid, state):
    reads = {n: state[n] for n in ("pos", "wq", "wk", "wv", "wo", "e0", "q", "k", "v", "p")}
    reads["r1"] = dresid
    keep = ("dq", "dk", "dv", "dh")

    def body(s):
        @pl.when(s["pos"][SEC] == 0)
        def _():
            backward_attention(of_row(s, row, ("e0", "q", "k", "v", "p", *keep)))

    got = kernel(f"first_attention_{row}", body, reads, {n: state[n] for n in keep}, {}, {**BACK, "ds": ROW["y"]}, flops=2 * 10**9, nbytes=8 * 10**6)
    return {**state, **got}


T2 = ROWS * L
AQ = D // 2


def aligned(index, size):
    return pl.multiple_of(index * size, size)


def feed_block(s, up, j):
    cols = pl.ds(aligned(j, BLK), BLK)
    if up:
        return tn(s["u"][...], s["e1"][:, cols])
    return tn(s["a"][:, cols], s["e2"][...])


def per_core(s, work):
    for core in range(2):
        pl.when(s["pos"][CORE] == core)(functools.partial(work, core))


def feed_send(pos, ops):
    def body(s):
        def work(core):
            for j in range(NBLK):
                s["out"][j * BLK : j * BLK + BLK, :] = feed_block(s, core == 0, j).astype(BF)

        per_core(s, work)

    return kernel("feed_send", body, {"pos": pos, **ops}, {}, {"out": ((FF, D), BF)}, flops=2 * 10**9, nbytes=10**7)["out"]


def feed_keep(pos, ops, got):
    def body(s):
        def work(core):
            for k in (1, 3, 2, 0):
                j = lax.rem(s["pos"][FIRST] + k, 4)
                more = s["got"][pl.ds(aligned(j, BLK), BLK), :].astype(F32)
                s[f"p{k}"][...] = (feed_block(s, core == 1, j) + more).astype(BF)

        per_core(s, work)

    news = {f"p{k}": ((BLK, D), BF) for k in range(4)}
    return list(kernel("feed_keep", body, {"pos": pos, **ops, "got": got}, {}, news, flops=2 * 10**9, nbytes=10**7).values())


def attention_block(s, out, i):
    if out:
        return tn(s["o"][...], s["e0"][...]) if i == 0 else tn(s["h"][...], s["dq"][...])
    return tn(s["h"][...], s["dk" if i == 0 else "dv"][...])


def attention_send(pos, ops, more):
    def body(s):
        def work(core):
            for i in range(2):
                s["out"][i * D : i * D + D, :] = attention_block(s, core == 1, i).astype(BF)

        per_core(s, work)
        ones = jnp.ones((8, T2), BF)

        def total(value):
            return nn(ones, value)[0:1, :]

        ln = s["ln"][0] + s["ln"][1]
        rows = [total(s["dq"][...]), total(s["dv"][...]), total(s["e0"][...]), ln[2:3], ln[3:4], total(s["e2"][...]), ln[0:1], ln[1:2]]
        rows += [total(s["e1"][:, j * BLK : j * BLK + BLK]) for j in range(NBLK)]
        s["vec"][...] = jnp.concatenate(rows + [jnp.zeros((VEC - len(rows), D), F32)], 0).astype(BF)
        s["out"][2 * D :, :] = s["vec"][...]

    news = {"out": ((2 * D + VEC, D), BF), "vec": ((VEC, D), BF)}
    got = kernel("attention_send", body, {"pos": pos, **ops, **more}, {}, news, flops=10**9, nbytes=8 * 10**6)
    return got["out"], got["vec"]


def attention_keep(pos, ops, vec, got):
    def body(s):
        def work(core):
            for i in range(2):
                rows = slice(i * D, i * D + D)
                s["acc"][rows, :] = (attention_block(s, core == 0, i) + s["got"][rows, :].astype(F32)).astype(BF)

        per_core(s, work)
        shared = (s["vec"][...].astype(F32) + s["got"][2 * D :, :].astype(F32)).astype(BF)
        for k in range(4):
            j = lax.rem(s["pos"][FIRST] + k, 4)
            s[f"p{k}"][:AQ, :] = s["acc"][pl.ds(aligned(j, AQ), AQ), :]
            s[f"p{k}"][AQ:, :] = shared

    news = {f"p{k}": ((AQ + VEC, D), BF) for k in range(4)}
    reads = {"pos": pos, **ops, "vec": vec, "got": got}
    return list(kernel("attention_keep", body, reads, {}, news, {"acc": ((2 * D, D), BF)}, flops=10**9, nbytes=8 * 10**6).values())


def total_of(s):
    wide = [s[f"g{k}"][...].astype(F32) for k in range(4)]
    return ((wide[0] + wide[2]) + (wide[1] + wide[3])).astype(BF)


def total_of(s, tag):
    wide = [s[f"{tag}{k}"][...].astype(F32) for k in range(4)]
    return ((wide[0] + wide[2]) + (wide[1] + wide[3])).astype(BF)


def by_distance(tag, values):
    return {f"{tag}{k}": v for k, v in enumerate(values)}


FQ, TQ = BLK // 4, AQ // 4
SHARD = FQ + TQ


def sum_split(pos, feeds, atts):
    def body(s):
        s["feed"][...] = total_of(s, "f")
        s["att"][...] = total_of(s, "t")
        for k in range(4):
            j = lax.rem(s["pos"][SECOND] + k, 4)
            s[f"p{k}"][:FQ, :] = s["feed"][pl.ds(aligned(j, FQ), FQ), :]
            s[f"p{k}"][FQ:SHARD, :] = s["att"][pl.ds(aligned(j, TQ), TQ), :]
            s[f"p{k}"][SHARD:, :] = s["att"][AQ:, :]

    reads = {"pos": pos, **by_distance("f", feeds), **by_distance("t", atts)}
    news = {f"p{k}": ((SHARD + VEC, D), BF) for k in range(4)}
    scratch = {"feed": ((BLK, D), BF), "att": ((AQ + VEC, D), BF)}
    return list(kernel("sum_split", body, reads, {}, news, scratch, nbytes=10**6).values())


def sum_four(got):
    def body(s):
        s["out"][...] = total_of(s, "g")

    return kernel("sum_four", body, by_distance("g", got), {}, {"out": (got[0].shape, BF)}, nbytes=10**6)["out"]


def sum_two(own, got):
    def body(s):
        total = (s["a"][...].astype(F32) + s["b"][...].astype(F32)).astype(BF)
        s["out"][...] = total[:SHARD]
        s["vec"][...] = total[SHARD:]

    got = kernel("sum_two", body, {"a": own, "b": got}, {}, {"out": ((SHARD, D), BF), "vec": ((VEC, D), BF)}, nbytes=10**6)
    return got["out"], got["vec"]


def join(pos, got):
    def body(s):
        for k in range(4):
            j = lax.rem(s["pos"][SECOND] + (4 - k), 4)
            s["out"][pl.ds(aligned(j, FQ), FQ), :] = s[f"g{k}"][:FQ, :]
            s["out"][pl.ds(aligned(j, TQ) + BLK, TQ), :] = s[f"g{k}"][FQ:, :]

    return kernel("join", body, {"pos": pos, **by_distance("g", got)}, {}, {"out": ((BLK + AQ, D), BF)}, nbytes=10**6)["out"]


MATRICES = ("o", "q", "k", "v")


def finish(pos, name, blocks, done):
    def body(s):
        sems = iter(range(2 * len(blocks)))
        started = []

        def move(source, target, sem):
            pltpu.make_async_copy(source, target, s["sems"].at[sem]).start()

        for i, (_, mine, k) in enumerate(blocks):
            s["wide"][i] = s[f"b{i}"][...].astype(F32)
            feed, att = s["wide"].at[i, pl.ds(0, BLK)], s["wide"].at[i, pl.ds(BLK, AQ)]
            piece = lax.rem(s["pos"][FIRST if mine else SECOND] + (4 - k), 4)
            down = (s["pos"][CORE] == 0) if mine else (s["pos"][CORE] == 1)
            sem = next(sems)

            @pl.when(down)
            def _():
                move(feed, s["down"].at[0, pl.ds(aligned(piece, BLK), BLK), :], sem)

            @pl.when(jnp.logical_not(down))
            def _():
                move(feed, s["up"].at[0, :, pl.ds(aligned(piece, BLK), BLK)], sem)

            started.append((feed, s["down"].at[0, pl.ds(0, BLK), :], sem))
            sem = next(sems)
            kind = jnp.where(down, 0, 2) + lax.div(piece, 2)
            at = aligned(lax.rem(piece, 2), AQ)
            for which, n in enumerate(MATRICES):

                @pl.when(kind == which)
                def _():
                    move(att, s[n].at[0, pl.ds(at, AQ), :], sem)

            started.append((att, s["o"].at[0, pl.ds(0, AQ), :], sem))
        for source, target, sem in started:
            pltpu.make_async_copy(source, target, s["sems"].at[sem]).wait()

    reads = {"pos": pos, **{f"b{i}": b[0] for i, b in enumerate(blocks)}}
    news = {} if done else {"up": ((1, D, FF), F32), "down": ((1, FF, D), F32), **{n: ((1, D, D), F32) for n in MATRICES}}
    scratch = {"wide": ((len(blocks), BLK + AQ, D), F32)}
    return kernel(name, body, reads, done, news, scratch, sems=2 * len(blocks), outside=("up", "down", *MATRICES), nbytes=3 * 10**6 * len(blocks))


def vector_finish(pos, mine, other):
    def body(s):
        own = (s["pos"][CORE] == 0).astype(F32)
        values = jnp.where(own > 0.5, s["mine"][...].astype(F32), s["other"][...].astype(F32))
        for i in VECTORS:
            s[str(i)][...] = values[i : i + 1, :]
        for j in range(NBLK):
            s[str(C1)][:, j * BLK : j * BLK + BLK] = values[C1 + j : C1 + j + 1, :]

    news = {**{str(i): ((1, D), F32) for i in VECTORS}, str(C1): ((1, FF), F32)}
    return kernel("vector_finish", body, {"pos": pos, "mine": mine, "other": other}, {}, news, free=news, nbytes=10**5)


def spot(y, z, x, core):
    return ((y * 2 + z) * 4 + x) * 2 + core


def everywhere(move):
    return [(spot(y, z, x, c), spot(*move(y, z, x, c))) for y in range(4) for z in range(2) for x in range(4) for c in range(2)]


def along(stage, distance):
    def move(y, z, x, core):
        if (core == 0) == (stage == 0):
            return y, z, (x + distance) % 4, core
        return (y + distance) % 4, z, x, core

    return everywhere(move)


def send(value, route):
    return lax.ppermute(value, "dp", route)


def to_core(value):
    return send(value, everywhere(lambda y, z, x, core: (y, z, x, 1 - core)))


def to_z(value):
    return send(value, everywhere(lambda y, z, x, core: (y, 1 - z, x, core)))


def spread(pieces, stage):
    sent = {k: send(pieces[k], along(stage, k)) for k in (1, 3, 2)}
    return [pieces[0]] + [sent[k] for k in (1, 2, 3)]


def shards(tokens, segments, cotangent, w_query, q_bias, w_key, w_value, v_bias, w_out, out_bias, ln1_gain, ln1_shift, w_up, up_bias, w_down, down_bias, ln2_gain, ln2_shift):
    dp = lax.axis_index("dp")
    core, x, y = dp % 2, (dp // 2) % 4, dp // 16
    first, second = jnp.where(core == 0, x, y), jnp.where(core == 0, y, x)
    here = jnp.stack([lax.axis_index("section"), core, first, second]).astype(jnp.int32)
    outside = {"here": here, "in_h": tokens, "in_seg": segments, "in_cot": cotangent}
    outside.update(in_wq=w_query, in_wk=w_key, in_wv=w_value, in_wo=w_out, in_w1=w_up, in_w2=w_down)
    vectors = {BQ: q_bias, BV: v_bias, BO: out_bias, G1: ln1_gain, S1: ln1_shift, C2: down_bias, G2: ln2_gain, S2: ln2_shift, C1: up_bias}
    outside.update({f"in_{i}": v for i, v in vectors.items()})

    def forth(value):
        return lax.ppermute(value, "section", [(0, 1)])

    def back(value):
        return lax.ppermute(value, "section", [(1, 0)])

    state = {}
    came, dcame = [], []
    for row in range(ROWS):
        sent, state = first_forward(row, outside, state)
        came.append(forth(sent))
    for row in range(ROWS):
        sent, state = second_both(row, came[row], state)
        dcame.append(back(sent))
    pos = state["pos"]

    def flat(*names):
        return {n: state[n].reshape((T2, state[n].shape[-1])) for n in names}

    dresid, state = first_feed(0, dcame[0], state)
    state = first_attention(0, dresid, state)
    dresid, state = first_feed(1, dcame[1], state)
    feed_ops = flat("u", "a", "e1", "e2")
    feed_in = to_core(feed_send(pos, feed_ops))
    state = first_attention(1, dresid, state)
    feeds = feed_keep(pos, feed_ops, feed_in)
    att_ops = flat("o", "h", "e0", "dq", "dk", "dv")
    att_out, att_vec = attention_send(pos, att_ops, {"ln": state["ln"], **flat("e1", "e2"), "after": feeds[0]})
    atts = attention_keep(pos, att_ops, att_vec, to_core(att_out))
    pieces = sum_split(pos, spread(feeds, 0), spread(atts, 0))
    mine = sum_four(spread(pieces, 1))
    shard, vec = sum_two(mine, to_z(mine))
    block = join(pos, spread([shard] * 4, 1))
    blocks = spread([block] * 4, 0)
    others = [to_core(b) for b in blocks]
    g = vector_finish(pos, vec, to_core(vec))
    full = finish(pos, "finish_own", [(blocks[0], True, 0), (others[0], False, 0)], {})
    full = finish(pos, "finish_mine", [(blocks[k], True, k) for k in (1, 3, 2)], full)
    full = finish(pos, "finish_other", [(others[k], False, k) for k in (1, 3, 2)], full)

    def vector(i):
        return g[str(i)]

    return (
        state["y"][None],
        state["dh"][None],
        full["q"],
        vector(BQ),
        full["k"],
        full["v"],
        vector(BV),
        full["o"],
        vector(BO),
        vector(G1),
        vector(S1),
        full["up"],
        vector(C1),
        full["down"],
        vector(C2),
        vector(G2),
        vector(S2),
    )


def solution(mesh):
    row, matrix, vector = P("dp", None, None), P("section", None, None), P("section", None)
    in_specs = (row, P("dp", None), row, matrix, vector, matrix, matrix, vector, matrix, vector, vector, vector, matrix, vector, matrix, vector, vector, vector)
    big = P("section", "dp", None, None)
    out_specs = (big, big, matrix, vector, matrix, matrix, vector, matrix, vector, vector, vector, matrix, vector, matrix, vector, vector, vector)
    return jax.shard_map(shards, mesh=mesh, in_specs=in_specs, out_specs=out_specs, check_vma=False)
```

```python
import functools

import jax
import jax.numpy as jnp
from jax import lax
from jax.experimental import pallas as pl
from jax.experimental.pallas import tpu as pltpu
from jax.sharding import PartitionSpec as P

BF, F32 = jnp.bfloat16, jnp.float32
ROWS, L, D, FF, HEADS, HEAD = 2, 256, 512, 2048, 8, 64
BLK = 512
NBLK = FF // BLK
NARROW = 256
GELU = 0.7978845608028654
VEC = 16
MiB = 1 << 20
SCALE = HEAD ** (-0.5)
BQ, BV, BO, G1, S1, C2, G2, S2, C1 = 0, 1, 2, 3, 4, 5, 6, 7, 8
SEC, CORE, FIRST, SECOND = 0, 1, 2, 3


def nn(a, b):
    return jnp.dot(a, b, preferred_element_type=F32)


def nt(a, b):
    return lax.dot_general(a, b, (((1,), (1,)), ((), ())), preferred_element_type=F32)


def tn(a, b):
    return lax.dot_general(a, b, (((0,), (0,)), ((), ())), preferred_element_type=F32)


def kernel(name, body, reads, updates, news, scratch=None, sems=0, outside=(), free=(), vmem=12, flops=0, nbytes=0):
    scratch = scratch or {}
    outs = {**updates, **news}
    names = list(reads) + list(updates)

    def spec(n):
        if n in outside:
            return pl.BlockSpec(memory_space=pltpu.HBM)
        if n in ("pos", "here"):
            return pl.BlockSpec(memory_space=pltpu.SMEM)
        return pl.BlockSpec(memory_space=pltpu.VMEM)

    def shape(n):
        if n == "pos":
            return pltpu.SMEM(*news[n])
        space = pltpu.HBM if n in outside else jax.ShapeDtypeStruct if n in free else pltpu.VMEM
        return space(*news[n]) if n in news else space(updates[n].shape, updates[n].dtype)

    reads = {n: pltpu.with_memory_space_constraint(v, pltpu.HBM) if n in outside else v for n, v in reads.items()}

    def whole(*refs):
        s = dict(zip(reads, refs))
        rest = refs[len(names) :]
        s.update(zip(outs, rest))
        s.update(zip(list(scratch) + ["sems"], rest[len(outs) :]))
        body(s)

    got = pl.pallas_call(
        whole,
        out_shape=[shape(n) for n in outs],
        in_specs=[spec(n) for n in names],
        out_specs=[spec(n) for n in outs],
        scratch_shapes=[pltpu.VMEM(*v) for v in scratch.values()] + ([pltpu.SemaphoreType.DMA((sems,))] if sems else []),
        input_output_aliases={len(reads) + i: i for i in range(len(updates))},
        compiler_params=pltpu.CompilerParams(vmem_limit_bytes=vmem * MiB),
        cost_estimate=pl.CostEstimate(flops=flops, bytes_accessed=nbytes, transcendentals=0),
        name=name,
    )(*reads.values(), *updates.values())
    return dict(zip(outs, got))


def norm_forward(resid, gain, shift):
    centre = resid - jnp.mean(resid, -1, keepdims=True)
    rstd = lax.rsqrt(jnp.mean(centre * centre, -1, keepdims=True) + 1e-05)
    unit = centre * rstd
    return unit, rstd, unit * gain + shift


def norm_backward(grad, unit, rstd, gain):
    scaled = grad * gain
    inner = scaled - jnp.mean(scaled, -1, keepdims=True)
    return rstd * (inner - unit * jnp.mean(scaled * unit, -1, keepdims=True))


def pair_lanes(pair):
    return slice(pair * 2 * HEAD, (pair + 1) * 2 * HEAD)


def lane_masks():
    lane = lax.broadcasted_iota(jnp.int32, (L, 128), 1)
    low = (lane < HEAD).astype(F32)
    return low.astype(BF), (1.0 - low).astype(BF), lane < HEAD


ROW = dict(
    h=((L, D), BF),
    y=((L, D), BF),
    o=((L, D), BF),
    u=((L, D), BF),
    a=((L, FF), BF),
    q=((L, D), BF),
    k=((L, D), BF),
    v=((L, D), BF),
    p=((HEADS * L, L), BF),
    gp=((L, FF), BF),
    x1=((L, D), F32),
    x2=((L, D), F32),
    rs=((L, 256), F32),
    e2=((L, D), BF),
    e1=((L, FF), BF),
    e0=((L, D), BF),
    dq=((L, D), BF),
    dk=((L, D), BF),
    dv=((L, D), BF),
    ln=((8, D), F32),
    dh=((L, D), F32),
)
FORWARD = ("h", "y", "o", "u", "a", "q", "k", "v", "p", "gp", "x1", "x2", "rs")
BACKWARD = ("e2", "e1", "e0", "dq", "dk", "dv", "ln", "dh")
WEIGHTS = dict(wq=((D, D), BF), wk=((D, D), BF), wv=((D, D), BF), wo=((D, D), BF), w1=((D, FF), BF), w2=((FF, D), BF))


def both_rows(names):
    return {n: ((ROWS,) + ROW[n][0], ROW[n][1]) for n in names}


def of_row(s, row, names):
    return {**s, **{n: s[n].at[row] for n in names}}


def forward(s, need, row):
    need("wq")
    hidden = s["h"][...]

    def vec(i):
        return s["vec"][i : i + 1, :]

    s["q"][...] = (nn(hidden, s["wq"][...]) + vec(BQ)).astype(BF)
    need("wk")
    s["k"][...] = nn(hidden, s["wk"][...]).astype(BF)
    need("wv")
    s["v"][...] = (nn(hidden, s["wv"][...]) + vec(BV)).astype(BF)
    seg = jnp.broadcast_to(s["seg"][row : row + 1, :].astype(F32), (L, L))
    same = seg == seg.T
    low, high, is_low = lane_masks()
    for head in range(HEADS):
        cols, rows = pair_lanes(head // 2), slice(head * L, head * L + L)
        scores = nt(s["q"][:, cols] * ((high if head % 2 else low) * SCALE), s["k"][:, cols])
        scores = jnp.where(same, scores, -1000000000.0)
        weight = jnp.exp(scores - jnp.max(scores, -1, keepdims=True))
        s["p"][rows, :] = (weight * (1.0 / jnp.sum(weight, -1, keepdims=True))).astype(BF)
    for pair in range(HEADS // 2):
        cols = pair_lanes(pair)
        both = nn(s["p"][pair * 2 * L : (pair + 1) * 2 * L, :], s["v"][:, cols])
        s["o"][:, cols] = jnp.where(is_low, both[:L], both[L:]).astype(BF)
    need("wo")
    resid = hidden.astype(F32) + nn(s["o"][...], s["wo"][...]) + vec(BO)
    unit, rstd, normed = norm_forward(resid, vec(G1), vec(S1))
    s["x1"][...] = unit
    s["rs"][:, :128] = jnp.broadcast_to(rstd, (L, 128))
    s["u"][...] = normed.astype(BF)
    need("w1")
    need("w2")
    total = normed + vec(C2)
    for j in range(FF // NARROW):
        cols = slice(j * NARROW, (j + 1) * NARROW)
        at = j * NARROW % BLK
        z = nn(s["u"][...], s["w1"][:, cols]) + vec(C1 + j * NARROW // BLK)[:, at : at + NARROW]
        square = z * z
        half = 0.5 + 0.5 * jnp.tanh(z * (GELU + (0.044715 * GELU) * square))
        active = z * half
        s["gp"][:, cols] = (half + (active * (2.0 - 2.0 * half)) * (GELU + (0.134145 * GELU) * square)).astype(BF)
        active = active.astype(BF)
        s["a"][:, cols] = active
        total = total + nn(active, s["w2"][cols, :])
    unit, rstd, out = norm_forward(total, vec(G2), vec(S2))
    s["y"][...] = out.astype(BF)
    s["x2"][...] = unit
    s["rs"][:, 128:] = jnp.broadcast_to(rstd, (L, 128))


BACK = dict(do=((L, D), BF), dsc=((HEADS * L, L), BF))


def backward_feed(s):
    gain1, gain2 = s["vec"][G1 : G1 + 1, :], s["vec"][G2 : G2 + 1, :]
    dout = s["dy"][...].astype(F32)
    unit = s["x2"][...]
    g_gain2 = jnp.sum(dout * unit, 0, keepdims=True)
    g_shift2 = jnp.sum(dout, 0, keepdims=True)
    dsecond = norm_backward(dout, unit, s["rs"][:, 128:129], gain2)
    s["e2"][...] = dsecond.astype(BF)
    for j in range(NBLK):
        cols = slice(j * BLK, j * BLK + BLK)
        dactive = nt(s["e2"][...], s["w2"][cols, :])
        s["e1"][:, cols] = (s["gp"][:, cols].astype(F32) * dactive).astype(BF)
    total = dsecond + nt(s["e1"][...], s["w1"][...])
    unit = s["x1"][...]
    g_gain1 = jnp.sum(total * unit, 0, keepdims=True)
    g_shift1 = jnp.sum(total, 0, keepdims=True)
    dresid = norm_backward(total, unit, s["rs"][:, 0:1], gain1)
    s["r1"][...] = dresid
    s["e0"][...] = dresid.astype(BF)
    s["ln"][...] = jnp.concatenate([g_gain2, g_shift2, g_gain1, g_shift1, jnp.zeros((4, D), F32)], 0)


def backward_attention(s):
    s["do"][...] = nt(s["e0"][...], s["wo"][...]).astype(BF)
    low, high, is_low = lane_masks()
    for pair in range(HEADS // 2):
        cols, rows = pair_lanes(pair), slice(pair * 2 * L, (pair + 1) * 2 * L)
        grad = s["do"][:, cols]
        dprobs = nt(jnp.concatenate([grad * low, grad * high], 0), s["v"][:, cols])
        probs = s["p"][rows, :].astype(F32)
        product = probs * dprobs
        s["dsc"][rows, :] = (product - probs * jnp.sum(product, -1, keepdims=True)).astype(BF)
    for pair in range(HEADS // 2):
        cols, rows = pair_lanes(pair), slice(pair * 2 * L, (pair + 1) * 2 * L)
        one, two = (slice((2 * pair + i) * L, (2 * pair + i + 1) * L) for i in range(2))
        both = nn(s["dsc"][rows, :], s["k"][:, cols])
        s["dq"][:, cols] = (jnp.where(is_low, both[:L], both[L:]) * SCALE).astype(BF)
        query, grad = s["q"][:, cols], s["do"][:, cols]
        s["dk"][:, cols] = (jnp.where(is_low, tn(s["dsc"][one, :], query), tn(s["dsc"][two, :], query)) * SCALE).astype(BF)
        s["dv"][:, cols] = jnp.where(is_low, tn(s["p"][one, :], grad), tn(s["p"][two, :], grad)).astype(BF)
    grad = s["r1"][...] + nt(s["dq"][...], s["wq"][...])
    grad = grad + nt(s["dk"][...], s["wk"][...]) + nt(s["dv"][...], s["wv"][...])
    s["ds"][...] = grad.astype(BF)
    s["dh"][...] = grad


VECTORS = (BQ, BV, BO, G1, S1, C2, G2, S2)


def first_forward(row, outside, state):
    if row == 0:
        reads, updates = outside, {}
        news = {**WEIGHTS, "vec": ((VEC, D), F32), "seg": ((ROWS, L), jnp.int32), "cot": ((ROWS, L, D), BF), "pos": ((4,), jnp.int32)}
        news.update(both_rows(FORWARD))
    else:
        keep = ("vec", "seg", "pos", *WEIGHTS)
        reads, updates = {n: state[n] for n in keep}, {n: state[n] for n in FORWARD}
        news = {}
    news["sent"] = ROW["y"]

    def body(s):
        copies = {}
        late = [n for n in WEIGHTS if n not in ("wq", "wk", "wv")] if row == 0 else []

        def start(n, source, target):
            copies[n] = pltpu.make_async_copy(source, target, s["sems"].at[len(copies)])
            copies[n].start()

        def need(n):
            if n in waiting:
                copies[waiting.pop(waiting.index(n))].wait()
            if n == "wv" and late:
                for m in late:
                    start(m, s["in_" + m].at[0], s[m])
                    waiting.append(m)
                start("cot", s["in_cot"], s["cot"])
                waiting.append("cot")

        if row == 0:
            start("h", s["in_h"], s["h"])
            start("wq", s["in_wq"].at[0], s["wq"])
            for i in VECTORS:
                start(i, s[f"in_{i}"], s["vec"].at[pl.ds(i, 1), :])
            for n in ("wk", "wv"):
                start(n, s["in_" + n].at[0], s[n])
            start("seg", s["in_seg"], s["seg"])
            for j in range(NBLK):
                start(C1 + j, s[f"in_{C1}"].at[:, pl.ds(j * BLK, BLK)], s["vec"].at[pl.ds(C1 + j, 1), :])
            for i in range(4):
                s["pos"][i] = s["here"][i]
            for n in ("h", "seg", *VECTORS, *range(C1, C1 + NBLK)):
                copies[n].wait()
        r = of_row(s, row, FORWARD)
        first = ["wq", "wk", "wv"] if row == 0 else []
        waiting = list(first)

        @pl.when(s["pos" if row else "here"][SEC] == 0)
        def _():
            forward(r, need, row)
            s["sent"][...] = r["y"][...]
            need("cot")

        if row == 0:
            for n in (*late, "cot"):
                copies.pop(n)
            waiting = list(first)

            @pl.when(s["here"][SEC] != 0)
            def _():
                for n in ("wv", "wq", "wk", *late, "cot"):
                    need(n)

    got = kernel(f"first_forward_{row}", body, reads, updates, news, sems=32 * (row == 0), outside=[n for n in reads if n.startswith("in_")], flops=3 * 10**9, nbytes=8 * 10**6)
    return got.pop("sent"), {**state, **got}


def second_both(row, arrived, state):
    reads = {n: state[n] for n in ("vec", "seg", "pos", "cot", *WEIGHTS)}
    reads["arrived"] = arrived
    updates = {n: state[n] for n in FORWARD}
    news = {"ds": ROW["y"]}
    if row == 0:
        news.update(both_rows(BACKWARD))
    else:
        updates.update({n: state[n] for n in BACKWARD})

    def body(s):
        r = of_row(s, row, FORWARD + BACKWARD)
        r["dy"] = s["cot"].at[row]

        @pl.when(s["pos"][SEC] == 1)
        def _():
            r["h"][...] = s["arrived"][...]
            forward(r, lambda n: None, row)
            backward_feed(r)
            backward_attention(r)

    got = kernel(f"second_both_{row}", body, reads, updates, news, {**BACK, "r1": ROW["dh"]}, flops=6 * 10**9, nbytes=8 * 10**6)
    return got.pop("ds"), {**state, **got}


def first_feed(row, arrived, state):
    reads = {n: state[n] for n in ("vec", "pos", "w1", "w2", "x1", "x2", "rs", "gp")}
    reads["dy"] = arrived
    keep = ("e2", "e1", "e0", "ln")

    def body(s):
        @pl.when(s["pos"][SEC] == 0)
        def _():
            backward_feed(of_row(s, row, ("x1", "x2", "rs", "gp", *keep)))

    got = kernel(f"first_feed_{row}", body, reads, {n: state[n] for n in keep}, {"r1": ROW["dh"]}, flops=10**9, nbytes=8 * 10**6)
    return got.pop("r1"), {**state, **got}


def first_attention(row, dresid, state):
    reads = {n: state[n] for n in ("pos", "wq", "wk", "wv", "wo", "e0", "q", "k", "v", "p")}
    reads["r1"] = dresid
    keep = ("dq", "dk", "dv", "dh")

    def body(s):
        @pl.when(s["pos"][SEC] == 0)
        def _():
            backward_attention(of_row(s, row, ("e0", "q", "k", "v", "p", *keep)))

    got = kernel(f"first_attention_{row}", body, reads, {n: state[n] for n in keep}, {}, {**BACK, "ds": ROW["y"]}, flops=2 * 10**9, nbytes=8 * 10**6)
    return {**state, **got}


T2 = ROWS * L
AQ = D // 2


def aligned(index, size):
    return pl.multiple_of(index * size, size)


def feed_block(s, up, j):
    cols = pl.ds(aligned(j, BLK), BLK)
    if up:
        return tn(s["u"][...], s["e1"][:, cols])
    return tn(s["a"][:, cols], s["e2"][...])


def per_core(s, work):
    for core in range(2):
        pl.when(s["pos"][CORE] == core)(functools.partial(work, core))


def feed_send(pos, ops):
    def body(s):
        def work(core):
            for j in range(NBLK):
                s["out"][j * BLK : j * BLK + BLK, :] = feed_block(s, core == 0, j).astype(BF)

        per_core(s, work)

    return kernel("feed_send", body, {"pos": pos, **ops}, {}, {"out": ((FF, D), BF)}, flops=2 * 10**9, nbytes=10**7)["out"]


def feed_keep(pos, ops, got):
    def body(s):
        def work(core):
            for k in (1, 3, 2, 0):
                j = lax.rem(s["pos"][FIRST] + k, 4)
                more = s["got"][pl.ds(aligned(j, BLK), BLK), :].astype(F32)
                s[f"p{k}"][...] = (feed_block(s, core == 1, j) + more).astype(BF)

        per_core(s, work)

    news = {f"p{k}": ((BLK, D), BF) for k in range(4)}
    return list(kernel("feed_keep", body, {"pos": pos, **ops, "got": got}, {}, news).values())


def attention_block(s, out, i):
    if out:
        return tn(s["o"][...], s["e0"][...]) if i == 0 else tn(s["h"][...], s["dq"][...])
    return tn(s["h"][...], s["dk" if i == 0 else "dv"][...])


def attention_send(pos, ops, more):
    def body(s):
        def work(core):
            for i in range(2):
                s["out"][i * D : i * D + D, :] = attention_block(s, core == 1, i).astype(BF)

        per_core(s, work)
        ones = jnp.ones((8, T2), BF)

        def total(value):
            return nn(ones, value)[0:1, :]

        ln = s["ln"][0] + s["ln"][1]
        rows = [total(s["dq"][...]), total(s["dv"][...]), total(s["e0"][...]), ln[2:3], ln[3:4], total(s["e2"][...]), ln[0:1], ln[1:2]]
        rows += [total(s["e1"][:, j * BLK : j * BLK + BLK]) for j in range(NBLK)]
        s["vec"][...] = jnp.concatenate(rows + [jnp.zeros((VEC - len(rows), D), F32)], 0).astype(BF)
        s["out"][2 * D :, :] = s["vec"][...]

    news = {"out": ((2 * D + VEC, D), BF), "vec": ((VEC, D), BF)}
    got = kernel("attention_send", body, {"pos": pos, **ops, **more}, {}, news)
    return got["out"], got["vec"]


def attention_keep(pos, ops, vec, got):
    def body(s):
        def work(core):
            for i in range(2):
                rows = slice(i * D, i * D + D)
                s["acc"][rows, :] = (attention_block(s, core == 0, i) + s["got"][rows, :].astype(F32)).astype(BF)

        per_core(s, work)
        shared = (s["vec"][...].astype(F32) + s["got"][2 * D :, :].astype(F32)).astype(BF)
        for k in range(4):
            j = lax.rem(s["pos"][FIRST] + k, 4)
            s[f"p{k}"][:AQ, :] = s["acc"][pl.ds(aligned(j, AQ), AQ), :]
            s[f"p{k}"][AQ:, :] = shared

    news = {f"p{k}": ((AQ + VEC, D), BF) for k in range(4)}
    reads = {"pos": pos, **ops, "vec": vec, "got": got}
    return list(kernel("attention_keep", body, reads, {}, news, {"acc": ((2 * D, D), BF)}).values())


def total_of(s):
    wide = [s[f"g{k}"][...].astype(F32) for k in range(4)]
    return ((wide[0] + wide[2]) + (wide[1] + wide[3])).astype(BF)


def total_of(s, tag):
    wide = [s[f"{tag}{k}"][...].astype(F32) for k in range(4)]
    return ((wide[0] + wide[2]) + (wide[1] + wide[3])).astype(BF)


def by_distance(tag, values):
    return {f"{tag}{k}": v for k, v in enumerate(values)}


FQ, TQ = BLK // 4, AQ // 4
SHARD = FQ + TQ


def sum_split(pos, feeds, atts):
    def body(s):
        s["feed"][...] = total_of(s, "f")
        s["att"][...] = total_of(s, "t")
        for k in range(4):
            j = lax.rem(s["pos"][SECOND] + k, 4)
            s[f"p{k}"][:FQ, :] = s["feed"][pl.ds(aligned(j, FQ), FQ), :]
            s[f"p{k}"][FQ:SHARD, :] = s["att"][pl.ds(aligned(j, TQ), TQ), :]
            s[f"p{k}"][SHARD:, :] = s["att"][AQ:, :]

    reads = {"pos": pos, **by_distance("f", feeds), **by_distance("t", atts)}
    news = {f"p{k}": ((SHARD + VEC, D), BF) for k in range(4)}
    scratch = {"feed": ((BLK, D), BF), "att": ((AQ + VEC, D), BF)}
    return list(kernel("sum_split", body, reads, {}, news, scratch).values())


def sum_four(got):
    def body(s):
        s["out"][...] = total_of(s, "g")

    return kernel("sum_four", body, by_distance("g", got), {}, {"out": (got[0].shape, BF)})["out"]


def sum_two(own, got):
    def body(s):
        total = (s["a"][...].astype(F32) + s["b"][...].astype(F32)).astype(BF)
        s["out"][...] = total[:SHARD]
        s["vec"][...] = total[SHARD:]

    got = kernel("sum_two", body, {"a": own, "b": got}, {}, {"out": ((SHARD, D), BF), "vec": ((VEC, D), BF)})
    return got["out"], got["vec"]


def join(pos, got):
    def body(s):
        for k in range(4):
            j = lax.rem(s["pos"][SECOND] + (4 - k), 4)
            s["out"][pl.ds(aligned(j, FQ), FQ), :] = s[f"g{k}"][:FQ, :]
            s["out"][pl.ds(aligned(j, TQ) + BLK, TQ), :] = s[f"g{k}"][FQ:, :]

    return kernel("join", body, {"pos": pos, **by_distance("g", got)}, {}, {"out": ((BLK + AQ, D), BF)})["out"]


MATRICES = ("o", "q", "k", "v")


def finish(pos, name, blocks, done):
    def body(s):
        sems = iter(range(2 * len(blocks)))
        started = []

        def move(source, target, sem):
            pltpu.make_async_copy(source, target, s["sems"].at[sem]).start()

        for i, (_, mine, k) in enumerate(blocks):
            s["wide"][i] = s[f"b{i}"][...].astype(F32)
            feed, att = s["wide"].at[i, pl.ds(0, BLK)], s["wide"].at[i, pl.ds(BLK, AQ)]
            piece = lax.rem(s["pos"][FIRST if mine else SECOND] + (4 - k), 4)
            down = (s["pos"][CORE] == 0) if mine else (s["pos"][CORE] == 1)
            sem = next(sems)

            @pl.when(down)
            def _():
                move(feed, s["down"].at[0, pl.ds(aligned(piece, BLK), BLK), :], sem)

            @pl.when(jnp.logical_not(down))
            def _():
                move(feed, s["up"].at[0, :, pl.ds(aligned(piece, BLK), BLK)], sem)

            started.append((feed, s["down"].at[0, pl.ds(0, BLK), :], sem))
            sem = next(sems)
            kind = jnp.where(down, 0, 2) + lax.div(piece, 2)
            at = aligned(lax.rem(piece, 2), AQ)
            for which, n in enumerate(MATRICES):

                @pl.when(kind == which)
                def _():
                    move(att, s[n].at[0, pl.ds(at, AQ), :], sem)

            started.append((att, s["o"].at[0, pl.ds(0, AQ), :], sem))
        for source, target, sem in started:
            pltpu.make_async_copy(source, target, s["sems"].at[sem]).wait()

    reads = {"pos": pos, **{f"b{i}": b[0] for i, b in enumerate(blocks)}}
    news = {} if done else {"up": ((1, D, FF), F32), "down": ((1, FF, D), F32), **{n: ((1, D, D), F32) for n in MATRICES}}
    scratch = {"wide": ((len(blocks), BLK + AQ, D), F32)}
    return kernel(name, body, reads, done, news, scratch, sems=2 * len(blocks), outside=("up", "down", *MATRICES))


def hold(values, after):
    updates = {f"x{i}": v for i, v in enumerate(values)}
    reads = {f"a{i}": v for i, v in enumerate(after)}
    return list(kernel("hold", lambda s: None, reads, updates, {}, outside=reads).values())


def store(y, dh):
    def body(s):
        moves = [pltpu.make_async_copy(s[n], s["out_" + n].at[0], s["sems"].at[i]) for i, n in enumerate(("y", "dh"))]
        for move in moves:
            move.start()
        for move in moves:
            move.wait()

    news = {"out_y": ((1, *y.shape), BF), "out_dh": ((1, *dh.shape), F32)}
    got = kernel("store", body, {"y": y, "dh": dh}, {}, news, sems=2, outside=news)
    return got["out_y"], got["out_dh"]


def vector_finish(pos, mine, other):
    def body(s):
        own = (s["pos"][CORE] == 0).astype(F32)
        values = jnp.where(own > 0.5, s["mine"][...].astype(F32), s["other"][...].astype(F32))
        for i in VECTORS:
            s[str(i)][...] = values[i : i + 1, :]
        for j in range(NBLK):
            s[str(C1)][:, j * BLK : j * BLK + BLK] = values[C1 + j : C1 + j + 1, :]

    news = {**{str(i): ((1, D), F32) for i in VECTORS}, str(C1): ((1, FF), F32)}
    return kernel("vector_finish", body, {"pos": pos, "mine": mine, "other": other}, {}, news, free=news)


def spot(y, z, x, core):
    return ((y * 2 + z) * 4 + x) * 2 + core


def everywhere(move):
    return [(spot(y, z, x, c), spot(*move(y, z, x, c))) for y in range(4) for z in range(2) for x in range(4) for c in range(2)]


def along(stage, distance):
    def move(y, z, x, core):
        if (core == 0) == (stage == 0):
            return y, z, (x + distance) % 4, core
        return (y + distance) % 4, z, x, core

    return everywhere(move)


def send(value, route):
    return lax.ppermute(value, "dp", route)


def to_core(value):
    return send(value, everywhere(lambda y, z, x, core: (y, z, x, 1 - core)))


def to_z(value):
    return send(value, everywhere(lambda y, z, x, core: (y, 1 - z, x, core)))


def spread(pieces, stage):
    sent = {k: send(pieces[k], along(stage, k)) for k in (1, 3, 2)}
    return [pieces[0]] + [sent[k] for k in (1, 2, 3)]


def shards(tokens, segments, cotangent, w_query, q_bias, w_key, w_value, v_bias, w_out, out_bias, ln1_gain, ln1_shift, w_up, up_bias, w_down, down_bias, ln2_gain, ln2_shift):
    dp = lax.axis_index("dp")
    core, x, y = dp % 2, (dp // 2) % 4, dp // 16
    first, second = jnp.where(core == 0, x, y), jnp.where(core == 0, y, x)
    here = jnp.stack([lax.axis_index("section"), core, first, second]).astype(jnp.int32)
    outside = {"here": here, "in_h": tokens, "in_seg": segments, "in_cot": cotangent}
    outside.update(in_wq=w_query, in_wk=w_key, in_wv=w_value, in_wo=w_out, in_w1=w_up, in_w2=w_down)
    vectors = {BQ: q_bias, BV: v_bias, BO: out_bias, G1: ln1_gain, S1: ln1_shift, C2: down_bias, G2: ln2_gain, S2: ln2_shift, C1: up_bias}
    outside.update({f"in_{i}": v for i, v in vectors.items()})

    def forth(value):
        return lax.ppermute(value, "section", [(0, 1)])

    def back(value):
        return lax.ppermute(value, "section", [(1, 0)])

    state = {}
    came, dcame = [], []
    for row in range(ROWS):
        sent, state = first_forward(row, outside, state)
        came.append(forth(sent))
    for row in range(ROWS):
        sent, state = second_both(row, came[row], state)
        dcame.append(back(sent))
    pos = state["pos"]

    def flat(*names):
        return {n: state[n].reshape((T2, state[n].shape[-1])) for n in names}

    dresid, state = first_feed(0, dcame[0], state)
    state = first_attention(0, dresid, state)
    dresid, state = first_feed(1, dcame[1], state)
    feed_ops = flat("u", "a", "e1", "e2")
    feed_in = to_core(feed_send(pos, feed_ops))
    state = first_attention(1, dresid, state)
    feeds = feed_keep(pos, feed_ops, feed_in)
    att_ops = flat("o", "h", "e0", "dq", "dk", "dv")
    att_out, att_vec = attention_send(pos, att_ops, {"ln": state["ln"], **flat("e1", "e2"), "after": feeds[0]})
    atts = attention_keep(pos, att_ops, att_vec, to_core(att_out))
    pieces = sum_split(pos, spread(feeds, 0), spread(atts, 0))
    mine = sum_four(spread(pieces, 1))
    shard, vec = sum_two(mine, to_z(mine))
    block = join(pos, spread([shard] * 4, 1))
    blocks = spread([block] * 4, 0)
    others = [to_core(block)]
    g = vector_finish(pos, vec, to_core(vec))
    full = finish(pos, "finish_own", [(blocks[0], True, 0), (others[0], False, 0)], {})
    y, dh = store(state["y"], state["dh"])
    held = hold(blocks[1:], [full["up"], y, dh, g[str(BQ)]])
    others = [to_core(b) for b in held]
    full = finish(pos, "finish_mine", [(held[k - 1], True, k) for k in (1, 3, 2)], full)
    full = finish(pos, "finish_other", [(others[k - 1], False, k) for k in (1, 3, 2)], full)

    def vector(i):
        return g[str(i)]

    return (
        y,
        dh,
        full["q"],
        vector(BQ),
        full["k"],
        full["v"],
        vector(BV),
        full["o"],
        vector(BO),
        vector(G1),
        vector(S1),
        full["up"],
        vector(C1),
        full["down"],
        vector(C2),
        vector(G2),
        vector(S2),
    )


def solution(mesh):
    row, matrix, vector = P("dp", None, None), P("section", None, None), P("section", None)
    in_specs = (row, P("dp", None), row, matrix, vector, matrix, matrix, vector, matrix, vector, vector, vector, matrix, vector, matrix, vector, vector, vector)
    big = P("section", "dp", None, None)
    out_specs = (big, big, matrix, vector, matrix, matrix, vector, matrix, vector, vector, vector, matrix, vector, matrix, vector, vector, vector)
    return jax.shard_map(shards, mesh=mesh, in_specs=in_specs, out_specs=out_specs, check_vma=False)
```

```python
import functools

import jax
import jax.numpy as jnp
from jax import lax
from jax.experimental import pallas as pl
from jax.experimental.pallas import tpu as pltpu
from jax.sharding import PartitionSpec as P

BF, F32 = jnp.bfloat16, jnp.float32
ROWS, L, D, FF, HEADS, HEAD = 2, 256, 512, 2048, 8, 64
BLK = 512
NBLK = FF // BLK
NARROW = 256
GELU = 0.7978845608028654
VEC = 16
MiB = 1 << 20
SCALE = HEAD ** (-0.5)
BQ, BV, BO, G1, S1, C2, G2, S2, C1 = 0, 1, 2, 3, 4, 5, 6, 7, 8
SEC, CORE, FIRST, SECOND = 0, 1, 2, 3


def nn(a, b):
    return jnp.dot(a, b, preferred_element_type=F32)


def nt(a, b):
    return lax.dot_general(a, b, (((1,), (1,)), ((), ())), preferred_element_type=F32)


def tn(a, b):
    return lax.dot_general(a, b, (((0,), (0,)), ((), ())), preferred_element_type=F32)


def kernel(name, body, reads, updates, news, scratch=None, sems=0, outside=(), free=(), vmem=12, flops=1000, nbytes=1000):
    scratch = scratch or {}
    outs = {**updates, **news}
    names = list(reads) + list(updates)

    def spec(n):
        if n in outside:
            return pl.BlockSpec(memory_space=pltpu.HBM)
        if n == "pos":
            return pl.BlockSpec(memory_space=pltpu.SMEM)
        return pl.BlockSpec(memory_space=pltpu.VMEM)

    def shape(n):
        if n == "pos":
            return pltpu.SMEM(*news[n])
        space = pltpu.HBM if n in outside else jax.ShapeDtypeStruct if n in free else pltpu.VMEM
        return space(*news[n]) if n in news else space(updates[n].shape, updates[n].dtype)

    reads = {n: pltpu.with_memory_space_constraint(v, pltpu.HBM) if n in outside else v for n, v in reads.items()}

    def whole(*refs):
        s = dict(zip(reads, refs))
        rest = refs[len(names) :]
        s.update(zip(outs, rest))
        s.update(zip(list(scratch) + ["sems"], rest[len(outs) :]))
        body(s)

    got = pl.pallas_call(
        whole,
        out_shape=[shape(n) for n in outs],
        in_specs=[spec(n) for n in names],
        out_specs=[spec(n) for n in outs],
        scratch_shapes=[pltpu.VMEM(*v) for v in scratch.values()] + ([pltpu.SemaphoreType.DMA((sems,))] if sems else []),
        input_output_aliases={len(reads) + i: i for i in range(len(updates))},
        compiler_params=pltpu.CompilerParams(vmem_limit_bytes=vmem * MiB),
        cost_estimate=pl.CostEstimate(flops=flops, bytes_accessed=nbytes, transcendentals=0),
        name=name,
    )(*reads.values(), *updates.values())
    return dict(zip(outs, got))


def norm_forward(resid, gain, shift):
    centre = resid - jnp.mean(resid, -1, keepdims=True)
    rstd = lax.rsqrt(jnp.mean(centre * centre, -1, keepdims=True) + 1e-05)
    unit = centre * rstd
    return unit, rstd, unit * gain + shift


def norm_backward(grad, unit, rstd, gain):
    scaled = grad * gain
    inner = scaled - jnp.mean(scaled, -1, keepdims=True)
    return rstd * (inner - unit * jnp.mean(scaled * unit, -1, keepdims=True))


def pair_lanes(pair):
    return slice(pair * 2 * HEAD, (pair + 1) * 2 * HEAD)


def lane_masks():
    lane = lax.broadcasted_iota(jnp.int32, (L, 128), 1)
    low = (lane < HEAD).astype(F32)
    return low.astype(BF), (1.0 - low).astype(BF), lane < HEAD


ROW = dict(
    h=((L, D), BF),
    y=((L, D), BF),
    o=((L, D), BF),
    u=((L, D), BF),
    a=((L, FF), BF),
    q=((L, D), BF),
    k=((L, D), BF),
    v=((L, D), BF),
    p=((HEADS * L, L), BF),
    gp=((L, FF), BF),
    x1=((L, D), F32),
    x2=((L, D), F32),
    rs=((L, 256), F32),
    e2=((L, D), BF),
    e1=((L, FF), BF),
    e0=((L, D), BF),
    dq=((L, D), BF),
    dk=((L, D), BF),
    dv=((L, D), BF),
    ln=((8, D), F32),
    dh=((L, D), F32),
)
FORWARD = ("h", "y", "o", "u", "a", "q", "k", "v", "p", "gp", "x1", "x2", "rs")
BACKWARD = ("e2", "e1", "e0", "dq", "dk", "dv", "ln", "dh")
WEIGHTS = dict(wq=((D, D), BF), wk=((D, D), BF), wv=((D, D), BF), wo=((D, D), BF), w1=((D, FF), BF), w2=((FF, D), BF))


def both_rows(names):
    return {n: ((ROWS,) + ROW[n][0], ROW[n][1]) for n in names}


def of_row(s, row, names):
    return {**s, **{n: s[n].at[row] for n in names}}


def forward(s, need, row):
    need("wq")
    hidden = s["h"][...]

    def vec(i):
        return s["vec"][i : i + 1, :]

    s["q"][...] = (nn(hidden, s["wq"][...]) + vec(BQ)).astype(BF)
    need("wk")
    s["k"][...] = nn(hidden, s["wk"][...]).astype(BF)
    need("wv")
    s["v"][...] = (nn(hidden, s["wv"][...]) + vec(BV)).astype(BF)
    seg = jnp.broadcast_to(s["seg"][row : row + 1, :].astype(F32), (L, L))
    same = seg == seg.T
    low, high, is_low = lane_masks()
    for head in range(HEADS):
        cols, rows = pair_lanes(head // 2), slice(head * L, head * L + L)
        scores = nt(s["q"][:, cols] * ((high if head % 2 else low) * SCALE), s["k"][:, cols])
        scores = jnp.where(same, scores, -1000000000.0)
        weight = jnp.exp(scores - jnp.max(scores, -1, keepdims=True))
        s["p"][rows, :] = (weight * (1.0 / jnp.sum(weight, -1, keepdims=True))).astype(BF)
    for pair in range(HEADS // 2):
        cols = pair_lanes(pair)
        both = nn(s["p"][pair * 2 * L : (pair + 1) * 2 * L, :], s["v"][:, cols])
        s["o"][:, cols] = jnp.where(is_low, both[:L], both[L:]).astype(BF)
    need("wo")
    resid = hidden.astype(F32) + nn(s["o"][...], s["wo"][...]) + vec(BO)
    unit, rstd, normed = norm_forward(resid, vec(G1), vec(S1))
    s["x1"][...] = unit
    s["rs"][:, :128] = jnp.broadcast_to(rstd, (L, 128))
    s["u"][...] = normed.astype(BF)
    need("w1")
    need("w2")
    s["x2"][...] = normed + vec(C2)
    for i in range(2):
        rows = slice(i * L // 2, (i + 1) * L // 2)
        total = s["x2"][rows, :]
        for j in range(FF // NARROW):
            cols = slice(j * NARROW, (j + 1) * NARROW)
            at = j * NARROW % BLK
            z = nn(s["u"][rows, :], s["w1"][:, cols]) + vec(C1 + j * NARROW // BLK)[:, at : at + NARROW]
            square = z * z
            half = 0.5 + 0.5 * jnp.tanh(z * (GELU + (0.044715 * GELU) * square))
            active = z * half
            s["gp"][rows, cols] = (half + (active * (2.0 - 2.0 * half)) * (GELU + (0.134145 * GELU) * square)).astype(BF)
            active = active.astype(BF)
            s["a"][rows, cols] = active
            total = total + nn(active, s["w2"][cols, :])
        s["x2"][rows, :] = total
    total = s["x2"][...]
    unit, rstd, out = norm_forward(total, vec(G2), vec(S2))
    s["y"][...] = out.astype(BF)
    s["x2"][...] = unit
    s["rs"][:, 128:] = jnp.broadcast_to(rstd, (L, 128))


BACK = dict(do=((L, D), BF), dsc=((HEADS * L, L), BF))


def backward_feed(s):
    gain1, gain2 = s["vec"][G1 : G1 + 1, :], s["vec"][G2 : G2 + 1, :]
    dout = s["dy"][...].astype(F32)
    unit = s["x2"][...]
    g_gain2 = jnp.sum(dout * unit, 0, keepdims=True)
    g_shift2 = jnp.sum(dout, 0, keepdims=True)
    dsecond = norm_backward(dout, unit, s["rs"][:, 128:129], gain2)
    s["e2"][...] = dsecond.astype(BF)
    for j in range(NBLK):
        cols = slice(j * BLK, j * BLK + BLK)
        dactive = nt(s["e2"][...], s["w2"][cols, :])
        s["e1"][:, cols] = (s["gp"][:, cols].astype(F32) * dactive).astype(BF)
    total = dsecond + nt(s["e1"][...], s["w1"][...])
    unit = s["x1"][...]
    g_gain1 = jnp.sum(total * unit, 0, keepdims=True)
    g_shift1 = jnp.sum(total, 0, keepdims=True)
    dresid = norm_backward(total, unit, s["rs"][:, 0:1], gain1)
    s["r1"][...] = dresid
    s["e0"][...] = dresid.astype(BF)
    s["ln"][...] = jnp.concatenate([g_gain2, g_shift2, g_gain1, g_shift1, jnp.zeros((4, D), F32)], 0)


def backward_attention(s):
    s["do"][...] = nt(s["e0"][...], s["wo"][...]).astype(BF)
    low, high, is_low = lane_masks()
    for pair in range(HEADS // 2):
        cols, rows = pair_lanes(pair), slice(pair * 2 * L, (pair + 1) * 2 * L)
        grad = s["do"][:, cols]
        dprobs = nt(jnp.concatenate([grad * low, grad * high], 0), s["v"][:, cols])
        probs = s["p"][rows, :].astype(F32)
        product = probs * dprobs
        s["dsc"][rows, :] = (product - probs * jnp.sum(product, -1, keepdims=True)).astype(BF)
    for pair in range(HEADS // 2):
        cols, rows = pair_lanes(pair), slice(pair * 2 * L, (pair + 1) * 2 * L)
        one, two = (slice((2 * pair + i) * L, (2 * pair + i + 1) * L) for i in range(2))
        both = nn(s["dsc"][rows, :], s["k"][:, cols])
        s["dq"][:, cols] = (jnp.where(is_low, both[:L], both[L:]) * SCALE).astype(BF)
        query, grad = s["q"][:, cols], s["do"][:, cols]
        s["dk"][:, cols] = (jnp.where(is_low, tn(s["dsc"][one, :], query), tn(s["dsc"][two, :], query)) * SCALE).astype(BF)
        s["dv"][:, cols] = jnp.where(is_low, tn(s["p"][one, :], grad), tn(s["p"][two, :], grad)).astype(BF)
    grad = s["r1"][...] + nt(s["dq"][...], s["wq"][...])
    grad = grad + nt(s["dk"][...], s["wk"][...]) + nt(s["dv"][...], s["wv"][...])
    s["ds"][...] = grad.astype(BF)
    s["dh"][...] = grad


VECTORS = (BQ, BV, BO, G1, S1, C2, G2, S2)


LOADED = {**WEIGHTS, "vec": ((VEC, D), F32), "seg": ((ROWS, L), jnp.int32), "cot": ((ROWS, L, D), BF)}


def first_forward(row, outside, state):
    if row == 0:
        reads, updates = outside, {}
        news = {**LOADED, "pos": ((4,), jnp.int32), **both_rows(FORWARD)}
    else:
        reads, updates = {**outside, "pos": state["pos"]}, {n: state[n] for n in (*LOADED, *FORWARD)}
        news = {}
    news["sent"] = ROW["y"]

    def body(s):
        copies, waiting = {}, []

        def start(n, source, target):
            copies[n] = pltpu.make_async_copy(source, target, s["sems"].at[len(copies)])
            copies[n].start()
            waiting.append(n)

        def need(n):
            if n in waiting:
                waiting.remove(n)
                copies[n].wait()
            if n == "wq" and "h" in copies and "wo" not in copies:
                for m in ("wo", "w1", "w2"):
                    start(m, s["in_" + m].at[0], s[m])
                start("cot", s["in_cot"], s["cot"])

        def load():
            start("h", s["in_h"], s["h"])
            start("wq", s["in_wq"].at[0], s["wq"])
            for i in VECTORS:
                start(i, s[f"in_{i}"], s["vec"].at[pl.ds(i, 1), :])
            for n in ("wk", "wv"):
                start(n, s["in_" + n].at[0], s[n])
            start("seg", s["in_seg"], s["seg"])
            for j in range(NBLK):
                start(C1 + j, s[f"in_{C1}"].at[:, pl.ds(j * BLK, BLK)], s["vec"].at[pl.ds(C1 + j, 1), :])

        if row == 0:
            place = pltpu.make_async_copy(s["in_pos"], s["pos"], s["sems"].at[SEMS - 1])
            place.start()
            place.wait()

        @pl.when(s["pos"][SEC] == 0)
        def _():
            if row == 0:
                load()
                for n in ("h", "seg", *VECTORS, *range(C1, C1 + NBLK)):
                    need(n)
            r = of_row(s, row, FORWARD)
            forward(r, need, row)
            s["sent"][...] = r["y"][...]
            need("cot")

        copies.clear()
        if row == 1:

            @pl.when(s["pos"][SEC] == 1)
            def _():
                load()
                need("wq")
                for n in list(waiting):
                    need(n)

    got = kernel(f"first_forward_{row}", body, reads, updates, news, sems=SEMS, outside=list(outside), flops=3 * 10**9, nbytes=8 * 10**6)
    return got.pop("sent"), {**state, **got}


SEMS = 32


def second_both(row, arrived, state):
    reads = {n: state[n] for n in ("vec", "seg", "pos", "cot", *WEIGHTS)}
    reads["arrived"] = arrived
    updates = {n: state[n] for n in FORWARD}
    news = {"ds": ROW["y"]}
    if row == 0:
        news.update(both_rows(BACKWARD))
    else:
        updates.update({n: state[n] for n in BACKWARD})

    def body(s):
        r = of_row(s, row, FORWARD + BACKWARD)
        r["dy"] = s["cot"].at[row]

        @pl.when(s["pos"][SEC] == 1)
        def _():
            r["h"][...] = s["arrived"][...]
            forward(r, lambda n: None, row)
            backward_feed(r)
            backward_attention(r)

    got = kernel(f"second_both_{row}", body, reads, updates, news, {**BACK, "r1": ROW["dh"]}, flops=6 * 10**9, nbytes=8 * 10**6)
    return got.pop("ds"), {**state, **got}


def first_feed(row, arrived, state, after):
    reads = {n: state[n] for n in ("vec", "pos", "w1", "w2", "x1", "x2", "rs", "gp")}
    reads.update(dy=arrived, **after)
    keep = ("e2", "e1", "e0", "ln")

    def body(s):
        @pl.when(s["pos"][SEC] == 0)
        def _():
            backward_feed(of_row(s, row, ("x1", "x2", "rs", "gp", *keep)))

    got = kernel(f"first_feed_{row}", body, reads, {n: state[n] for n in keep}, {"r1": ROW["dh"]}, flops=10**9, nbytes=8 * 10**6)
    return got.pop("r1"), {**state, **got}


def first_attention(row, dresid, state):
    reads = {n: state[n] for n in ("pos", "wq", "wk", "wv", "wo", "e0", "q", "k", "v", "p")}
    reads["r1"] = dresid
    keep = ("dq", "dk", "dv", "dh")

    def body(s):
        @pl.when(s["pos"][SEC] == 0)
        def _():
            backward_attention(of_row(s, row, ("e0", "q", "k", "v", "p", *keep)))

    got = kernel(f"first_attention_{row}", body, reads, {n: state[n] for n in keep}, {}, {**BACK, "ds": ROW["y"]}, flops=2 * 10**9, nbytes=8 * 10**6)
    return {**state, **got}


T2 = ROWS * L
AQ = D // 2


def aligned(index, size):
    return pl.multiple_of(index * size, size)


def per_core(s, work):
    for core in range(2):
        pl.when(s["pos"][CORE] == core)(functools.partial(work, core))


def feed_block(s, up, j, rows):
    cols = pl.ds(aligned(j, BLK), BLK)
    if up:
        return tn(s["u"][rows, :], s["e1"][rows, cols])
    return tn(s["a"][rows, cols], s["e2"][rows, :])


def attention_block(s, out, i, rows):
    left, right = (("o", "e0"), ("h", "dq"))[i] if out else ("h", ("dk", "dv")[i])
    return tn(s[left][rows, :], s[right][rows, :])


def vector_rows(s, row, rows):
    ones = jnp.ones((8, L), BF)

    def total(value):
        return nn(ones, value)[0:1, :]

    ln = s["ln"][row]
    got = [total(s[n][rows, :]) for n in ("dq", "dv", "e0")] + [ln[2:3], ln[3:4], total(s["e2"][rows, :]), ln[0:1], ln[1:2]]
    got += [total(s["e1"][rows, j * BLK : j * BLK + BLK]) for j in range(NBLK)]
    return jnp.concatenate(got + [jnp.zeros((VEC - len(got), D), F32)], 0)


FIRST_ROW, LAST_ROW = slice(0, L), slice(L, 2 * L)


def first_products(pos, ops):
    def body(s):
        def work(core):
            for j in range(NBLK):
                rows = slice(j * BLK, j * BLK + BLK)
                s["fs"][rows, :] = feed_block(s, core == 0, j, FIRST_ROW).astype(BF)
                s["fk"][rows, :] = feed_block(s, core == 1, j, FIRST_ROW).astype(BF)
            for i in range(2):
                rows = slice(i * D, i * D + D)
                s["ts"][rows, :] = attention_block(s, core == 1, i, FIRST_ROW).astype(BF)
                s["tk"][rows, :] = attention_block(s, core == 0, i, FIRST_ROW).astype(BF)

        per_core(s, work)
        s["vec"][...] = vector_rows(s, 0, FIRST_ROW)

    news = {"fs": ((FF, D), BF), "fk": ((FF, D), BF), "ts": ((2 * D, D), BF), "tk": ((2 * D, D), BF), "vec": ((VEC, D), F32)}
    return kernel("first_products", body, {"pos": pos, **ops}, {}, news)


def feed_send(pos, ops, early, distances, after):
    def body(s):
        def work(core):
            for i, k in enumerate(distances):
                j = lax.rem(s["pos"][SECOND] + k, 4)
                more = s["early"][pl.ds(aligned(j, BLK), BLK), :].astype(F32)
                s["out"][i * BLK : i * BLK + BLK, :] = (feed_block(s, core == 0, j, LAST_ROW) + more).astype(BF)

        per_core(s, work)

    return kernel("feed_send", body, {"pos": pos, **ops, "early": early, **after}, {}, {"out": ((len(distances) * BLK, D), BF)})["out"]


def attention_send(pos, ops, early, early_vec, after):
    def body(s):
        def work(core):
            for i in range(2):
                rows = slice(i * D, i * D + D)
                s["out"][rows, :] = (attention_block(s, core == 1, i, LAST_ROW) + s["early"][rows, :].astype(F32)).astype(BF)

        per_core(s, work)
        s["vec"][...] = (s["early_vec"][...] + vector_rows(s, 1, LAST_ROW)).astype(BF)
        s["out"][2 * D :, :] = s["vec"][...]

    news = {"out": ((2 * D + VEC, D), BF), "vec": ((VEC, D), BF)}
    got = kernel("attention_send", body, {"pos": pos, **ops, "early": early, "early_vec": early_vec, **after}, {}, news)
    return got["out"], got["vec"]


def feed_keep(pos, ops, early, distances, got, after):
    def body(s):
        def work(core):
            for i, k in enumerate(distances):
                j = lax.rem(s["pos"][FIRST] + k, 4)
                more = s["got"][i * BLK : i * BLK + BLK, :].astype(F32) + s["early"][pl.ds(aligned(j, BLK), BLK), :].astype(F32)
                s[f"p{k}"][...] = (feed_block(s, core == 1, j, LAST_ROW) + more).astype(BF)

        per_core(s, work)

    news = {f"p{k}": ((BLK, D), BF) for k in distances}
    return kernel("feed_keep", body, {"pos": pos, **ops, "early": early, "got": got, **after}, {}, news)


def attention_keep(pos, ops, early, vec, got):
    def body(s):
        def work(core):
            for i in range(2):
                rows = slice(i * D, i * D + D)
                more = s["got"][rows, :].astype(F32) + s["early"][rows, :].astype(F32)
                s["acc"][rows, :] = (attention_block(s, core == 0, i, LAST_ROW) + more).astype(BF)

        per_core(s, work)
        shared = (s["vec"][...].astype(F32) + s["got"][2 * D :, :].astype(F32)).astype(BF)
        for k in range(4):
            j = lax.rem(s["pos"][FIRST] + k, 4)
            s[f"p{k}"][:AQ, :] = s["acc"][pl.ds(aligned(j, AQ), AQ), :]
            s[f"p{k}"][AQ:, :] = shared

    news = {f"p{k}": ((AQ + VEC, D), BF) for k in range(4)}
    reads = {"pos": pos, **ops, "early": early, "vec": vec, "got": got}
    return list(kernel("attention_keep", body, reads, {}, news, {"acc": ((2 * D, D), BF)}).values())


def total_of(s, tag):
    wide = [s[f"{tag}{k}"][...].astype(F32) for k in range(4)]
    return ((wide[0] + wide[2]) + (wide[1] + wide[3])).astype(BF)


def by_distance(tag, values):
    return {f"{tag}{k}": v for k, v in enumerate(values)}


FQ, TQ = BLK // 4, AQ // 4
SHARD = FQ + TQ


def sum_split(pos, feed, atts):
    def body(s):
        s["att"][...] = total_of(s, "t")
        for k in range(4):
            j = lax.rem(s["pos"][SECOND] + k, 4)
            s[f"p{k}"][:FQ, :] = s["feed"][pl.ds(aligned(j, FQ), FQ), :]
            s[f"p{k}"][FQ:SHARD, :] = s["att"][pl.ds(aligned(j, TQ), TQ), :]
            s[f"p{k}"][SHARD:, :] = s["att"][AQ:, :]

    reads = {"pos": pos, "feed": feed, **by_distance("t", atts)}
    news = {f"p{k}": ((SHARD + VEC, D), BF) for k in range(4)}
    scratch = {"att": ((AQ + VEC, D), BF)}
    return list(kernel("sum_split", body, reads, {}, news, scratch).values())


def sum_four(got):
    def body(s):
        s["out"][...] = total_of(s, "g")

    return kernel("sum_four", body, by_distance("g", got), {}, {"out": (got[0].shape, BF)})["out"]


def sum_two(own, got):
    def body(s):
        total = (s["a"][...].astype(F32) + s["b"][...].astype(F32)).astype(BF)
        s["out"][...] = total[:SHARD]
        s["vec"][...] = total[SHARD:]

    got = kernel("sum_two", body, {"a": own, "b": got}, {}, {"out": ((SHARD, D), BF), "vec": ((VEC, D), BF)})
    return got["out"], got["vec"]


def join(pos, got):
    def body(s):
        for k in range(4):
            j = lax.rem(s["pos"][SECOND] + (4 - k), 4)
            s["out"][pl.ds(aligned(j, FQ), FQ), :] = s[f"g{k}"][:FQ, :]
            s["out"][pl.ds(aligned(j, TQ) + BLK, TQ), :] = s[f"g{k}"][FQ:, :]

    return kernel("join", body, {"pos": pos, **by_distance("g", got)}, {}, {"out": ((BLK + AQ, D), BF)})["out"]


MATRICES = ("o", "q", "k", "v")


def finish(pos, name, blocks, done):
    def body(s):
        sems = iter(range(2 * len(blocks)))
        started = []

        def move(source, target, sem):
            pltpu.make_async_copy(source, target, s["sems"].at[sem]).start()

        for i, (_, mine, k) in enumerate(blocks):
            parts = [s[f"b{i}{half}"] for half in "ab"[: len(blocks[i][0])]]
            rows = (BLK + AQ) // len(parts)
            for n, part in enumerate(parts):
                s["wide"][i, n * rows : (n + 1) * rows, :] = part[...].astype(F32)
            feed, att = s["wide"].at[i, pl.ds(0, BLK)], s["wide"].at[i, pl.ds(BLK, AQ)]
            piece = lax.rem(s["pos"][FIRST if mine else SECOND] + (4 - k), 4)
            down = (s["pos"][CORE] == 0) if mine else (s["pos"][CORE] == 1)
            sem = next(sems)

            @pl.when(down)
            def _():
                move(feed, s["down"].at[0, pl.ds(aligned(piece, BLK), BLK), :], sem)

            @pl.when(jnp.logical_not(down))
            def _():
                move(feed, s["up"].at[0, :, pl.ds(aligned(piece, BLK), BLK)], sem)

            started.append((feed, s["down"].at[0, pl.ds(0, BLK), :], sem))
            sem = next(sems)
            kind = jnp.where(down, 0, 2) + lax.div(piece, 2)
            at = aligned(lax.rem(piece, 2), AQ)
            for which, n in enumerate(MATRICES):

                @pl.when(kind == which)
                def _():
                    move(att, s[n].at[0, pl.ds(at, AQ), :], sem)

            started.append((att, s["o"].at[0, pl.ds(0, AQ), :], sem))
        for source, target, sem in started:
            pltpu.make_async_copy(source, target, s["sems"].at[sem]).wait()

    reads = {"pos": pos, **{f"b{i}{half}": b for i, block in enumerate(blocks) for half, b in zip("ab", block[0])}}
    news = {} if done else {"up": ((1, D, FF), F32), "down": ((1, FF, D), F32), **{n: ((1, D, D), F32) for n in MATRICES}}
    scratch = {"wide": ((len(blocks), BLK + AQ, D), F32)}
    return kernel(name, body, reads, done, news, scratch, sems=2 * len(blocks), outside=("up", "down", *MATRICES))


def halves(behind, ahead):
    half = behind.shape[0] // 2

    def body(s):
        s["up"][...] = s["behind"][:half, :]
        s["low"][...] = s["ahead"][half:, :]

    got = kernel("halves", body, {"behind": behind, "ahead": ahead}, {}, {"up": ((half, D), BF), "low": ((half, D), BF)})
    return got["up"], got["low"]


def hold(values, after):
    updates = {f"x{i}": v for i, v in enumerate(values)}
    reads = {f"a{i}": v for i, v in enumerate(after)}
    return list(kernel("hold", lambda s: None, reads, updates, {}, outside=reads).values())


def store(y, dh):
    def body(s):
        moves = [pltpu.make_async_copy(s[n], s["out_" + n].at[0], s["sems"].at[i]) for i, n in enumerate(("y", "dh"))]
        for move in moves:
            move.start()
        for move in moves:
            move.wait()

    news = {"out_y": ((1, *y.shape), BF), "out_dh": ((1, *dh.shape), F32)}
    got = kernel("store", body, {"y": y, "dh": dh}, {}, news, sems=2, outside=news)
    return got["out_y"], got["out_dh"]


def vector_finish(pos, mine, other):
    def body(s):
        own = (s["pos"][CORE] == 0).astype(F32)
        values = jnp.where(own > 0.5, s["mine"][...].astype(F32), s["other"][...].astype(F32))
        for i in VECTORS:
            s[str(i)][...] = values[i : i + 1, :]
        for j in range(NBLK):
            s[str(C1)][:, j * BLK : j * BLK + BLK] = values[C1 + j : C1 + j + 1, :]

    news = {**{str(i): ((1, D), F32) for i in VECTORS}, str(C1): ((1, FF), F32)}
    return kernel("vector_finish", body, {"pos": pos, "mine": mine, "other": other}, {}, news, free=news)


def spot(y, z, x, core):
    return ((y * 2 + z) * 4 + x) * 2 + core


def everywhere(move):
    return [(spot(y, z, x, c), spot(*move(y, z, x, c))) for y in range(4) for z in range(2) for x in range(4) for c in range(2)]


def along(stage, distance):
    def move(y, z, x, core):
        if (core == 0) == (stage == 0):
            return y, z, (x + distance) % 4, core
        return (y + distance) % 4, z, x, core

    return everywhere(move)


def send(value, route):
    return lax.ppermute(value, "dp", route)


def to_core(value):
    return send(value, everywhere(lambda y, z, x, core: (y, z, x, 1 - core)))


def to_z(value):
    return send(value, everywhere(lambda y, z, x, core: (y, 1 - z, x, core)))


def spread(pieces, stage):
    sent = {k: send(pieces[k], along(stage, k)) for k in (1, 3, 2)}
    return [pieces[0]] + [sent[k] for k in (1, 2, 3)]


def shards(tokens, segments, cotangent, w_query, q_bias, w_key, w_value, v_bias, w_out, out_bias, ln1_gain, ln1_shift, w_up, up_bias, w_down, down_bias, ln2_gain, ln2_shift):
    dp = lax.axis_index("dp")
    core, x, y = dp % 2, (dp // 2) % 4, dp // 16
    first, second = jnp.where(core == 0, x, y), jnp.where(core == 0, y, x)
    here = jnp.stack([lax.axis_index("section"), core, first, second]).astype(jnp.int32)
    outside = {"in_pos": here, "in_h": tokens, "in_seg": segments, "in_cot": cotangent}
    outside.update(in_wq=w_query, in_wk=w_key, in_wv=w_value, in_wo=w_out, in_w1=w_up, in_w2=w_down)
    vectors = {BQ: q_bias, BV: v_bias, BO: out_bias, G1: ln1_gain, S1: ln1_shift, C2: down_bias, G2: ln2_gain, S2: ln2_shift, C1: up_bias}
    outside.update({f"in_{i}": v for i, v in vectors.items()})

    def forth(value):
        return lax.ppermute(value, "section", [(0, 1)])

    def back(value):
        return lax.ppermute(value, "section", [(1, 0)])

    state = {}
    came, dcame = [], []
    for row in range(ROWS):
        sent, state = first_forward(row, outside, state)
        came.append(forth(sent))
    for row in range(ROWS):
        sent, state = second_both(row, came[row], state)
        dcame.append(back(sent))
    pos = state["pos"]

    def flat(*names):
        return {n: state[n].reshape((T2, state[n].shape[-1])) for n in names}

    dresid, state = first_feed(0, dcame[0], state, {})
    state = first_attention(0, dresid, state)
    names = ("u", "a", "o", "h", "e1", "e2", "e0", "dq", "dk", "dv")
    early = first_products(pos, {**flat(*names), "ln": state["ln"]})
    dresid, state = first_feed(1, dcame[1], state, {"after": early["vec"]})
    near, far = (1, 3), (2, 0)
    feed_ops = flat("u", "a", "e1", "e2")
    near_out = feed_send(pos, feed_ops, early["fs"], near, {})
    far_out = feed_send(pos, feed_ops, early["fs"], far, {"after": near_out})
    state = first_attention(1, dresid, state)
    feeds = feed_keep(pos, feed_ops, early["fk"], near, to_core(near_out), {})
    feeds.update(feed_keep(pos, feed_ops, early["fk"], far, to_core(far_out), {"after": feeds["p3"]}))
    ops = flat(*names)
    att_out, vec = attention_send(pos, {**ops, "ln": state["ln"]}, early["ts"], early["vec"], {"after": feeds["p2"]})
    atts = attention_keep(pos, flat("o", "h", "e0", "dq", "dk", "dv"), early["tk"], vec, to_core(att_out))
    pieces = sum_split(pos, sum_four(spread([feeds[f"p{k}"] for k in range(4)], 0)), spread(atts, 0))
    mine = sum_four(spread(pieces, 1))
    shard, vec = sum_two(mine, to_z(mine))
    block = join(pos, spread([shard] * 4, 1))
    g = vector_finish(pos, vec, to_core(vec))
    y, dh = store(state["y"], state["dh"])
    sides = {1: send(block, along(0, 1)), 3: send(block, along(0, 3))}
    full = finish(pos, "finish_own", [((block,), True, 0), ((to_core(block),), False, 0)], {})
    sides = dict(zip(sides, hold(list(sides.values()), [y, dh, g[str(BQ)], full["up"]])))
    up, low = halves(sides[1], sides[3])
    opposite = [send(up, along(0, 1)), send(low, along(0, 3))]
    others = {k: to_core(b) for k, b in sides.items()}
    full = finish(pos, "finish_sides", [((b,), True, k) for k, b in sides.items()], full)
    full = finish(pos, "finish_sides", [((b,), False, k) for k, b in others.items()], full)
    opposite = hold(opposite, [full["up"]])
    others = [to_core(b) for b in opposite]
    full = finish(pos, "finish_last", [(opposite, True, 2)], full)
    full = finish(pos, "finish_last", [(others, False, 2)], full)

    def vector(i):
        return g[str(i)]

    return (
        y,
        dh,
        full["q"],
        vector(BQ),
        full["k"],
        full["v"],
        vector(BV),
        full["o"],
        vector(BO),
        vector(G1),
        vector(S1),
        full["up"],
        vector(C1),
        full["down"],
        vector(C2),
        vector(G2),
        vector(S2),
    )


def solution(mesh):
    row, matrix, vector = P("dp", None, None), P("section", None, None), P("section", None)
    in_specs = (row, P("dp", None), row, matrix, vector, matrix, matrix, vector, matrix, vector, vector, vector, matrix, vector, matrix, vector, vector, vector)
    big = P("section", "dp", None, None)
    out_specs = (big, big, matrix, vector, matrix, matrix, vector, matrix, vector, vector, vector, matrix, vector, matrix, vector, vector, vector)
    return jax.shard_map(shards, mesh=mesh, in_specs=in_specs, out_specs=out_specs, check_vma=False)
```

```python
import functools

import jax
import jax.numpy as jnp
from jax import lax
from jax.experimental import pallas as pl
from jax.experimental.pallas import tpu as pltpu
from jax.sharding import PartitionSpec as P

BF, F32 = jnp.bfloat16, jnp.float32
ROWS, L, D, FF, HEADS, HEAD = 2, 256, 512, 2048, 8, 64
BLK = 512
NBLK = FF // BLK
NARROW = 256
GELU = 0.7978845608028654
VEC = 16
MiB = 1 << 20
SCALE = HEAD ** (-0.5)
BQ, BV, BO, G1, S1, C2, G2, S2, C1 = 0, 1, 2, 3, 4, 5, 6, 7, 8
SEC, CORE, FIRST, SECOND = 0, 1, 2, 3


def nn(a, b):
    return jnp.dot(a, b, preferred_element_type=F32)


def nt(a, b):
    return lax.dot_general(a, b, (((1,), (1,)), ((), ())), preferred_element_type=F32)


def tn(a, b):
    return lax.dot_general(a, b, (((0,), (0,)), ((), ())), preferred_element_type=F32)


def kernel(name, body, reads, updates, news, scratch=None, sems=0, outside=(), free=(), vmem=12, flops=1000, nbytes=1000):
    scratch = scratch or {}
    outs = {**updates, **news}
    names = list(reads) + list(updates)

    def spec(n):
        if n == "in_pos":
            return pl.BlockSpec(memory_space=pl.ANY)
        if n in outside:
            return pl.BlockSpec(memory_space=pltpu.HBM)
        if n == "pos":
            return pl.BlockSpec(memory_space=pltpu.SMEM)
        return pl.BlockSpec(memory_space=pltpu.VMEM)

    def shape(n):
        if n == "pos":
            return pltpu.SMEM(*news[n])
        space = pltpu.HBM if n in outside else jax.ShapeDtypeStruct if n in free else pltpu.VMEM
        return space(*news[n]) if n in news else space(updates[n].shape, updates[n].dtype)

    reads = {n: pltpu.with_memory_space_constraint(v, pltpu.HBM) if n in outside and n != "in_pos" else v for n, v in reads.items()}

    def whole(*refs):
        s = dict(zip(reads, refs))
        rest = refs[len(names) :]
        s.update(zip(outs, rest))
        s.update(zip(list(scratch) + ["sems"], rest[len(outs) :]))
        body(s)

    got = pl.pallas_call(
        whole,
        out_shape=[shape(n) for n in outs],
        in_specs=[spec(n) for n in names],
        out_specs=[spec(n) for n in outs],
        scratch_shapes=[pltpu.VMEM(*v) for v in scratch.values()] + ([pltpu.SemaphoreType.DMA((sems,))] if sems else []),
        input_output_aliases={len(reads) + i: i for i in range(len(updates))},
        compiler_params=pltpu.CompilerParams(vmem_limit_bytes=vmem * MiB),
        cost_estimate=pl.CostEstimate(flops=flops, bytes_accessed=nbytes, transcendentals=0),
        name=name,
    )(*reads.values(), *updates.values())
    return dict(zip(outs, got))


def norm_forward(resid, gain, shift):
    centre = resid - jnp.mean(resid, -1, keepdims=True)
    rstd = lax.rsqrt(jnp.mean(centre * centre, -1, keepdims=True) + 1e-05)
    unit = centre * rstd
    return unit, rstd, unit * gain + shift


def norm_backward(grad, unit, rstd, gain):
    scaled = grad * gain
    inner = scaled - jnp.mean(scaled, -1, keepdims=True)
    return rstd * (inner - unit * jnp.mean(scaled * unit, -1, keepdims=True))


def pair_lanes(pair):
    return slice(pair * 2 * HEAD, (pair + 1) * 2 * HEAD)


def lane_masks():
    lane = lax.broadcasted_iota(jnp.int32, (L, 128), 1)
    low = (lane < HEAD).astype(F32)
    return low.astype(BF), (1.0 - low).astype(BF), lane < HEAD


ROW = dict(
    h=((L, D), BF),
    y=((L, D), BF),
    o=((L, D), BF),
    u=((L, D), BF),
    a=((L, FF), BF),
    q=((L, D), BF),
    k=((L, D), BF),
    v=((L, D), BF),
    p=((HEADS * L, L), BF),
    gp=((L, FF), BF),
    x1=((L, D), F32),
    x2=((L, D), F32),
    rs=((L, 256), F32),
    e2=((L, D), BF),
    e1=((L, FF), BF),
    e0=((L, D), BF),
    dq=((L, D), BF),
    dk=((L, D), BF),
    dv=((L, D), BF),
    ln=((8, D), F32),
    dh=((L, D), F32),
)
FORWARD = ("h", "y", "o", "u", "a", "q", "k", "v", "p", "gp", "x1", "x2", "rs")
BACKWARD = ("e2", "e1", "e0", "dq", "dk", "dv", "ln", "dh")
WEIGHTS = dict(wq=((D, D), BF), wk=((D, D), BF), wv=((D, D), BF), wo=((D, D), BF), w1=((D, FF), BF), w2=((FF, D), BF))


def both_rows(names):
    return {n: ((ROWS,) + ROW[n][0], ROW[n][1]) for n in names}


def of_row(s, row, names):
    return {**s, **{n: s[n].at[row] for n in names}}


def forward(s, need, row):
    need("wq")
    hidden = s["h"][...]

    def vec(i):
        return s["vec"][i : i + 1, :]

    s["q"][...] = (nn(hidden, s["wq"][...]) + vec(BQ)).astype(BF)
    need("wk")
    s["k"][...] = nn(hidden, s["wk"][...]).astype(BF)
    need("wv")
    s["v"][...] = (nn(hidden, s["wv"][...]) + vec(BV)).astype(BF)
    seg = jnp.broadcast_to(s["seg"][row : row + 1, :].astype(F32), (L, L))
    same = seg == seg.T
    low, high, is_low = lane_masks()
    for head in range(HEADS):
        cols, rows = pair_lanes(head // 2), slice(head * L, head * L + L)
        scores = nt(s["q"][:, cols] * ((high if head % 2 else low) * SCALE), s["k"][:, cols])
        scores = jnp.where(same, scores, -1000000000.0)
        weight = jnp.exp(scores - jnp.max(scores, -1, keepdims=True))
        s["p"][rows, :] = (weight * (1.0 / jnp.sum(weight, -1, keepdims=True))).astype(BF)
    for pair in range(HEADS // 2):
        cols = pair_lanes(pair)
        both = nn(s["p"][pair * 2 * L : (pair + 1) * 2 * L, :], s["v"][:, cols])
        s["o"][:, cols] = jnp.where(is_low, both[:L], both[L:]).astype(BF)
    need("wo")
    resid = hidden.astype(F32) + nn(s["o"][...], s["wo"][...]) + vec(BO)
    unit, rstd, normed = norm_forward(resid, vec(G1), vec(S1))
    s["x1"][...] = unit
    s["rs"][:, :128] = jnp.broadcast_to(rstd, (L, 128))
    s["u"][...] = normed.astype(BF)
    need("w1")
    need("w2")
    total = normed + vec(C2)
    for j in range(FF // NARROW):
        cols = slice(j * NARROW, (j + 1) * NARROW)
        at = j * NARROW % BLK
        z = nn(s["u"][...], s["w1"][:, cols]) + vec(C1 + j * NARROW // BLK)[:, at : at + NARROW]
        square = z * z
        half = 0.5 + 0.5 * jnp.tanh(z * (GELU + (0.044715 * GELU) * square))
        active = z * half
        s["gp"][:, cols] = (half + (active * (2.0 - 2.0 * half)) * (GELU + (0.134145 * GELU) * square)).astype(BF)
        active = active.astype(BF)
        s["a"][:, cols] = active
        total = total + nn(active, s["w2"][cols, :])
    unit, rstd, out = norm_forward(total, vec(G2), vec(S2))
    s["y"][...] = out.astype(BF)
    s["x2"][...] = unit
    s["rs"][:, 128:] = jnp.broadcast_to(rstd, (L, 128))


BACK = dict(do=((L, D), BF), dsc=((HEADS * L, L), BF))


def backward_feed(s):
    gain1, gain2 = s["vec"][G1 : G1 + 1, :], s["vec"][G2 : G2 + 1, :]
    dout = s["dy"][...].astype(F32)
    unit = s["x2"][...]
    g_gain2 = jnp.sum(dout * unit, 0, keepdims=True)
    g_shift2 = jnp.sum(dout, 0, keepdims=True)
    dsecond = norm_backward(dout, unit, s["rs"][:, 128:129], gain2)
    s["e2"][...] = dsecond.astype(BF)
    for j in range(NBLK):
        cols = slice(j * BLK, j * BLK + BLK)
        dactive = nt(s["e2"][...], s["w2"][cols, :])
        s["e1"][:, cols] = (s["gp"][:, cols].astype(F32) * dactive).astype(BF)
    total = dsecond + nt(s["e1"][...], s["w1"][...])
    unit = s["x1"][...]
    g_gain1 = jnp.sum(total * unit, 0, keepdims=True)
    g_shift1 = jnp.sum(total, 0, keepdims=True)
    dresid = norm_backward(total, unit, s["rs"][:, 0:1], gain1)
    s["r1"][...] = dresid
    s["e0"][...] = dresid.astype(BF)
    s["ln"][...] = jnp.concatenate([g_gain2, g_shift2, g_gain1, g_shift1, jnp.zeros((4, D), F32)], 0)


def backward_attention(s):
    s["do"][...] = nt(s["e0"][...], s["wo"][...]).astype(BF)
    low, high, is_low = lane_masks()
    for pair in range(HEADS // 2):
        cols, rows = pair_lanes(pair), slice(pair * 2 * L, (pair + 1) * 2 * L)
        grad = s["do"][:, cols]
        dprobs = nt(jnp.concatenate([grad * low, grad * high], 0), s["v"][:, cols])
        probs = s["p"][rows, :].astype(F32)
        product = probs * dprobs
        s["dsc"][rows, :] = (product - probs * jnp.sum(product, -1, keepdims=True)).astype(BF)
    for pair in range(HEADS // 2):
        cols, rows = pair_lanes(pair), slice(pair * 2 * L, (pair + 1) * 2 * L)
        one, two = (slice((2 * pair + i) * L, (2 * pair + i + 1) * L) for i in range(2))
        both = nn(s["dsc"][rows, :], s["k"][:, cols])
        s["dq"][:, cols] = (jnp.where(is_low, both[:L], both[L:]) * SCALE).astype(BF)
        query, grad = s["q"][:, cols], s["do"][:, cols]
        s["dk"][:, cols] = (jnp.where(is_low, tn(s["dsc"][one, :], query), tn(s["dsc"][two, :], query)) * SCALE).astype(BF)
        s["dv"][:, cols] = jnp.where(is_low, tn(s["p"][one, :], grad), tn(s["p"][two, :], grad)).astype(BF)
    grad = s["r1"][...] + nt(s["dq"][...], s["wq"][...])
    grad = grad + nt(s["dk"][...], s["wk"][...]) + nt(s["dv"][...], s["wv"][...])
    s["ds"][...] = grad.astype(BF)
    s["dh"][...] = grad


VECTORS = (BQ, BV, BO, G1, S1, C2, G2, S2)


LOADED = {**WEIGHTS, "vec": ((VEC, D), F32), "seg": ((ROWS, L), jnp.int32), "cot": ((ROWS, L, D), BF)}


def first_forward(row, outside, state):
    if row == 0:
        reads, updates = outside, {}
        news = {**LOADED, "pos": ((4,), jnp.int32), **both_rows(FORWARD)}
    else:
        reads, updates = {**outside, "pos": state["pos"]}, {n: state[n] for n in (*LOADED, *FORWARD)}
        news = {}
    news["sent"] = ROW["y"]

    def body(s):
        copies, waiting = {}, []

        def start(n, source, target):
            copies[n] = pltpu.make_async_copy(source, target, s["sems"].at[len(copies)])
            copies[n].start()
            waiting.append(n)

        def rest():
            for m in ("wo", "w1", "w2"):
                start(m, s["in_" + m].at[0], s[m])
            start("cot", s["in_cot"], s["cot"])

        def need(n):
            if n in waiting:
                waiting.remove(n)
                copies[n].wait()
            if n == "wq" and row == 0:
                rest()

        def load():
            start("h", s["in_h"], s["h"])
            start("wq", s["in_wq"].at[0], s["wq"])
            for i in VECTORS:
                start(i, s[f"in_{i}"], s["vec"].at[pl.ds(i, 1), :])
            for n in ("wk", "wv"):
                start(n, s["in_" + n].at[0], s[n])
            start("seg", s["in_seg"], s["seg"])
            for j in range(NBLK):
                start(C1 + j, s[f"in_{C1}"].at[:, pl.ds(j * BLK, BLK)], s["vec"].at[pl.ds(C1 + j, 1), :])

        if row == 0:
            place = pltpu.make_async_copy(s["in_pos"], s["pos"], s["sems"].at[SEMS - 1])
            place.start()
            load()
            place.wait()
            first = list(waiting)

            @pl.when(s["pos"][SEC] == 1)
            def _():
                for n in first:
                    copies[n].wait()

        @pl.when(s["pos"][SEC] == 0)
        def _():
            if row == 0:
                for n in ("h", "seg", *VECTORS, *range(C1, C1 + NBLK)):
                    need(n)
            r = of_row(s, row, FORWARD)
            forward(r, need, row)
            s["sent"][...] = r["y"][...]
            need("cot")

        if row == 1:

            @pl.when(s["pos"][SEC] == 1)
            def _():
                rest()
                for n in list(waiting):
                    need(n)

    got = kernel(f"first_forward_{row}", body, reads, updates, news, sems=SEMS, outside=list(outside), flops=3 * 10**9, nbytes=8 * 10**6)
    return got.pop("sent"), {**state, **got}


SEMS = 32


def second_both(row, arrived, state):
    reads = {n: state[n] for n in ("vec", "seg", "pos", "cot", *WEIGHTS)}
    reads["arrived"] = arrived
    updates = {n: state[n] for n in FORWARD}
    news = {"ds": ROW["y"]}
    if row == 0:
        news.update(both_rows(BACKWARD))
    else:
        updates.update({n: state[n] for n in BACKWARD})

    def body(s):
        r = of_row(s, row, FORWARD + BACKWARD)
        r["dy"] = s["cot"].at[row]

        @pl.when(s["pos"][SEC] == 1)
        def _():
            r["h"][...] = s["arrived"][...]
            forward(r, lambda n: None, row)
            backward_feed(r)
            backward_attention(r)

    got = kernel(f"second_both_{row}", body, reads, updates, news, {**BACK, "r1": ROW["dh"]}, flops=6 * 10**9, nbytes=8 * 10**6)
    return got.pop("ds"), {**state, **got}


def first_feed(row, arrived, state, after):
    reads = {n: state[n] for n in ("vec", "pos", "w1", "w2", "x1", "x2", "rs", "gp")}
    reads.update(dy=arrived, **after)
    keep = ("e2", "e1", "e0", "ln")

    def body(s):
        @pl.when(s["pos"][SEC] == 0)
        def _():
            backward_feed(of_row(s, row, ("x1", "x2", "rs", "gp", *keep)))

    got = kernel(f"first_feed_{row}", body, reads, {n: state[n] for n in keep}, {"r1": ROW["dh"]}, flops=10**9, nbytes=8 * 10**6)
    return got.pop("r1"), {**state, **got}


def first_attention(row, dresid, state):
    reads = {n: state[n] for n in ("pos", "wq", "wk", "wv", "wo", "e0", "q", "k", "v", "p")}
    reads["r1"] = dresid
    keep = ("dq", "dk", "dv", "dh")

    def body(s):
        @pl.when(s["pos"][SEC] == 0)
        def _():
            backward_attention(of_row(s, row, ("e0", "q", "k", "v", "p", *keep)))

    got = kernel(f"first_attention_{row}", body, reads, {n: state[n] for n in keep}, {}, {**BACK, "ds": ROW["y"]}, flops=2 * 10**9, nbytes=8 * 10**6)
    return {**state, **got}


T2 = ROWS * L
AQ = D // 2


def aligned(index, size):
    return pl.multiple_of(index * size, size)


def per_core(s, work):
    for core in range(2):
        pl.when(s["pos"][CORE] == core)(functools.partial(work, core))


def feed_block(s, up, j, rows):
    cols = pl.ds(aligned(j, BLK), BLK)
    if up:
        return tn(s["u"][rows, :], s["e1"][rows, cols])
    return tn(s["a"][rows, cols], s["e2"][rows, :])


def attention_block(s, out, i, rows):
    left, right = (("o", "e0"), ("h", "dq"))[i] if out else ("h", ("dk", "dv")[i])
    return tn(s[left][rows, :], s[right][rows, :])


def vector_rows(s, row, rows):
    ones = jnp.ones((8, L), BF)

    def total(value):
        return nn(ones, value)[0:1, :]

    ln = s["ln"][row]
    got = [total(s[n][rows, :]) for n in ("dq", "dv", "e0")] + [ln[2:3], ln[3:4], total(s["e2"][rows, :]), ln[0:1], ln[1:2]]
    got += [total(s["e1"][rows, j * BLK : j * BLK + BLK]) for j in range(NBLK)]
    return jnp.concatenate(got + [jnp.zeros((VEC - len(got), D), F32)], 0)


FIRST_ROW, LAST_ROW = slice(0, L), slice(L, 2 * L)


def first_products(pos, ops):
    def body(s):
        def work(core):
            for j in range(NBLK):
                rows = slice(j * BLK, j * BLK + BLK)
                s["fs"][rows, :] = feed_block(s, core == 0, j, FIRST_ROW).astype(BF)
                s["fk"][rows, :] = feed_block(s, core == 1, j, FIRST_ROW).astype(BF)
            for i in range(2):
                rows = slice(i * D, i * D + D)
                s["ts"][rows, :] = attention_block(s, core == 1, i, FIRST_ROW).astype(BF)
                s["tk"][rows, :] = attention_block(s, core == 0, i, FIRST_ROW).astype(BF)

        per_core(s, work)
        s["vec"][...] = vector_rows(s, 0, FIRST_ROW)

    news = {"fs": ((FF, D), BF), "fk": ((FF, D), BF), "ts": ((2 * D, D), BF), "tk": ((2 * D, D), BF), "vec": ((VEC, D), F32)}
    return kernel("first_products", body, {"pos": pos, **ops}, {}, news)


def feed_send(pos, ops, early, distances, after):
    def body(s):
        def work(core):
            for i, k in enumerate(distances):
                j = lax.rem(s["pos"][SECOND] + k, 4)
                more = s["early"][pl.ds(aligned(j, BLK), BLK), :].astype(F32)
                s["out"][i * BLK : i * BLK + BLK, :] = (feed_block(s, core == 0, j, LAST_ROW) + more).astype(BF)

        per_core(s, work)

    return kernel("feed_send", body, {"pos": pos, **ops, "early": early, **after}, {}, {"out": ((len(distances) * BLK, D), BF)})["out"]


def attention_send(pos, ops, early, early_vec, after):
    def body(s):
        def work(core):
            for i in range(2):
                rows = slice(i * D, i * D + D)
                s["out"][rows, :] = (attention_block(s, core == 1, i, LAST_ROW) + s["early"][rows, :].astype(F32)).astype(BF)

        per_core(s, work)
        s["vec"][...] = (s["early_vec"][...] + vector_rows(s, 1, LAST_ROW)).astype(BF)
        s["out"][2 * D :, :] = s["vec"][...]

    news = {"out": ((2 * D + VEC, D), BF), "vec": ((VEC, D), BF)}
    got = kernel("attention_send", body, {"pos": pos, **ops, "early": early, "early_vec": early_vec, **after}, {}, news)
    return got["out"], got["vec"]


def feed_keep(pos, ops, early, distances, got, after):
    def body(s):
        def work(core):
            for i, k in enumerate(distances):
                j = lax.rem(s["pos"][FIRST] + k, 4)
                more = s["got"][i * BLK : i * BLK + BLK, :].astype(F32) + s["early"][pl.ds(aligned(j, BLK), BLK), :].astype(F32)
                s[f"p{k}"][...] = (feed_block(s, core == 1, j, LAST_ROW) + more).astype(BF)

        per_core(s, work)

    news = {f"p{k}": ((BLK, D), BF) for k in distances}
    return kernel("feed_keep", body, {"pos": pos, **ops, "early": early, "got": got, **after}, {}, news)


def attention_keep(pos, ops, early, vec, got):
    def body(s):
        def work(core):
            for i in range(2):
                rows = slice(i * D, i * D + D)
                more = s["got"][rows, :].astype(F32) + s["early"][rows, :].astype(F32)
                s["acc"][rows, :] = (attention_block(s, core == 0, i, LAST_ROW) + more).astype(BF)

        per_core(s, work)
        shared = (s["vec"][...].astype(F32) + s["got"][2 * D :, :].astype(F32)).astype(BF)
        for k in range(4):
            j = lax.rem(s["pos"][FIRST] + k, 4)
            s[f"p{k}"][:AQ, :] = s["acc"][pl.ds(aligned(j, AQ), AQ), :]
            s[f"p{k}"][AQ:, :] = shared

    news = {f"p{k}": ((AQ + VEC, D), BF) for k in range(4)}
    reads = {"pos": pos, **ops, "early": early, "vec": vec, "got": got}
    return list(kernel("attention_keep", body, reads, {}, news, {"acc": ((2 * D, D), BF)}).values())


def total_of(s, tag):
    wide = [s[f"{tag}{k}"][...].astype(F32) for k in range(4)]
    return ((wide[0] + wide[2]) + (wide[1] + wide[3])).astype(BF)


def by_distance(tag, values):
    return {f"{tag}{k}": v for k, v in enumerate(values)}


FQ, TQ = BLK // 4, AQ // 4
SHARD = FQ + TQ


def sum_split(pos, feed, atts):
    def body(s):
        s["att"][...] = total_of(s, "t")
        for k in range(4):
            j = lax.rem(s["pos"][SECOND] + k, 4)
            s[f"p{k}"][:FQ, :] = s["feed"][pl.ds(aligned(j, FQ), FQ), :]
            s[f"p{k}"][FQ:SHARD, :] = s["att"][pl.ds(aligned(j, TQ), TQ), :]
            s[f"p{k}"][SHARD:, :] = s["att"][AQ:, :]

    reads = {"pos": pos, "feed": feed, **by_distance("t", atts)}
    news = {f"p{k}": ((SHARD + VEC, D), BF) for k in range(4)}
    scratch = {"att": ((AQ + VEC, D), BF)}
    return list(kernel("sum_split", body, reads, {}, news, scratch).values())


def sum_four(got):
    def body(s):
        s["out"][...] = total_of(s, "g")

    return kernel("sum_four", body, by_distance("g", got), {}, {"out": (got[0].shape, BF)})["out"]


def sum_two(own, got):
    def body(s):
        total = (s["a"][...].astype(F32) + s["b"][...].astype(F32)).astype(BF)
        s["out"][...] = total[:SHARD]
        s["vec"][...] = total[SHARD:]

    got = kernel("sum_two", body, {"a": own, "b": got}, {}, {"out": ((SHARD, D), BF), "vec": ((VEC, D), BF)})
    return got["out"], got["vec"]


def join(pos, got):
    def body(s):
        for k in range(4):
            j = lax.rem(s["pos"][SECOND] + (4 - k), 4)
            s["out"][pl.ds(aligned(j, FQ), FQ), :] = s[f"g{k}"][:FQ, :]
            s["out"][pl.ds(aligned(j, TQ) + BLK, TQ), :] = s[f"g{k}"][FQ:, :]

    return kernel("join", body, {"pos": pos, **by_distance("g", got)}, {}, {"out": ((BLK + AQ, D), BF)})["out"]


MATRICES = ("o", "q", "k", "v")


def finish(pos, name, blocks, done):
    def body(s):
        sems = iter(range(2 * len(blocks)))
        started = []

        def move(source, target, sem):
            pltpu.make_async_copy(source, target, s["sems"].at[sem]).start()

        for i, (_, mine, k) in enumerate(blocks):
            parts = [s[f"b{i}{half}"] for half in "ab"[: len(blocks[i][0])]]
            rows = (BLK + AQ) // len(parts)
            for n, part in enumerate(parts):
                s["wide"][i, n * rows : (n + 1) * rows, :] = part[...].astype(F32)
            feed, att = s["wide"].at[i, pl.ds(0, BLK)], s["wide"].at[i, pl.ds(BLK, AQ)]
            piece = lax.rem(s["pos"][FIRST if mine else SECOND] + (4 - k), 4)
            down = (s["pos"][CORE] == 0) if mine else (s["pos"][CORE] == 1)
            sem = next(sems)

            @pl.when(down)
            def _():
                move(feed, s["down"].at[0, pl.ds(aligned(piece, BLK), BLK), :], sem)

            @pl.when(jnp.logical_not(down))
            def _():
                move(feed, s["up"].at[0, :, pl.ds(aligned(piece, BLK), BLK)], sem)

            started.append((feed, s["down"].at[0, pl.ds(0, BLK), :], sem))
            sem = next(sems)
            kind = jnp.where(down, 0, 2) + lax.div(piece, 2)
            at = aligned(lax.rem(piece, 2), AQ)
            for which, n in enumerate(MATRICES):

                @pl.when(kind == which)
                def _():
                    move(att, s[n].at[0, pl.ds(at, AQ), :], sem)

            started.append((att, s["o"].at[0, pl.ds(0, AQ), :], sem))
        for source, target, sem in started:
            pltpu.make_async_copy(source, target, s["sems"].at[sem]).wait()

    reads = {"pos": pos, **{f"b{i}{half}": b for i, block in enumerate(blocks) for half, b in zip("ab", block[0])}}
    news = {} if done else {"up": ((1, D, FF), F32), "down": ((1, FF, D), F32), **{n: ((1, D, D), F32) for n in MATRICES}}
    scratch = {"wide": ((len(blocks), BLK + AQ, D), F32)}
    return kernel(name, body, reads, done, news, scratch, sems=2 * len(blocks), outside=("up", "down", *MATRICES))


def halves(behind, ahead):
    half = behind.shape[0] // 2

    def body(s):
        s["up"][...] = s["behind"][:half, :]
        s["low"][...] = s["ahead"][half:, :]

    got = kernel("halves", body, {"behind": behind, "ahead": ahead}, {}, {"up": ((half, D), BF), "low": ((half, D), BF)})
    return got["up"], got["low"]


def hold(values, after):
    updates = {f"x{i}": v for i, v in enumerate(values)}
    reads = {f"a{i}": v for i, v in enumerate(after)}
    return list(kernel("hold", lambda s: None, reads, updates, {}, outside=reads).values())


def store(y, dh):
    def body(s):
        moves = [pltpu.make_async_copy(s[n], s["out_" + n].at[0], s["sems"].at[i]) for i, n in enumerate(("y", "dh"))]
        for move in moves:
            move.start()
        for move in moves:
            move.wait()

    news = {"out_y": ((1, *y.shape), BF), "out_dh": ((1, *dh.shape), F32)}
    got = kernel("store", body, {"y": y, "dh": dh}, {}, news, sems=2, outside=news)
    return got["out_y"], got["out_dh"]


def vector_finish(pos, mine, other):
    def body(s):
        own = (s["pos"][CORE] == 0).astype(F32)
        values = jnp.where(own > 0.5, s["mine"][...].astype(F32), s["other"][...].astype(F32))
        for i in VECTORS:
            s[str(i)][...] = values[i : i + 1, :]
        for j in range(NBLK):
            s[str(C1)][:, j * BLK : j * BLK + BLK] = values[C1 + j : C1 + j + 1, :]

    news = {**{str(i): ((1, D), F32) for i in VECTORS}, str(C1): ((1, FF), F32)}
    return kernel("vector_finish", body, {"pos": pos, "mine": mine, "other": other}, {}, news, free=news)


def spot(y, z, x, core):
    return ((y * 2 + z) * 4 + x) * 2 + core


def everywhere(move):
    return [(spot(y, z, x, c), spot(*move(y, z, x, c))) for y in range(4) for z in range(2) for x in range(4) for c in range(2)]


def along(stage, distance):
    def move(y, z, x, core):
        if (core == 0) == (stage == 0):
            return y, z, (x + distance) % 4, core
        return (y + distance) % 4, z, x, core

    return everywhere(move)


def send(value, route):
    return lax.ppermute(value, "dp", route)


def to_core(value):
    return send(value, everywhere(lambda y, z, x, core: (y, z, x, 1 - core)))


def to_z(value):
    return send(value, everywhere(lambda y, z, x, core: (y, 1 - z, x, core)))


def spread(pieces, stage):
    sent = {k: send(pieces[k], along(stage, k)) for k in (1, 3, 2)}
    return [pieces[0]] + [sent[k] for k in (1, 2, 3)]


def shards(tokens, segments, cotangent, w_query, q_bias, w_key, w_value, v_bias, w_out, out_bias, ln1_gain, ln1_shift, w_up, up_bias, w_down, down_bias, ln2_gain, ln2_shift):
    dp = lax.axis_index("dp")
    core, x, y = dp % 2, (dp // 2) % 4, dp // 16
    first, second = jnp.where(core == 0, x, y), jnp.where(core == 0, y, x)
    here = jnp.stack([lax.axis_index("section"), core, first, second]).astype(jnp.int32)
    outside = {"in_pos": here, "in_h": tokens, "in_seg": segments, "in_cot": cotangent}
    outside.update(in_wq=w_query, in_wk=w_key, in_wv=w_value, in_wo=w_out, in_w1=w_up, in_w2=w_down)
    vectors = {BQ: q_bias, BV: v_bias, BO: out_bias, G1: ln1_gain, S1: ln1_shift, C2: down_bias, G2: ln2_gain, S2: ln2_shift, C1: up_bias}
    outside.update({f"in_{i}": v for i, v in vectors.items()})

    def forth(value):
        return lax.ppermute(value, "section", [(0, 1)])

    def back(value):
        return lax.ppermute(value, "section", [(1, 0)])

    state = {}
    came, dcame = [], []
    for row in range(ROWS):
        sent, state = first_forward(row, outside, state)
        came.append(forth(sent))
    for row in range(ROWS):
        sent, state = second_both(row, came[row], state)
        dcame.append(back(sent))
    pos = state["pos"]

    def flat(*names):
        return {n: state[n].reshape((T2, state[n].shape[-1])) for n in names}

    dresid, state = first_feed(0, dcame[0], state, {})
    state = first_attention(0, dresid, state)
    names = ("u", "a", "o", "h", "e1", "e2", "e0", "dq", "dk", "dv")
    early = first_products(pos, {**flat(*names), "ln": state["ln"]})
    dresid, state = first_feed(1, dcame[1], state, {"after": early["vec"]})
    near, far = (1, 3), (2, 0)
    feed_ops = flat("u", "a", "e1", "e2")
    near_out = feed_send(pos, feed_ops, early["fs"], near, {})
    far_out = feed_send(pos, feed_ops, early["fs"], far, {"after": near_out})
    state = first_attention(1, dresid, state)
    feeds = feed_keep(pos, feed_ops, early["fk"], near, to_core(near_out), {})
    ops = flat(*names)
    att_out, vec = attention_send(pos, {**ops, "ln": state["ln"]}, early["ts"], early["vec"], {"after": feeds["p3"]})
    atts = attention_keep(pos, flat("o", "h", "e0", "dq", "dk", "dv"), early["tk"], vec, to_core(att_out))
    feeds.update(feed_keep(pos, feed_ops, early["fk"], far, to_core(far_out), {"after": atts[0]}))
    pieces = sum_split(pos, sum_four(spread([feeds[f"p{k}"] for k in range(4)], 0)), spread(atts, 0))
    mine = sum_four(spread(pieces, 1))
    shard, vec = sum_two(mine, to_z(mine))
    block = join(pos, spread([shard] * 4, 1))
    g = vector_finish(pos, vec, to_core(vec))
    y, dh = store(state["y"], state["dh"])
    sides = {1: send(block, along(0, 1)), 3: send(block, along(0, 3))}
    full = finish(pos, "finish_own", [((block,), True, 0), ((to_core(block),), False, 0)], {})
    sides = dict(zip(sides, hold(list(sides.values()), [y, dh, g[str(BQ)], full["up"]])))
    up, low = halves(sides[1], sides[3])
    opposite = [send(up, along(0, 1)), send(low, along(0, 3))]
    others = {k: to_core(b) for k, b in sides.items()}
    full = finish(pos, "finish_sides", [((b,), True, k) for k, b in sides.items()], full)
    full = finish(pos, "finish_sides", [((b,), False, k) for k, b in others.items()], full)
    opposite = hold(opposite, [full["up"]])
    others = [to_core(b) for b in opposite]
    full = finish(pos, "finish_last", [(opposite, True, 2)], full)
    full = finish(pos, "finish_last", [(others, False, 2)], full)

    def vector(i):
        return g[str(i)]

    return (
        y,
        dh,
        full["q"],
        vector(BQ),
        full["k"],
        full["v"],
        vector(BV),
        full["o"],
        vector(BO),
        vector(G1),
        vector(S1),
        full["up"],
        vector(C1),
        full["down"],
        vector(C2),
        vector(G2),
        vector(S2),
    )


def solution(mesh):
    row, matrix, vector = P("dp", None, None), P("section", None, None), P("section", None)
    in_specs = (row, P("dp", None), row, matrix, vector, matrix, matrix, vector, matrix, vector, vector, vector, matrix, vector, matrix, vector, vector, vector)
    big = P("section", "dp", None, None)
    out_specs = (big, big, matrix, vector, matrix, matrix, vector, matrix, vector, vector, vector, matrix, vector, matrix, vector, vector, vector)
    return jax.shard_map(shards, mesh=mesh, in_specs=in_specs, out_specs=out_specs, check_vma=False)
```

```python
import functools

import jax
import jax.numpy as jnp
from jax import lax
from jax.experimental import pallas as pl
from jax.experimental.pallas import tpu as pltpu
from jax.sharding import PartitionSpec as P

BF, F32 = jnp.bfloat16, jnp.float32
ROWS, L, D, FF, HEADS, HEAD = 2, 256, 512, 2048, 8, 64
BLK = 512
NBLK = FF // BLK
NARROW = 256
GELU = 0.7978845608028654
VEC = 16
MiB = 1 << 20
SCALE = HEAD ** (-0.5)
BQ, BV, BO, G1, S1, C2, G2, S2, C1 = 0, 1, 2, 3, 4, 5, 6, 7, 8
SEC, CORE, FIRST, SECOND = 0, 1, 2, 3


def nn(a, b):
    return jnp.dot(a, b, preferred_element_type=F32)


def nt(a, b):
    return lax.dot_general(a, b, (((1,), (1,)), ((), ())), preferred_element_type=F32)


def tn(a, b):
    return lax.dot_general(a, b, (((0,), (0,)), ((), ())), preferred_element_type=F32)


def kernel(name, body, reads, updates, news, scratch=None, sems=0, outside=(), free=(), vmem=12, flops=1000, nbytes=1000):
    scratch = scratch or {}
    outs = {**updates, **news}
    names = list(reads) + list(updates)

    def spec(n):
        if n == "in_pos":
            return pl.BlockSpec(memory_space=pl.ANY)
        if n in outside:
            return pl.BlockSpec(memory_space=pltpu.HBM)
        if n == "pos":
            return pl.BlockSpec(memory_space=pltpu.SMEM)
        return pl.BlockSpec(memory_space=pltpu.VMEM)

    def shape(n):
        if n == "pos":
            return pltpu.SMEM(*news[n])
        space = pltpu.HBM if n in outside else jax.ShapeDtypeStruct if n in free else pltpu.VMEM
        return space(*news[n]) if n in news else space(updates[n].shape, updates[n].dtype)

    reads = {n: pltpu.with_memory_space_constraint(v, pltpu.HBM) if n in outside and n != "in_pos" else v for n, v in reads.items()}

    def whole(*refs):
        s = dict(zip(reads, refs))
        rest = refs[len(names) :]
        s.update(zip(outs, rest))
        s.update(zip(list(scratch) + ["sems"], rest[len(outs) :]))
        body(s)

    got = pl.pallas_call(
        whole,
        out_shape=[shape(n) for n in outs],
        in_specs=[spec(n) for n in names],
        out_specs=[spec(n) for n in outs],
        scratch_shapes=[pltpu.VMEM(*v) for v in scratch.values()] + ([pltpu.SemaphoreType.DMA((sems,))] if sems else []),
        input_output_aliases={len(reads) + i: i for i in range(len(updates))},
        compiler_params=pltpu.CompilerParams(vmem_limit_bytes=vmem * MiB),
        cost_estimate=pl.CostEstimate(flops=flops, bytes_accessed=nbytes, transcendentals=0),
        name=name,
    )(*reads.values(), *updates.values())
    return dict(zip(outs, got))


def norm_forward(resid, gain, shift):
    centre = resid - jnp.mean(resid, -1, keepdims=True)
    rstd = lax.rsqrt(jnp.mean(centre * centre, -1, keepdims=True) + 1e-05)
    unit = centre * rstd
    return unit, rstd, unit * gain + shift


def norm_backward(grad, unit, rstd, gain):
    scaled = grad * gain
    inner = scaled - jnp.mean(scaled, -1, keepdims=True)
    return rstd * (inner - unit * jnp.mean(scaled * unit, -1, keepdims=True))


def pair_lanes(pair):
    return slice(pair * 2 * HEAD, (pair + 1) * 2 * HEAD)


def lane_masks():
    lane = lax.broadcasted_iota(jnp.int32, (L, 128), 1)
    low = (lane < HEAD).astype(F32)
    return low.astype(BF), (1.0 - low).astype(BF), lane < HEAD


ROW = dict(
    h=((L, D), BF),
    y=((L, D), BF),
    o=((L, D), BF),
    u=((L, D), BF),
    a=((L, FF), BF),
    q=((L, D), BF),
    k=((L, D), BF),
    v=((L, D), BF),
    p=((HEADS * L, L), BF),
    gp=((L, FF), BF),
    x1=((L, D), F32),
    x2=((L, D), F32),
    rs=((L, 256), F32),
    e2=((L, D), BF),
    e1=((L, FF), BF),
    e0=((L, D), BF),
    dq=((L, D), BF),
    dk=((L, D), BF),
    dv=((L, D), BF),
    ln=((8, D), F32),
    dh=((L, D), F32),
)
FORWARD = ("h", "y", "o", "u", "a", "q", "k", "v", "p", "gp", "x1", "x2", "rs")
BACKWARD = ("e2", "e1", "e0", "dq", "dk", "dv", "ln", "dh")
WEIGHTS = dict(wq=((D, D), BF), wk=((D, D), BF), wv=((D, D), BF), wo=((D, D), BF), w1=((D, FF), BF), w2=((FF, D), BF))


LATE = dict(z=((L, FF), F32), half=((L, FF), F32))


def both_rows(names):
    return {n: ((ROWS,) + ROW[n][0], ROW[n][1]) for n in names}


def of_row(s, row, names):
    return {**s, **{n: s[n].at[row] for n in names}}


def gelu_slope(z, half):
    return half + (z * half * (2.0 - 2.0 * half)) * (GELU + (0.134145 * GELU) * (z * z))


def forward(s, need, row, late):
    need("wq")
    hidden = s["h"][...]

    def vec(i):
        return s["vec"][i : i + 1, :]

    s["q"][...] = (nn(hidden, s["wq"][...]) + vec(BQ)).astype(BF)
    need("wk")
    s["k"][...] = nn(hidden, s["wk"][...]).astype(BF)
    need("wv")
    s["v"][...] = (nn(hidden, s["wv"][...]) + vec(BV)).astype(BF)
    seg = jnp.broadcast_to(s["seg"][row : row + 1, :].astype(F32), (L, L))
    same = seg == seg.T
    low, high, is_low = lane_masks()
    for head in range(HEADS):
        cols, rows = pair_lanes(head // 2), slice(head * L, head * L + L)
        scores = nt(s["q"][:, cols] * ((high if head % 2 else low) * SCALE), s["k"][:, cols])
        scores = jnp.where(same, scores, -1000000000.0)
        weight = jnp.exp(scores - jnp.max(scores, -1, keepdims=True))
        s["p"][rows, :] = (weight * (1.0 / jnp.sum(weight, -1, keepdims=True))).astype(BF)
    for pair in range(HEADS // 2):
        cols = pair_lanes(pair)
        both = nn(s["p"][pair * 2 * L : (pair + 1) * 2 * L, :], s["v"][:, cols])
        s["o"][:, cols] = jnp.where(is_low, both[:L], both[L:]).astype(BF)
    need("wo")
    resid = hidden.astype(F32) + nn(s["o"][...], s["wo"][...]) + vec(BO)
    unit, rstd, normed = norm_forward(resid, vec(G1), vec(S1))
    s["x1"][...] = unit
    s["rs"][:, :128] = jnp.broadcast_to(rstd, (L, 128))
    s["u"][...] = normed.astype(BF)
    need("w1")
    need("w2")
    total = normed + vec(C2)
    for j in range(FF // NARROW):
        cols = slice(j * NARROW, (j + 1) * NARROW)
        at = j * NARROW % BLK
        z = nn(s["u"][...], s["w1"][:, cols]) + vec(C1 + j * NARROW // BLK)[:, at : at + NARROW]
        square = z * z
        half = 0.5 + 0.5 * jnp.tanh(z * (GELU + (0.044715 * GELU) * square))
        if late:
            s["z"][:, cols] = z
            s["half"][:, cols] = half
        else:
            s["gp"][:, cols] = gelu_slope(z, half).astype(BF)
        active = (z * half).astype(BF)
        s["a"][:, cols] = active
        total = total + nn(active, s["w2"][cols, :])
    unit, rstd, out = norm_forward(total, vec(G2), vec(S2))
    s["y"][...] = out.astype(BF)
    s["x2"][...] = unit
    s["rs"][:, 128:] = jnp.broadcast_to(rstd, (L, 128))


BACK = dict(do=((L, D), BF), dsc=((HEADS * L, L), BF))


def backward_feed(s, late):
    gain1, gain2 = s["vec"][G1 : G1 + 1, :], s["vec"][G2 : G2 + 1, :]
    dout = s["dy"][...].astype(F32)
    unit = s["x2"][...]
    g_gain2 = jnp.sum(dout * unit, 0, keepdims=True)
    g_shift2 = jnp.sum(dout, 0, keepdims=True)
    dsecond = norm_backward(dout, unit, s["rs"][:, 128:129], gain2)
    s["e2"][...] = dsecond.astype(BF)
    for j in range(NBLK):
        cols = slice(j * BLK, j * BLK + BLK)
        dactive = nt(s["e2"][...], s["w2"][cols, :])
        slope = gelu_slope(s["z"][:, cols], s["half"][:, cols]) if late else s["gp"][:, cols].astype(F32)
        s["e1"][:, cols] = (slope * dactive).astype(BF)
    total = dsecond + nt(s["e1"][...], s["w1"][...])
    unit = s["x1"][...]
    g_gain1 = jnp.sum(total * unit, 0, keepdims=True)
    g_shift1 = jnp.sum(total, 0, keepdims=True)
    dresid = norm_backward(total, unit, s["rs"][:, 0:1], gain1)
    s["r1"][...] = dresid
    s["e0"][...] = dresid.astype(BF)
    s["ln"][...] = jnp.concatenate([g_gain2, g_shift2, g_gain1, g_shift1, jnp.zeros((4, D), F32)], 0)


def backward_attention(s):
    s["do"][...] = nt(s["e0"][...], s["wo"][...]).astype(BF)
    low, high, is_low = lane_masks()
    for pair in range(HEADS // 2):
        cols, rows = pair_lanes(pair), slice(pair * 2 * L, (pair + 1) * 2 * L)
        grad = s["do"][:, cols]
        dprobs = nt(jnp.concatenate([grad * low, grad * high], 0), s["v"][:, cols])
        probs = s["p"][rows, :].astype(F32)
        product = probs * dprobs
        s["dsc"][rows, :] = (product - probs * jnp.sum(product, -1, keepdims=True)).astype(BF)
    for pair in range(HEADS // 2):
        cols, rows = pair_lanes(pair), slice(pair * 2 * L, (pair + 1) * 2 * L)
        one, two = (slice((2 * pair + i) * L, (2 * pair + i + 1) * L) for i in range(2))
        both = nn(s["dsc"][rows, :], s["k"][:, cols])
        s["dq"][:, cols] = (jnp.where(is_low, both[:L], both[L:]) * SCALE).astype(BF)
        query, grad = s["q"][:, cols], s["do"][:, cols]
        s["dk"][:, cols] = (jnp.where(is_low, tn(s["dsc"][one, :], query), tn(s["dsc"][two, :], query)) * SCALE).astype(BF)
        s["dv"][:, cols] = jnp.where(is_low, tn(s["p"][one, :], grad), tn(s["p"][two, :], grad)).astype(BF)
    grad = s["r1"][...] + nt(s["dq"][...], s["wq"][...])
    grad = grad + nt(s["dk"][...], s["wk"][...]) + nt(s["dv"][...], s["wv"][...])
    s["ds"][...] = grad.astype(BF)
    s["dh"][...] = grad


VECTORS = (BQ, BV, BO, G1, S1, C2, G2, S2)


LOADED = {**WEIGHTS, "vec": ((VEC, D), F32), "seg": ((ROWS, L), jnp.int32), "cot": ((ROWS, L, D), BF)}


def first_forward(row, outside, state, here):
    if row == 0:
        reads, updates = {**outside, "here": here}, {}
        news = {**LOADED, **LATE, "pos": ((4,), jnp.int32), **both_rows(FORWARD)}
    else:
        reads = {**outside, "pos": state["pos"]}
        updates = {n: state[n] for n in (*LOADED, *FORWARD)}
        news = {}
    news["sent"] = ROW["y"]

    def body(s):
        copies, waiting = {}, []

        def start(n, source, target):
            copies[n] = pltpu.make_async_copy(source, target, s["sems"].at[len(copies)])
            copies[n].start()
            waiting.append(n)

        def rest():
            for m in ("wo", "w1", "w2"):
                start(m, s["in_" + m].at[0], s[m])
            start("cot", s["in_cot"], s["cot"])

        def need(n):
            if n in waiting:
                waiting.remove(n)
                copies[n].wait()
            if n == "wq" and row == 0:
                rest()

        def load():
            start("h", s["in_h"], s["h"])
            start("wq", s["in_wq"].at[0], s["wq"])
            for i in VECTORS:
                start(i, s[f"in_{i}"], s["vec"].at[pl.ds(i, 1), :])
            for n in ("wk", "wv"):
                start(n, s["in_" + n].at[0], s[n])
            start("seg", s["in_seg"], s["seg"])
            for j in range(NBLK):
                start(C1 + j, s[f"in_{C1}"].at[:, pl.ds(j * BLK, BLK)], s["vec"].at[pl.ds(C1 + j, 1), :])

        if row == 0:
            place = pltpu.make_async_copy(s["in_pos"], s["pos"], s["sems"].at[SEMS - 1])
            place.start()

        @pl.when((s["here"][0, 0] if row == 0 else s["pos"][SEC]) == 0)
        def _():
            if row == 0:
                load()
                for n in ("h", "seg", *VECTORS, *range(C1, C1 + NBLK)):
                    need(n)
            r = of_row(s, row, FORWARD)
            forward(r, need, row, row == 0)
            s["sent"][...] = r["y"][...]
            need("cot")

        if row == 0:
            place.wait()
        else:
            copies.clear()

            @pl.when(s["pos"][SEC] == 1)
            def _():
                load()
                rest()
                for n in list(waiting):
                    need(n)

    got = kernel(f"first_forward_{row}", body, reads, updates, news, sems=SEMS, outside=list(outside), flops=3 * 10**9, nbytes=8 * 10**6)
    return got.pop("sent"), {**state, **got}


SEMS = 32


def first_slopes(state):
    def body(s):
        @pl.when(s["pos"][SEC] == 0)
        def _():
            for j in range(FF // 128):
                cols = slice(j * 128, j * 128 + 128)
                s["gp"][0, :, cols] = gelu_slope(s["z"][:, cols], s["half"][:, cols]).astype(BF)

    return {**state, **kernel("first_slopes", body, {n: state[n] for n in ("pos", *LATE)}, {"gp": state["gp"]}, {})}


def second_both(row, arrived, state):
    reads = {n: state[n] for n in ("vec", "seg", "pos", "cot", *WEIGHTS)}
    reads["arrived"] = arrived
    updates = {n: state[n] for n in (*FORWARD, *LATE)}
    news = {"ds": ROW["y"]}
    if row == 0:
        news.update(both_rows(BACKWARD))
    else:
        updates.update({n: state[n] for n in BACKWARD})

    def body(s):
        r = of_row(s, row, FORWARD + BACKWARD)
        r["dy"] = s["cot"].at[row]

        @pl.when(s["pos"][SEC] == 1)
        def _():
            r["h"][...] = s["arrived"][...]
            forward(r, lambda n: None, row, True)
            backward_feed(r, True)
            backward_attention(r)

    got = kernel(f"second_both_{row}", body, reads, updates, news, {**BACK, "r1": ROW["dh"]}, flops=6 * 10**9, nbytes=8 * 10**6)
    return got.pop("ds"), {**state, **got}


def first_feed(row, arrived, state, after):
    reads = {n: state[n] for n in ("vec", "pos", "w1", "w2", "x1", "x2", "rs", "gp")}
    reads.update(dy=arrived, **after)
    keep = ("e2", "e1", "e0", "ln")

    def body(s):
        @pl.when(s["pos"][SEC] == 0)
        def _():
            backward_feed(of_row(s, row, ("x1", "x2", "rs", "gp", *keep)), False)

    got = kernel(f"first_feed_{row}", body, reads, {n: state[n] for n in keep}, {"r1": ROW["dh"]}, flops=10**9, nbytes=8 * 10**6)
    return got.pop("r1"), {**state, **got}


def first_attention(row, dresid, state):
    reads = {n: state[n] for n in ("pos", "wq", "wk", "wv", "wo", "e0", "q", "k", "v", "p")}
    reads["r1"] = dresid
    keep = ("dq", "dk", "dv", "dh")

    def body(s):
        @pl.when(s["pos"][SEC] == 0)
        def _():
            backward_attention(of_row(s, row, ("e0", "q", "k", "v", "p", *keep)))

    got = kernel(f"first_attention_{row}", body, reads, {n: state[n] for n in keep}, {}, {**BACK, "ds": ROW["y"]}, flops=2 * 10**9, nbytes=8 * 10**6)
    return {**state, **got}


T2 = ROWS * L
AQ = D // 2


def aligned(index, size):
    return pl.multiple_of(index * size, size)


def per_core(s, work):
    for core in range(2):
        pl.when(s["pos"][CORE] == core)(functools.partial(work, core))


def feed_block(s, up, j, rows):
    cols = pl.ds(aligned(j, BLK), BLK)
    if up:
        return tn(s["u"][rows, :], s["e1"][rows, cols])
    return tn(s["a"][rows, cols], s["e2"][rows, :])


def attention_block(s, out, i, rows):
    left, right = (("o", "e0"), ("h", "dq"))[i] if out else ("h", ("dk", "dv")[i])
    return tn(s[left][rows, :], s[right][rows, :])


def vector_rows(s, row, rows):
    ones = jnp.ones((8, L), BF)

    def total(value):
        return nn(ones, value)[0:1, :]

    ln = s["ln"][row]
    got = [total(s[n][rows, :]) for n in ("dq", "dv", "e0")] + [ln[2:3], ln[3:4], total(s["e2"][rows, :]), ln[0:1], ln[1:2]]
    got += [total(s["e1"][rows, j * BLK : j * BLK + BLK]) for j in range(NBLK)]
    return jnp.concatenate(got + [jnp.zeros((VEC - len(got), D), F32)], 0)


FIRST_ROW, LAST_ROW = slice(0, L), slice(L, 2 * L)


def first_products(pos, ops):
    def body(s):
        def work(core):
            for j in range(NBLK):
                rows = slice(j * BLK, j * BLK + BLK)
                s["fs"][rows, :] = feed_block(s, core == 0, j, FIRST_ROW).astype(BF)
                s["fk"][rows, :] = feed_block(s, core == 1, j, FIRST_ROW).astype(BF)
            for i in range(2):
                rows = slice(i * D, i * D + D)
                s["ts"][rows, :] = attention_block(s, core == 1, i, FIRST_ROW).astype(BF)
                s["tk"][rows, :] = attention_block(s, core == 0, i, FIRST_ROW).astype(BF)

        per_core(s, work)
        s["vec"][...] = vector_rows(s, 0, FIRST_ROW)

    news = {"fs": ((FF, D), BF), "fk": ((FF, D), BF), "ts": ((2 * D, D), BF), "tk": ((2 * D, D), BF), "vec": ((VEC, D), F32)}
    return kernel("first_products", body, {"pos": pos, **ops}, {}, news)


def feed_send(pos, ops, early, distances, after):
    def body(s):
        def work(core):
            for i, k in enumerate(distances):
                j = lax.rem(s["pos"][SECOND] + k, 4)
                more = s["early"][pl.ds(aligned(j, BLK), BLK), :].astype(F32)
                s["out"][i * BLK : i * BLK + BLK, :] = (feed_block(s, core == 0, j, LAST_ROW) + more).astype(BF)

        per_core(s, work)

    return kernel("feed_send", body, {"pos": pos, **ops, "early": early, **after}, {}, {"out": ((len(distances) * BLK, D), BF)})["out"]


def attention_send(pos, ops, early, early_vec, after):
    def body(s):
        def work(core):
            for i in range(2):
                rows = slice(i * D, i * D + D)
                s["out"][rows, :] = (attention_block(s, core == 1, i, LAST_ROW) + s["early"][rows, :].astype(F32)).astype(BF)

        per_core(s, work)
        s["vec"][...] = (s["early_vec"][...] + vector_rows(s, 1, LAST_ROW)).astype(BF)
        s["out"][2 * D :, :] = s["vec"][...]

    news = {"out": ((2 * D + VEC, D), BF), "vec": ((VEC, D), BF)}
    got = kernel("attention_send", body, {"pos": pos, **ops, "early": early, "early_vec": early_vec, **after}, {}, news)
    return got["out"], got["vec"]


def feed_keep(pos, ops, early, distances, got, after):
    def body(s):
        def work(core):
            for i, k in enumerate(distances):
                j = lax.rem(s["pos"][FIRST] + k, 4)
                more = s["got"][i * BLK : i * BLK + BLK, :].astype(F32) + s["early"][pl.ds(aligned(j, BLK), BLK), :].astype(F32)
                s[f"p{k}"][...] = (feed_block(s, core == 1, j, LAST_ROW) + more).astype(BF)

        per_core(s, work)

    news = {f"p{k}": ((BLK, D), BF) for k in distances}
    return kernel("feed_keep", body, {"pos": pos, **ops, "early": early, "got": got, **after}, {}, news)


def attention_keep(pos, ops, early, vec, got):
    def body(s):
        def work(core):
            for i in range(2):
                rows = slice(i * D, i * D + D)
                more = s["got"][rows, :].astype(F32) + s["early"][rows, :].astype(F32)
                s["acc"][rows, :] = (attention_block(s, core == 0, i, LAST_ROW) + more).astype(BF)

        per_core(s, work)
        shared = (s["vec"][...].astype(F32) + s["got"][2 * D :, :].astype(F32)).astype(BF)
        for k in range(4):
            j = lax.rem(s["pos"][FIRST] + k, 4)
            s[f"p{k}"][:AQ, :] = s["acc"][pl.ds(aligned(j, AQ), AQ), :]
            s[f"p{k}"][AQ:, :] = shared

    news = {f"p{k}": ((AQ + VEC, D), BF) for k in range(4)}
    reads = {"pos": pos, **ops, "early": early, "vec": vec, "got": got}
    return list(kernel("attention_keep", body, reads, {}, news, {"acc": ((2 * D, D), BF)}).values())


def total_of(s, tag):
    wide = [s[f"{tag}{k}"][...].astype(F32) for k in range(4)]
    return ((wide[0] + wide[2]) + (wide[1] + wide[3])).astype(BF)


def by_distance(tag, values):
    return {f"{tag}{k}": v for k, v in enumerate(values)}


FQ, TQ = BLK // 4, AQ // 4
SHARD = FQ + TQ


def sum_split(pos, feed, atts):
    def body(s):
        s["att"][...] = total_of(s, "t")
        for k in range(4):
            j = lax.rem(s["pos"][SECOND] + k, 4)
            s[f"p{k}"][:FQ, :] = s["feed"][pl.ds(aligned(j, FQ), FQ), :]
            s[f"p{k}"][FQ:SHARD, :] = s["att"][pl.ds(aligned(j, TQ), TQ), :]
            s[f"p{k}"][SHARD:, :] = s["att"][AQ:, :]

    reads = {"pos": pos, "feed": feed, **by_distance("t", atts)}
    news = {f"p{k}": ((SHARD + VEC, D), BF) for k in range(4)}
    scratch = {"att": ((AQ + VEC, D), BF)}
    return list(kernel("sum_split", body, reads, {}, news, scratch).values())


def sum_four(got):
    def body(s):
        s["out"][...] = total_of(s, "g")

    return kernel("sum_four", body, by_distance("g", got), {}, {"out": (got[0].shape, BF)})["out"]


def sum_two(own, got):
    def body(s):
        total = (s["a"][...].astype(F32) + s["b"][...].astype(F32)).astype(BF)
        s["out"][...] = total[:SHARD]
        s["vec"][...] = total[SHARD:]

    got = kernel("sum_two", body, {"a": own, "b": got}, {}, {"out": ((SHARD, D), BF), "vec": ((VEC, D), BF)})
    return got["out"], got["vec"]


HALF = (BLK + AQ) // 2


def join(pos, got, vec):
    def body(s):
        for k in range(4):
            j = lax.rem(s["pos"][SECOND] + (4 - k), 4)
            s["out"][pl.ds(aligned(j, FQ), FQ), :] = s[f"g{k}"][:FQ, :]
            s["out"][pl.ds(aligned(j, TQ) + BLK, TQ), :] = s[f"g{k}"][FQ:, :]
        s["out"][2 * HALF :, :] = s["vec"][...]
        s["up"][...] = s["out"][:HALF, :]
        s["low"][...] = s["out"][HALF : 2 * HALF, :]

    news = {"out": ((2 * HALF + VEC, D), BF), "up": ((HALF, D), BF), "low": ((HALF, D), BF)}
    return kernel("join", body, {"pos": pos, **by_distance("g", got), "vec": vec}, {}, news).values()


MATRICES = ("o", "q", "k", "v")


def finish(pos, name, blocks, done):
    def body(s):
        sems = iter(range(2 * len(blocks)))
        started = []

        def move(source, target, sem):
            pltpu.make_async_copy(source, target, s["sems"].at[sem]).start()

        for i, (_, mine, k) in enumerate(blocks):
            parts = [s[f"b{i}{half}"] for half in "ab"[: len(blocks[i][0])]]
            rows = 2 * HALF // len(parts)
            for n, part in enumerate(parts):
                s["wide"][i, n * rows : (n + 1) * rows, :] = part[:rows, :].astype(F32)
            feed, att = s["wide"].at[i, pl.ds(0, BLK)], s["wide"].at[i, pl.ds(BLK, AQ)]
            piece = lax.rem(s["pos"][FIRST if mine else SECOND] + (4 - k), 4)
            down = (s["pos"][CORE] == 0) if mine else (s["pos"][CORE] == 1)
            sem = next(sems)

            @pl.when(down)
            def _():
                move(feed, s["down"].at[0, pl.ds(aligned(piece, BLK), BLK), :], sem)

            @pl.when(jnp.logical_not(down))
            def _():
                move(feed, s["up"].at[0, :, pl.ds(aligned(piece, BLK), BLK)], sem)

            started.append((feed, s["down"].at[0, pl.ds(0, BLK), :], sem))
            sem = next(sems)
            kind = jnp.where(down, 0, 2) + lax.div(piece, 2)
            at = aligned(lax.rem(piece, 2), AQ)
            for which, n in enumerate(MATRICES):

                @pl.when(kind == which)
                def _():
                    move(att, s[n].at[0, pl.ds(at, AQ), :], sem)

            started.append((att, s["o"].at[0, pl.ds(0, AQ), :], sem))
        for source, target, sem in started:
            pltpu.make_async_copy(source, target, s["sems"].at[sem]).wait()

    reads = {"pos": pos, **{f"b{i}{half}": b for i, block in enumerate(blocks) for half, b in zip("ab", block[0])}}
    news = {} if done else {"up": ((1, D, FF), F32), "down": ((1, FF, D), F32), **{n: ((1, D, D), F32) for n in MATRICES}}
    scratch = {"wide": ((len(blocks), BLK + AQ, D), F32)}
    return kernel(name, body, reads, done, news, scratch, sems=2 * len(blocks), outside=("up", "down", *MATRICES))


def hold(values, stored=(), near=()):
    updates = {f"x{i}": v for i, v in enumerate(values)}
    outside = {f"a{i}": v for i, v in enumerate(stored)}
    reads = {**outside, **{f"b{i}": v for i, v in enumerate(near)}}
    return list(kernel("hold", lambda s: None, reads, updates, {}, outside=outside).values())


def store(y, dh):
    def body(s):
        moves = [pltpu.make_async_copy(s[n], s["out_" + n].at[0], s["sems"].at[i]) for i, n in enumerate(("y", "dh"))]
        for move in moves:
            move.start()
        for move in moves:
            move.wait()

    news = {"out_y": ((1, *y.shape), BF), "out_dh": ((1, *dh.shape), F32)}
    got = kernel("store", body, {"y": y, "dh": dh}, {}, news, sems=2, outside=news)
    return got["out_y"], got["out_dh"]


def vector_finish(pos, mine, other):
    def body(s):
        own = (s["pos"][CORE] == 0).astype(F32)
        values = jnp.where(own > 0.5, s["mine"][2 * HALF :, :].astype(F32), s["other"][2 * HALF :, :].astype(F32))
        for i in VECTORS:
            s[str(i)][...] = values[i : i + 1, :]
        for j in range(NBLK):
            s[str(C1)][:, j * BLK : j * BLK + BLK] = values[C1 + j : C1 + j + 1, :]

    news = {**{str(i): ((1, D), F32) for i in VECTORS}, str(C1): ((1, FF), F32)}
    return kernel("vector_finish", body, {"pos": pos, "mine": mine, "other": other}, {}, news, free=news)


def spot(y, z, x, core):
    return ((y * 2 + z) * 4 + x) * 2 + core


def everywhere(move):
    return [(spot(y, z, x, c), spot(*move(y, z, x, c))) for y in range(4) for z in range(2) for x in range(4) for c in range(2)]


def along(stage, distance):
    def move(y, z, x, core):
        if (core == 0) == (stage == 0):
            return y, z, (x + distance) % 4, core
        return (y + distance) % 4, z, x, core

    return everywhere(move)


def send(value, route):
    return lax.ppermute(value, "dp", route)


def to_core(value):
    return send(value, everywhere(lambda y, z, x, core: (y, z, x, 1 - core)))


def to_z(value):
    return send(value, everywhere(lambda y, z, x, core: (y, 1 - z, x, core)))


def spread(pieces, stage):
    sent = {k: send(pieces[k], along(stage, k)) for k in (1, 3, 2)}
    return [pieces[0]] + [sent[k] for k in (1, 2, 3)]


def shards(tokens, segments, cotangent, w_query, q_bias, w_key, w_value, v_bias, w_out, out_bias, ln1_gain, ln1_shift, w_up, up_bias, w_down, down_bias, ln2_gain, ln2_shift):
    dp = lax.axis_index("dp")
    core, x, y = dp % 2, (dp // 2) % 4, dp // 16
    first, second = jnp.where(core == 0, x, y), jnp.where(core == 0, y, x)
    here = jnp.stack([lax.axis_index("section"), core, first, second]).astype(jnp.int32)
    outside = {"in_pos": here, "in_h": tokens, "in_seg": segments, "in_cot": cotangent}
    outside.update(in_wq=w_query, in_wk=w_key, in_wv=w_value, in_wo=w_out, in_w1=w_up, in_w2=w_down)
    vectors = {BQ: q_bias, BV: v_bias, BO: out_bias, G1: ln1_gain, S1: ln1_shift, C2: down_bias, G2: ln2_gain, S2: ln2_shift, C1: up_bias}
    outside.update({f"in_{i}": v for i, v in vectors.items()})

    def forth(value):
        return lax.ppermute(value, "section", [(0, 1)])

    def back(value):
        return lax.ppermute(value, "section", [(1, 0)])

    state = {}
    came, dcame = [], []
    for row in range(ROWS):
        sent, state = first_forward(row, outside, state, jnp.broadcast_to(here[:1], (8, 128)))
        came.append(forth(sent))
    state = first_slopes(state)
    for row in range(ROWS):
        sent, state = second_both(row, came[row], state)
        dcame.append(back(sent))
    pos = state["pos"]

    def flat(*names):
        return {n: state[n].reshape((T2, state[n].shape[-1])) for n in names}

    dresid, state = first_feed(0, dcame[0], state, {})
    state = first_attention(0, dresid, state)
    names = ("u", "a", "o", "h", "e1", "e2", "e0", "dq", "dk", "dv")
    early = first_products(pos, {**flat(*names), "ln": state["ln"]})
    dresid, state = first_feed(1, dcame[1], state, {"after": early["vec"]})
    near, far = (1, 3), (2, 0)
    feed_ops = flat("u", "a", "e1", "e2")
    near_out = feed_send(pos, feed_ops, early["fs"], near, {})
    far_out = feed_send(pos, feed_ops, early["fs"], far, {"after": near_out})
    state = first_attention(1, dresid, state)
    feeds = feed_keep(pos, feed_ops, early["fk"], near, to_core(near_out), {})
    ops = flat(*names)
    att_out, vec = attention_send(pos, {**ops, "ln": state["ln"]}, early["ts"], early["vec"], {"after": feeds["p3"]})
    atts = attention_keep(pos, flat("o", "h", "e0", "dq", "dk", "dv"), early["tk"], vec, to_core(att_out))
    feeds.update(feed_keep(pos, feed_ops, early["fk"], far, to_core(far_out), {"after": atts[0]}))
    pieces = sum_split(pos, sum_four(spread([feeds[f"p{k}"] for k in range(4)], 0)), spread(atts, 0))
    mine = sum_four(spread(pieces, 1))
    shard, vec = sum_two(mine, to_z(mine))
    block, up, low = join(pos, spread([shard] * 4, 1), vec)
    up_behind, low_ahead = send(up, along(0, 1)), send(low, along(0, 3))
    low_behind, up_ahead = send(low, along(0, 1)), send(up, along(0, 3))
    other = to_core(block)
    y, dh = store(state["y"], state["dh"])
    g = vector_finish(pos, block, other)
    full = finish(pos, "finish_own", [((block,), True, 0), ((other,), False, 0)], {})
    up_behind, low_ahead = hold([up_behind, low_ahead], [y, dh, g[str(BQ)], full["up"]])
    opposite = [send(up_behind, along(0, 1)), send(low_ahead, along(0, 3))]
    low_behind, up_ahead = hold([low_behind, up_ahead], near=[up_behind, low_ahead])
    sides = [((up_behind, low_behind), 1), ((up_ahead, low_ahead), 3)]
    full = finish(pos, "finish_sides", [(b, True, k) for b, k in sides], full)
    opposite = hold(opposite, [full["up"]])
    full = finish(pos, "finish_sides", [([to_core(half) for half in b], False, k) for b, k in sides], full)
    others = [to_core(b) for b in opposite]
    full = finish(pos, "finish_last", [(opposite, True, 2)], full)
    full = finish(pos, "finish_last", [(others, False, 2)], full)

    def vector(i):
        return g[str(i)]

    return (
        y,
        dh,
        full["q"],
        vector(BQ),
        full["k"],
        full["v"],
        vector(BV),
        full["o"],
        vector(BO),
        vector(G1),
        vector(S1),
        full["up"],
        vector(C1),
        full["down"],
        vector(C2),
        vector(G2),
        vector(S2),
    )


def solution(mesh):
    row, matrix, vector = P("dp", None, None), P("section", None, None), P("section", None)
    in_specs = (row, P("dp", None), row, matrix, vector, matrix, matrix, vector, matrix, vector, vector, vector, matrix, vector, matrix, vector, vector, vector)
    big = P("section", "dp", None, None)
    out_specs = (big, big, matrix, vector, matrix, matrix, vector, matrix, vector, vector, vector, matrix, vector, matrix, vector, vector, vector)
    return jax.shard_map(shards, mesh=mesh, in_specs=in_specs, out_specs=out_specs, check_vma=False)
```

```python
import functools

import jax
import jax.numpy as jnp
from jax import lax
from jax.experimental import pallas as pl
from jax.experimental.pallas import tpu as pltpu
from jax.sharding import PartitionSpec as P

BF, F32 = jnp.bfloat16, jnp.float32
ROWS, L, D, FF, HEADS, HEAD = 2, 256, 512, 2048, 8, 64
BLK = 512
NBLK = FF // BLK
NARROW = 256
GELU = 0.7978845608028654
VEC = 16
MiB = 1 << 20
SCALE = HEAD ** (-0.5)
BQ, BV, BO, G1, S1, C2, G2, S2, C1 = 0, 1, 2, 3, 4, 5, 6, 7, 8
SEC, CORE, FIRST, SECOND = 0, 1, 2, 3


def nn(a, b):
    return jnp.dot(a, b, preferred_element_type=F32)


def nt(a, b):
    return lax.dot_general(a, b, (((1,), (1,)), ((), ())), preferred_element_type=F32)


def tn(a, b):
    return lax.dot_general(a, b, (((0,), (0,)), ((), ())), preferred_element_type=F32)


def kernel(name, body, reads, updates, news, scratch=None, sems=0, outside=(), free=(), vmem=12, flops=1000, nbytes=1000):
    scratch = scratch or {}
    outs = {**updates, **news}
    names = list(reads) + list(updates)

    def spec(n):
        if n == "in_pos":
            return pl.BlockSpec(memory_space=pl.ANY)
        if n in outside:
            return pl.BlockSpec(memory_space=pltpu.HBM)
        if n == "pos":
            return pl.BlockSpec(memory_space=pltpu.SMEM)
        return pl.BlockSpec(memory_space=pltpu.VMEM)

    def shape(n):
        if n == "pos":
            return pltpu.SMEM(*news[n])
        space = pltpu.HBM if n in outside else jax.ShapeDtypeStruct if n in free else pltpu.VMEM
        return space(*news[n]) if n in news else space(updates[n].shape, updates[n].dtype)

    reads = {n: pltpu.with_memory_space_constraint(v, pltpu.HBM) if n in outside and n != "in_pos" else v for n, v in reads.items()}

    def whole(*refs):
        s = dict(zip(reads, refs))
        rest = refs[len(names) :]
        s.update(zip(outs, rest))
        s.update(zip(list(scratch) + ["sems"], rest[len(outs) :]))
        body(s)

    got = pl.pallas_call(
        whole,
        out_shape=[shape(n) for n in outs],
        in_specs=[spec(n) for n in names],
        out_specs=[spec(n) for n in outs],
        scratch_shapes=[pltpu.VMEM(*v) for v in scratch.values()] + ([pltpu.SemaphoreType.DMA((sems,))] if sems else []),
        input_output_aliases={len(reads) + i: i for i in range(len(updates))},
        compiler_params=pltpu.CompilerParams(vmem_limit_bytes=vmem * MiB),
        cost_estimate=pl.CostEstimate(flops=flops, bytes_accessed=nbytes, transcendentals=0),
        name=name,
    )(*reads.values(), *updates.values())
    return dict(zip(outs, got))


def norm_forward(resid, gain, shift):
    centre = resid - jnp.mean(resid, -1, keepdims=True)
    rstd = lax.rsqrt(jnp.mean(centre * centre, -1, keepdims=True) + 1e-05)
    unit = centre * rstd
    return unit, rstd, unit * gain + shift


def norm_backward(grad, unit, rstd, gain):
    scaled = grad * gain
    inner = scaled - jnp.mean(scaled, -1, keepdims=True)
    return rstd * (inner - unit * jnp.mean(scaled * unit, -1, keepdims=True))


def pair_lanes(pair):
    return slice(pair * 2 * HEAD, (pair + 1) * 2 * HEAD)


def lane_masks():
    lane = lax.broadcasted_iota(jnp.int32, (L, 128), 1)
    low = (lane < HEAD).astype(F32)
    return low.astype(BF), (1.0 - low).astype(BF), lane < HEAD


ROW = dict(
    h=((L, D), BF),
    y=((L, D), BF),
    o=((L, D), BF),
    u=((L, D), BF),
    a=((L, FF), BF),
    q=((L, D), BF),
    k=((L, D), BF),
    v=((L, D), BF),
    p=((HEADS * L, L), BF),
    gp=((L, FF), BF),
    x1=((L, D), F32),
    x2=((L, D), F32),
    rs=((L, 256), F32),
    e2=((L, D), BF),
    e1=((L, FF), BF),
    e0=((L, D), BF),
    dq=((L, D), BF),
    dk=((L, D), BF),
    dv=((L, D), BF),
    ln=((8, D), F32),
    dh=((L, D), F32),
)
FORWARD = ("h", "y", "o", "u", "a", "q", "k", "v", "p", "gp", "x1", "x2", "rs")
BACKWARD = ("e2", "e1", "e0", "dq", "dk", "dv", "ln", "dh")
WEIGHTS = dict(wq=((D, D), BF), wk=((D, D), BF), wv=((D, D), BF), wo=((D, D), BF), w1=((D, FF), BF), w2=((FF, D), BF))


LATE = dict(z=((L, FF), F32), half=((L, FF), F32))


def both_rows(names):
    return {n: ((ROWS,) + ROW[n][0], ROW[n][1]) for n in names}


def of_row(s, row, names):
    return {**s, **{n: s[n].at[row] for n in names}}


def gelu_slope(z, half):
    return half + (z * half * (2.0 - 2.0 * half)) * (GELU + (0.134145 * GELU) * (z * z))


def forward(s, need, row, late):
    need("wq")
    hidden = s["h"][...]

    def vec(i):
        return s["vec"][i : i + 1, :]

    s["q"][...] = (nn(hidden, s["wq"][...]) + vec(BQ)).astype(BF)
    need("wk")
    s["k"][...] = nn(hidden, s["wk"][...]).astype(BF)
    need("wv")
    s["v"][...] = (nn(hidden, s["wv"][...]) + vec(BV)).astype(BF)
    seg = jnp.broadcast_to(s["seg"][row : row + 1, :].astype(F32), (L, L))
    same = seg == seg.T
    low, high, is_low = lane_masks()
    for head in range(HEADS):
        cols, rows = pair_lanes(head // 2), slice(head * L, head * L + L)
        scores = nt(s["q"][:, cols] * ((high if head % 2 else low) * SCALE), s["k"][:, cols])
        scores = jnp.where(same, scores, -1000000000.0)
        weight = jnp.exp(scores - jnp.max(scores, -1, keepdims=True))
        s["p"][rows, :] = (weight * (1.0 / jnp.sum(weight, -1, keepdims=True))).astype(BF)
    for pair in range(HEADS // 2):
        cols = pair_lanes(pair)
        both = nn(s["p"][pair * 2 * L : (pair + 1) * 2 * L, :], s["v"][:, cols])
        s["o"][:, cols] = jnp.where(is_low, both[:L], both[L:]).astype(BF)
    need("wo")
    resid = hidden.astype(F32) + nn(s["o"][...], s["wo"][...]) + vec(BO)
    unit, rstd, normed = norm_forward(resid, vec(G1), vec(S1))
    s["x1"][...] = unit
    s["rs"][:, :128] = jnp.broadcast_to(rstd, (L, 128))
    s["u"][...] = normed.astype(BF)
    need("w1")
    need("w2")
    total = normed + vec(C2)
    for j in range(FF // NARROW):
        cols = slice(j * NARROW, (j + 1) * NARROW)
        at = j * NARROW % BLK
        z = nn(s["u"][...], s["w1"][:, cols]) + vec(C1 + j * NARROW // BLK)[:, at : at + NARROW]
        square = z * z
        half = 0.5 + 0.5 * jnp.tanh(z * (GELU + (0.044715 * GELU) * square))
        if late:
            s["z"][:, cols] = z
            s["half"][:, cols] = half
        else:
            s["gp"][:, cols] = gelu_slope(z, half).astype(BF)
        active = (z * half).astype(BF)
        s["a"][:, cols] = active
        total = total + nn(active, s["w2"][cols, :])
    unit, rstd, out = norm_forward(total, vec(G2), vec(S2))
    s["y"][...] = out.astype(BF)
    s["x2"][...] = unit
    s["rs"][:, 128:] = jnp.broadcast_to(rstd, (L, 128))


BACK = dict(do=((L, D), BF), dsc=((HEADS * L, L), BF))


def backward_feed(s, late):
    gain1, gain2 = s["vec"][G1 : G1 + 1, :], s["vec"][G2 : G2 + 1, :]
    dout = s["dy"][...].astype(F32)
    unit = s["x2"][...]
    g_gain2 = jnp.sum(dout * unit, 0, keepdims=True)
    g_shift2 = jnp.sum(dout, 0, keepdims=True)
    dsecond = norm_backward(dout, unit, s["rs"][:, 128:129], gain2)
    s["e2"][...] = dsecond.astype(BF)
    for j in range(NBLK):
        cols = slice(j * BLK, j * BLK + BLK)
        dactive = nt(s["e2"][...], s["w2"][cols, :])
        slope = gelu_slope(s["z"][:, cols], s["half"][:, cols]) if late else s["gp"][:, cols].astype(F32)
        s["e1"][:, cols] = (slope * dactive).astype(BF)
    total = dsecond + nt(s["e1"][...], s["w1"][...])
    unit = s["x1"][...]
    g_gain1 = jnp.sum(total * unit, 0, keepdims=True)
    g_shift1 = jnp.sum(total, 0, keepdims=True)
    dresid = norm_backward(total, unit, s["rs"][:, 0:1], gain1)
    s["r1"][...] = dresid
    s["e0"][...] = dresid.astype(BF)
    s["ln"][...] = jnp.concatenate([g_gain2, g_shift2, g_gain1, g_shift1, jnp.zeros((4, D), F32)], 0)


def backward_attention(s):
    s["do"][...] = nt(s["e0"][...], s["wo"][...]).astype(BF)
    low, high, is_low = lane_masks()
    for pair in range(HEADS // 2):
        cols, rows = pair_lanes(pair), slice(pair * 2 * L, (pair + 1) * 2 * L)
        grad = s["do"][:, cols]
        dprobs = nt(jnp.concatenate([grad * low, grad * high], 0), s["v"][:, cols])
        probs = s["p"][rows, :].astype(F32)
        product = probs * dprobs
        s["dsc"][rows, :] = (product - probs * jnp.sum(product, -1, keepdims=True)).astype(BF)
    for pair in range(HEADS // 2):
        cols, rows = pair_lanes(pair), slice(pair * 2 * L, (pair + 1) * 2 * L)
        one, two = (slice((2 * pair + i) * L, (2 * pair + i + 1) * L) for i in range(2))
        both = nn(s["dsc"][rows, :], s["k"][:, cols])
        s["dq"][:, cols] = (jnp.where(is_low, both[:L], both[L:]) * SCALE).astype(BF)
        query, grad = s["q"][:, cols], s["do"][:, cols]
        s["dk"][:, cols] = (jnp.where(is_low, tn(s["dsc"][one, :], query), tn(s["dsc"][two, :], query)) * SCALE).astype(BF)
        s["dv"][:, cols] = jnp.where(is_low, tn(s["p"][one, :], grad), tn(s["p"][two, :], grad)).astype(BF)
    grad = s["r1"][...] + nt(s["dq"][...], s["wq"][...])
    grad = grad + nt(s["dk"][...], s["wk"][...]) + nt(s["dv"][...], s["wv"][...])
    s["ds"][...] = grad.astype(BF)
    s["dh"][...] = grad


VECTORS = (BQ, BV, BO, G1, S1, C2, G2, S2)


LOADED = {**WEIGHTS, "vec": ((VEC, D), F32), "seg": ((ROWS, L), jnp.int32), "cot": ((ROWS, L, D), BF)}


def first_forward(row, outside, state, here):
    if row == 0:
        reads, updates = {**outside, "here": here}, {}
        news = {**LOADED, **LATE, "pos": ((4,), jnp.int32), **both_rows(FORWARD)}
    else:
        reads = {**outside, "pos": state["pos"]}
        updates = {n: state[n] for n in (*LOADED, *FORWARD)}
        news = {}
    news["sent"] = ROW["y"]

    def body(s):
        copies, waiting = {}, []

        def start(n, source, target):
            copies[n] = pltpu.make_async_copy(source, target, s["sems"].at[len(copies)])
            copies[n].start()
            waiting.append(n)

        def rest():
            for m in ("wo", "w1", "w2"):
                start(m, s["in_" + m].at[0], s[m])
            start("cot", s["in_cot"], s["cot"])

        def need(n):
            if n in waiting:
                waiting.remove(n)
                copies[n].wait()
            if n == "wq" and row == 0:
                rest()

        def load():
            start("h", s["in_h"], s["h"])
            start("wq", s["in_wq"].at[0], s["wq"])
            for i in VECTORS:
                start(i, s[f"in_{i}"], s["vec"].at[pl.ds(i, 1), :])
            for n in ("wk", "wv"):
                start(n, s["in_" + n].at[0], s[n])
            start("seg", s["in_seg"], s["seg"])
            for j in range(NBLK):
                start(C1 + j, s[f"in_{C1}"].at[:, pl.ds(j * BLK, BLK)], s["vec"].at[pl.ds(C1 + j, 1), :])

        if row == 0:
            place = pltpu.make_async_copy(s["in_pos"], s["pos"], s["sems"].at[SEMS - 1])
            place.start()

        @pl.when((s["here"][0, 0] if row == 0 else s["pos"][SEC]) == 0)
        def _():
            if row == 0:
                load()
                for n in ("h", "seg", *VECTORS, *range(C1, C1 + NBLK)):
                    need(n)
            r = of_row(s, row, FORWARD)
            forward(r, need, row, row == 0)
            s["sent"][...] = r["y"][...]
            need("cot")

        if row == 0:
            place.wait()
        else:
            copies.clear()

            @pl.when(s["pos"][SEC] == 1)
            def _():
                load()
                rest()
                for n in list(waiting):
                    need(n)

    got = kernel(f"first_forward_{row}", body, reads, updates, news, sems=SEMS, outside=list(outside), flops=3 * 10**9, nbytes=8 * 10**6)
    return got.pop("sent"), {**state, **got}


SEMS = 32


def first_slopes(state):
    def body(s):
        @pl.when(s["pos"][SEC] == 0)
        def _():
            for j in range(FF // 128):
                cols = slice(j * 128, j * 128 + 128)
                s["gp"][0, :, cols] = gelu_slope(s["z"][:, cols], s["half"][:, cols]).astype(BF)

    return {**state, **kernel("first_slopes", body, {n: state[n] for n in ("pos", *LATE)}, {"gp": state["gp"]}, {})}


def second_both(row, arrived, state):
    reads = {n: state[n] for n in ("vec", "seg", "pos", "cot", *WEIGHTS)}
    reads["arrived"] = arrived
    updates = {n: state[n] for n in (*FORWARD, *LATE)}
    news = {"ds": ROW["y"]}
    if row == 0:
        news.update(both_rows(BACKWARD))
    else:
        updates.update({n: state[n] for n in BACKWARD})

    def body(s):
        r = of_row(s, row, FORWARD + BACKWARD)
        r["dy"] = s["cot"].at[row]

        @pl.when(s["pos"][SEC] == 1)
        def _():
            r["h"][...] = s["arrived"][...]
            forward(r, lambda n: None, row, True)
            backward_feed(r, True)
            backward_attention(r)

    got = kernel(f"second_both_{row}", body, reads, updates, news, {**BACK, "r1": ROW["dh"]}, flops=6 * 10**9, nbytes=8 * 10**6)
    return got.pop("ds"), {**state, **got}


def first_feed(row, arrived, state, after):
    reads = {n: state[n] for n in ("vec", "pos", "w1", "w2", "x1", "x2", "rs", "gp")}
    reads.update(dy=arrived, **after)
    keep = ("e2", "e1", "e0", "ln")

    def body(s):
        @pl.when(s["pos"][SEC] == 0)
        def _():
            backward_feed(of_row(s, row, ("x1", "x2", "rs", "gp", *keep)), False)

    got = kernel(f"first_feed_{row}", body, reads, {n: state[n] for n in keep}, {"r1": ROW["dh"]}, flops=10**9, nbytes=8 * 10**6)
    return got.pop("r1"), {**state, **got}


def first_attention(row, dresid, state):
    reads = {n: state[n] for n in ("pos", "wq", "wk", "wv", "wo", "e0", "q", "k", "v", "p")}
    reads["r1"] = dresid
    keep = ("dq", "dk", "dv", "dh")

    def body(s):
        @pl.when(s["pos"][SEC] == 0)
        def _():
            backward_attention(of_row(s, row, ("e0", "q", "k", "v", "p", *keep)))

    got = kernel(f"first_attention_{row}", body, reads, {n: state[n] for n in keep}, {}, {**BACK, "ds": ROW["y"]}, flops=2 * 10**9, nbytes=8 * 10**6)
    return {**state, **got}


T2 = ROWS * L
AQ = D // 2


def aligned(index, size):
    return pl.multiple_of(index * size, size)


def per_core(s, work):
    for core in range(2):
        pl.when(s["pos"][CORE] == core)(functools.partial(work, core))


def feed_block(s, up, j, rows):
    cols = pl.ds(aligned(j, BLK), BLK)
    if up:
        return tn(s["u"][rows, :], s["e1"][rows, cols])
    return tn(s["a"][rows, cols], s["e2"][rows, :])


def attention_block(s, out, i, rows):
    left, right = (("o", "e0"), ("h", "dq"))[i] if out else ("h", ("dk", "dv")[i])
    return tn(s[left][rows, :], s[right][rows, :])


def vector_rows(s, row, rows):
    ones = jnp.ones((8, L), BF)

    def total(value):
        return nn(ones, value)[0:1, :]

    ln = s["ln"][row]
    got = [total(s[n][rows, :]) for n in ("dq", "dv", "e0")] + [ln[2:3], ln[3:4], total(s["e2"][rows, :]), ln[0:1], ln[1:2]]
    got += [total(s["e1"][rows, j * BLK : j * BLK + BLK]) for j in range(NBLK)]
    return jnp.concatenate(got + [jnp.zeros((VEC - len(got), D), F32)], 0)


FIRST_ROW, LAST_ROW = slice(0, L), slice(L, 2 * L)


def first_products(pos, ops):
    def body(s):
        def work(core):
            for j in range(NBLK):
                rows = slice(j * BLK, j * BLK + BLK)
                s["fs"][rows, :] = feed_block(s, core == 0, j, FIRST_ROW).astype(BF)
                s["fk"][rows, :] = feed_block(s, core == 1, j, FIRST_ROW).astype(BF)
            for i in range(2):
                rows = slice(i * D, i * D + D)
                s["ts"][rows, :] = attention_block(s, core == 1, i, FIRST_ROW).astype(BF)
                s["tk"][rows, :] = attention_block(s, core == 0, i, FIRST_ROW).astype(BF)

        per_core(s, work)
        s["vec"][...] = vector_rows(s, 0, FIRST_ROW)

    news = {"fs": ((FF, D), BF), "fk": ((FF, D), BF), "ts": ((2 * D, D), BF), "tk": ((2 * D, D), BF), "vec": ((VEC, D), F32)}
    return kernel("first_products", body, {"pos": pos, **ops}, {}, news)


def feed_send(pos, ops, early, distances, after):
    def body(s):
        def work(core):
            for i, k in enumerate(distances):
                j = lax.rem(s["pos"][SECOND] + k, 4)
                more = s["early"][pl.ds(aligned(j, BLK), BLK), :].astype(F32)
                s["out"][i * BLK : i * BLK + BLK, :] = (feed_block(s, core == 0, j, LAST_ROW) + more).astype(BF)

        per_core(s, work)

    return kernel("feed_send", body, {"pos": pos, **ops, "early": early, **after}, {}, {"out": ((len(distances) * BLK, D), BF)})["out"]


def attention_send(pos, ops, early, early_vec, after):
    def body(s):
        def work(core):
            for i in range(2):
                rows = slice(i * D, i * D + D)
                s["out"][rows, :] = (attention_block(s, core == 1, i, LAST_ROW) + s["early"][rows, :].astype(F32)).astype(BF)

        per_core(s, work)
        s["vec"][...] = (s["early_vec"][...] + vector_rows(s, 1, LAST_ROW)).astype(BF)
        s["out"][2 * D :, :] = s["vec"][...]

    news = {"out": ((2 * D + VEC, D), BF), "vec": ((VEC, D), BF)}
    got = kernel("attention_send", body, {"pos": pos, **ops, "early": early, "early_vec": early_vec, **after}, {}, news)
    return got["out"], got["vec"]


def feed_keep(pos, ops, early, distances, got, after):
    def body(s):
        def work(core):
            for i, k in enumerate(distances):
                j = lax.rem(s["pos"][FIRST] + k, 4)
                more = s["got"][i * BLK : i * BLK + BLK, :].astype(F32) + s["early"][pl.ds(aligned(j, BLK), BLK), :].astype(F32)
                s[f"p{k}"][...] = (feed_block(s, core == 1, j, LAST_ROW) + more).astype(BF)

        per_core(s, work)

    news = {f"p{k}": ((BLK, D), BF) for k in distances}
    return kernel("feed_keep", body, {"pos": pos, **ops, "early": early, "got": got, **after}, {}, news)


def attention_keep(pos, ops, early, vec, got):
    def body(s):
        def work(core):
            for i in range(2):
                rows = slice(i * D, i * D + D)
                more = s["got"][rows, :].astype(F32) + s["early"][rows, :].astype(F32)
                s["acc"][rows, :] = (attention_block(s, core == 0, i, LAST_ROW) + more).astype(BF)

        per_core(s, work)
        shared = (s["vec"][...].astype(F32) + s["got"][2 * D :, :].astype(F32)).astype(BF)
        for k in range(4):
            j = lax.rem(s["pos"][FIRST] + k, 4)
            s[f"p{k}"][:AQ, :] = s["acc"][pl.ds(aligned(j, AQ), AQ), :]
            s[f"p{k}"][AQ:, :] = shared

    news = {f"p{k}": ((AQ + VEC, D), BF) for k in range(4)}
    reads = {"pos": pos, **ops, "early": early, "vec": vec, "got": got}
    return list(kernel("attention_keep", body, reads, {}, news, {"acc": ((2 * D, D), BF)}).values())


def total_of(s, tag):
    wide = [s[f"{tag}{k}"][...].astype(F32) for k in range(4)]
    return ((wide[0] + wide[2]) + (wide[1] + wide[3])).astype(BF)


def by_distance(tag, values):
    return {f"{tag}{k}": v for k, v in enumerate(values)}


FQ, TQ = BLK // 4, AQ // 4
SHARD = FQ + TQ


def sum_split(pos, feed, atts):
    def body(s):
        s["att"][...] = total_of(s, "t")
        for k in range(4):
            j = lax.rem(s["pos"][SECOND] + k, 4)
            s[f"p{k}"][:FQ, :] = s["feed"][pl.ds(aligned(j, FQ), FQ), :]
            s[f"p{k}"][FQ:SHARD, :] = s["att"][pl.ds(aligned(j, TQ), TQ), :]
            s[f"p{k}"][SHARD:, :] = s["att"][AQ:, :]

    reads = {"pos": pos, "feed": feed, **by_distance("t", atts)}
    news = {f"p{k}": ((SHARD + VEC, D), BF) for k in range(4)}
    scratch = {"att": ((AQ + VEC, D), BF)}
    return list(kernel("sum_split", body, reads, {}, news, scratch).values())


def sum_four(got):
    def body(s):
        s["out"][...] = total_of(s, "g")

    return kernel("sum_four", body, by_distance("g", got), {}, {"out": (got[0].shape, BF)})["out"]


def sum_two(own, got):
    def body(s):
        total = (s["a"][...].astype(F32) + s["b"][...].astype(F32)).astype(BF)
        s["out"][...] = total[:SHARD]
        s["vec"][...] = total[SHARD:]

    got = kernel("sum_two", body, {"a": own, "b": got}, {}, {"out": ((SHARD, D), BF), "vec": ((VEC, D), BF)})
    return got["out"], got["vec"]


HALF = (BLK + AQ) // 2


def join(pos, got, vec):
    def body(s):
        for k in range(4):
            j = lax.rem(s["pos"][SECOND] + (4 - k), 4)
            s["out"][pl.ds(aligned(j, FQ), FQ), :] = s[f"g{k}"][:FQ, :]
            s["out"][pl.ds(aligned(j, TQ) + BLK, TQ), :] = s[f"g{k}"][FQ:, :]
        s["out"][2 * HALF :, :] = s["vec"][...]
        s["up"][...] = s["out"][:HALF, :]
        s["low"][...] = s["out"][HALF : 2 * HALF, :]

    news = {"out": ((2 * HALF + VEC, D), BF), "up": ((HALF, D), BF), "low": ((HALF, D), BF)}
    return kernel("join", body, {"pos": pos, **by_distance("g", got), "vec": vec}, {}, news).values()


MATRICES = ("o", "q", "k", "v")


def pair(one, two):
    def body(s):
        s["out"][:HALF, :] = s["one"][...]
        s["out"][HALF:, :] = s["two"][...]

    return kernel("pair", body, {"one": one, "two": two}, {}, {"out": ((2 * HALF, D), BF)})["out"]


def finish(pos, name, halves, done):
    arrays = []
    for array, *_ in halves:
        arrays += [] if any(array is a for a in arrays) else [array]

    def named(array):
        return "b%d" % [array is a for a in arrays].index(True)

    def body(s):
        started = []

        def move(source, target, sem):
            pltpu.make_async_copy(source, target, s["sems"].at[sem]).start()

        for i, (array, row, mine, k, lower) in enumerate(halves):
            s["wide"][i] = s[named(array)][row : row + HALF, :].astype(F32)
            rest = BLK - HALF if lower else HALF
            feed = s["wide"].at[i, pl.ds(0, rest)]
            piece = lax.rem(s["pos"][FIRST if mine else SECOND] + (4 - k), 4)
            down = (s["pos"][CORE] == 0) if mine else (s["pos"][CORE] == 1)
            at, cols = pl.ds(pl.multiple_of(piece * BLK + lower * HALF, 128), rest), pl.ds(aligned(piece, BLK), BLK)
            pl.when(down)(functools.partial(move, feed, s["down"].at[0, at, :], 2 * i))
            pl.when(jnp.logical_not(down))(functools.partial(move, feed, s["up"].at[0, pl.ds(lower * HALF, rest), cols], 2 * i))
            started.append((feed, s["down"].at[0, pl.ds(0, rest), :], 2 * i))
            if lower:
                att = s["wide"].at[i, pl.ds(rest, AQ)]
                kind = jnp.where(down, 0, 2) + lax.div(piece, 2)
                at = pl.ds(aligned(lax.rem(piece, 2), AQ), AQ)
                for which, n in enumerate(MATRICES):
                    pl.when(kind == which)(functools.partial(move, att, s[n].at[0, at, :], 2 * i + 1))
                started.append((att, s["o"].at[0, pl.ds(0, AQ), :], 2 * i + 1))
        for source, target, sem in started:
            pltpu.make_async_copy(source, target, s["sems"].at[sem]).wait()

    reads = {"pos": pos, **{named(v): v for v in arrays}}
    news = {} if done else {"up": ((1, D, FF), F32), "down": ((1, FF, D), F32), **{n: ((1, D, D), F32) for n in MATRICES}}
    scratch = {"wide": ((len(halves), HALF, D), F32)}
    return kernel(name, body, reads, done, news, scratch, sems=2 * len(halves), outside=("up", "down", *MATRICES))


def hold(values, stored=(), near=()):
    updates = {f"x{i}": v for i, v in enumerate(values)}
    outside = {f"a{i}": v for i, v in enumerate(stored)}
    reads = {**outside, **{f"b{i}": v for i, v in enumerate(near)}}
    return list(kernel("hold", lambda s: None, reads, updates, {}, outside=outside).values())


def store(y, dh):
    def body(s):
        moves = [pltpu.make_async_copy(s[n], s["out_" + n].at[0], s["sems"].at[i]) for i, n in enumerate(("y", "dh"))]
        for move in moves:
            move.start()
        for move in moves:
            move.wait()

    news = {"out_y": ((1, *y.shape), BF), "out_dh": ((1, *dh.shape), F32)}
    got = kernel("store", body, {"y": y, "dh": dh}, {}, news, sems=2, outside=news)
    return got["out_y"], got["out_dh"]


def vector_finish(pos, mine, other):
    def body(s):
        own = (s["pos"][CORE] == 0).astype(F32)
        values = jnp.where(own > 0.5, s["mine"][2 * HALF :, :].astype(F32), s["other"][2 * HALF :, :].astype(F32))
        for i in VECTORS:
            s[str(i)][...] = values[i : i + 1, :]
        for j in range(NBLK):
            s[str(C1)][:, j * BLK : j * BLK + BLK] = values[C1 + j : C1 + j + 1, :]

    news = {**{str(i): ((1, D), F32) for i in VECTORS}, str(C1): ((1, FF), F32)}
    return kernel("vector_finish", body, {"pos": pos, "mine": mine, "other": other}, {}, news, free=news)


def spot(y, z, x, core):
    return ((y * 2 + z) * 4 + x) * 2 + core


def everywhere(move):
    return [(spot(y, z, x, c), spot(*move(y, z, x, c))) for y in range(4) for z in range(2) for x in range(4) for c in range(2)]


def along(stage, distance):
    def move(y, z, x, core):
        if (core == 0) == (stage == 0):
            return y, z, (x + distance) % 4, core
        return (y + distance) % 4, z, x, core

    return everywhere(move)


def send(value, route):
    return lax.ppermute(value, "dp", route)


def to_core(value):
    return send(value, everywhere(lambda y, z, x, core: (y, z, x, 1 - core)))


def to_z(value):
    return send(value, everywhere(lambda y, z, x, core: (y, 1 - z, x, core)))


def spread(pieces, stage):
    sent = {k: send(pieces[k], along(stage, k)) for k in (1, 3, 2)}
    return [pieces[0]] + [sent[k] for k in (1, 2, 3)]


def shards(tokens, segments, cotangent, w_query, q_bias, w_key, w_value, v_bias, w_out, out_bias, ln1_gain, ln1_shift, w_up, up_bias, w_down, down_bias, ln2_gain, ln2_shift):
    dp = lax.axis_index("dp")
    core, x, y = dp % 2, (dp // 2) % 4, dp // 16
    first, second = jnp.where(core == 0, x, y), jnp.where(core == 0, y, x)
    here = jnp.stack([lax.axis_index("section"), core, first, second]).astype(jnp.int32)
    outside = {"in_pos": here, "in_h": tokens, "in_seg": segments, "in_cot": cotangent}
    outside.update(in_wq=w_query, in_wk=w_key, in_wv=w_value, in_wo=w_out, in_w1=w_up, in_w2=w_down)
    vectors = {BQ: q_bias, BV: v_bias, BO: out_bias, G1: ln1_gain, S1: ln1_shift, C2: down_bias, G2: ln2_gain, S2: ln2_shift, C1: up_bias}
    outside.update({f"in_{i}": v for i, v in vectors.items()})

    def forth(value):
        return lax.ppermute(value, "section", [(0, 1)])

    def back(value):
        return lax.ppermute(value, "section", [(1, 0)])

    state = {}
    came, dcame = [], []
    for row in range(ROWS):
        sent, state = first_forward(row, outside, state, jnp.broadcast_to(here[:1], (8, 128)))
        came.append(forth(sent))
    state = first_slopes(state)
    for row in range(ROWS):
        sent, state = second_both(row, came[row], state)
        dcame.append(back(sent))
    pos = state["pos"]

    def flat(*names):
        return {n: state[n].reshape((T2, state[n].shape[-1])) for n in names}

    dresid, state = first_feed(0, dcame[0], state, {})
    state = first_attention(0, dresid, state)
    names = ("u", "a", "o", "h", "e1", "e2", "e0", "dq", "dk", "dv")
    early = first_products(pos, {**flat(*names), "ln": state["ln"]})
    dresid, state = first_feed(1, dcame[1], state, {"after": early["vec"]})
    near, far = (1, 3), (2, 0)
    feed_ops = flat("u", "a", "e1", "e2")
    near_out = feed_send(pos, feed_ops, early["fs"], near, {})
    far_out = feed_send(pos, feed_ops, early["fs"], far, {"after": near_out})
    state = first_attention(1, dresid, state)
    feeds = feed_keep(pos, feed_ops, early["fk"], near, to_core(near_out), {})
    ops = flat(*names)
    att_out, vec = attention_send(pos, {**ops, "ln": state["ln"]}, early["ts"], early["vec"], {"after": feeds["p3"]})
    atts = attention_keep(pos, flat("o", "h", "e0", "dq", "dk", "dv"), early["tk"], vec, to_core(att_out))
    feeds.update(feed_keep(pos, feed_ops, early["fk"], far, to_core(far_out), {"after": atts[0]}))
    pieces = sum_split(pos, sum_four(spread([feeds[f"p{k}"] for k in range(4)], 0)), spread(atts, 0))
    mine = sum_four(spread(pieces, 1))
    shard, vec = sum_two(mine, to_z(mine))
    block, up, low = join(pos, spread([shard] * 4, 1), vec)
    up_behind, low_ahead = send(up, along(0, 1)), send(low, along(0, 3))
    low_behind, up_ahead = send(low, along(0, 1)), send(up, along(0, 3))
    other = to_core(block)
    y, dh = store(state["y"], state["dh"])
    g = vector_finish(pos, block, other)
    own = [(v, h * HALF, mine, 0, h) for v, mine in ((block, True), (other, False)) for h in range(2)]
    full = finish(pos, "finish_own", own, {})
    up_behind, low_ahead = hold([up_behind, low_ahead], [y, dh, g[str(BQ)], full["up"]])
    opposite = [send(up_behind, along(0, 1)), send(low_ahead, along(0, 3))]
    first = pair(up_behind, low_ahead)
    low_behind, up_ahead = hold([low_behind, up_ahead], near=[up_behind, low_ahead])
    sides = [(up_behind, 0, True, 1, 0), (low_behind, 0, True, 1, 1), (up_ahead, 0, True, 3, 0), (low_ahead, 0, True, 3, 1)]
    full = finish(pos, "finish_sides", sides, full)
    opposite = hold(opposite, [full["up"]])
    others = [to_core(b) for b in opposite]
    first = to_core(first)
    second = [(first, 0, False, 1, 0), (first, HALF, False, 3, 1), (to_core(low_behind), 0, False, 1, 1), (to_core(up_ahead), 0, False, 3, 0)]
    full = finish(pos, "finish_second", second + [(b, 0, True, 2, h) for h, b in enumerate(opposite)], full)
    full = finish(pos, "finish_last", [(b, 0, False, 2, h) for h, b in enumerate(others)], full)

    def vector(i):
        return g[str(i)]

    return (
        y,
        dh,
        full["q"],
        vector(BQ),
        full["k"],
        full["v"],
        vector(BV),
        full["o"],
        vector(BO),
        vector(G1),
        vector(S1),
        full["up"],
        vector(C1),
        full["down"],
        vector(C2),
        vector(G2),
        vector(S2),
    )


def solution(mesh):
    row, matrix, vector = P("dp", None, None), P("section", None, None), P("section", None)
    in_specs = (row, P("dp", None), row, matrix, vector, matrix, matrix, vector, matrix, vector, vector, vector, matrix, vector, matrix, vector, vector, vector)
    big = P("section", "dp", None, None)
    out_specs = (big, big, matrix, vector, matrix, matrix, vector, matrix, vector, vector, vector, matrix, vector, matrix, vector, vector, vector)
    return jax.shard_map(shards, mesh=mesh, in_specs=in_specs, out_specs=out_specs, check_vma=False)
```

```python
import functools

import jax
import jax.numpy as jnp
from jax import lax
from jax.experimental import pallas as pl
from jax.experimental.pallas import tpu as pltpu
from jax.sharding import PartitionSpec as P

BF, F32 = jnp.bfloat16, jnp.float32
ROWS, L, D, FF, HEADS, HEAD = 2, 256, 512, 2048, 8, 64
BLK = 512
NBLK = FF // BLK
NARROW = 256
GELU = 0.7978845608028654
VEC = 16
MiB = 1 << 20
SCALE = HEAD ** (-0.5)
BQ, BV, BO, G1, S1, C2, G2, S2, C1 = 0, 1, 2, 3, 4, 5, 6, 7, 8
SEC, CORE, FIRST, SECOND = 0, 1, 2, 3


def nn(a, b):
    return jnp.dot(a, b, preferred_element_type=F32)


def nt(a, b):
    return lax.dot_general(a, b, (((1,), (1,)), ((), ())), preferred_element_type=F32)


def tn(a, b):
    return lax.dot_general(a, b, (((0,), (0,)), ((), ())), preferred_element_type=F32)


def kernel(name, body, reads, updates, news, scratch=None, sems=0, outside=(), free=(), vmem=12, flops=1000, nbytes=1000):
    scratch = scratch or {}
    outs = {**updates, **news}
    names = list(reads) + list(updates)

    def spec(n):
        if n == "in_pos":
            return pl.BlockSpec(memory_space=pl.ANY)
        if n in outside:
            return pl.BlockSpec(memory_space=pltpu.HBM)
        if n == "pos":
            return pl.BlockSpec(memory_space=pltpu.SMEM)
        return pl.BlockSpec(memory_space=pltpu.VMEM)

    def shape(n):
        if n == "pos":
            return pltpu.SMEM(*news[n])
        space = pltpu.HBM if n in outside else jax.ShapeDtypeStruct if n in free else pltpu.VMEM
        return space(*news[n]) if n in news else space(updates[n].shape, updates[n].dtype)

    reads = {n: pltpu.with_memory_space_constraint(v, pltpu.HBM) if n in outside and n != "in_pos" else v for n, v in reads.items()}

    def whole(*refs):
        s = dict(zip(reads, refs))
        rest = refs[len(names) :]
        s.update(zip(outs, rest))
        s.update(zip(list(scratch) + ["sems"], rest[len(outs) :]))
        body(s)

    got = pl.pallas_call(
        whole,
        out_shape=[shape(n) for n in outs],
        in_specs=[spec(n) for n in names],
        out_specs=[spec(n) for n in outs],
        scratch_shapes=[pltpu.VMEM(*v) for v in scratch.values()] + ([pltpu.SemaphoreType.DMA((sems,))] if sems else []),
        input_output_aliases={len(reads) + i: i for i in range(len(updates))},
        compiler_params=pltpu.CompilerParams(vmem_limit_bytes=vmem * MiB),
        cost_estimate=pl.CostEstimate(flops=flops, bytes_accessed=nbytes, transcendentals=0),
        name=name,
    )(*reads.values(), *updates.values())
    return dict(zip(outs, got))


def norm_forward(resid, gain, shift):
    centre = resid - jnp.mean(resid, -1, keepdims=True)
    rstd = lax.rsqrt(jnp.mean(centre * centre, -1, keepdims=True) + 1e-05)
    unit = centre * rstd
    return unit, rstd, unit * gain + shift


def norm_backward(grad, unit, rstd, gain):
    scaled = grad * gain
    inner = scaled - jnp.mean(scaled, -1, keepdims=True)
    return rstd * (inner - unit * jnp.mean(scaled * unit, -1, keepdims=True))


def pair_lanes(pair):
    return slice(pair * 2 * HEAD, (pair + 1) * 2 * HEAD)


def lane_masks():
    lane = lax.broadcasted_iota(jnp.int32, (L, 128), 1)
    low = (lane < HEAD).astype(F32)
    return low.astype(BF), (1.0 - low).astype(BF), lane < HEAD


ROW = dict(
    h=((L, D), BF),
    y=((L, D), BF),
    o=((L, D), BF),
    u=((L, D), BF),
    a=((L, FF), BF),
    q=((L, D), BF),
    k=((L, D), BF),
    v=((L, D), BF),
    p=((HEADS * L, L), BF),
    gp=((L, FF), BF),
    x1=((L, D), F32),
    x2=((L, D), F32),
    rs=((L, 256), F32),
    e2=((L, D), BF),
    e1=((L, FF), BF),
    e0=((L, D), BF),
    dq=((L, D), BF),
    dk=((L, D), BF),
    dv=((L, D), BF),
    ln=((8, D), F32),
    dh=((L, D), F32),
)
FORWARD = ("h", "y", "o", "u", "a", "q", "k", "v", "p", "gp", "x1", "x2", "rs")
BACKWARD = ("e2", "e1", "e0", "dq", "dk", "dv", "ln", "dh")
WEIGHTS = dict(wq=((D, D), BF), wk=((D, D), BF), wv=((D, D), BF), wo=((D, D), BF), w1=((D, FF), BF), w2=((FF, D), BF))


LATE = dict(z=((L, FF), F32), half=((L, FF), F32))


def both_rows(names):
    return {n: ((ROWS,) + ROW[n][0], ROW[n][1]) for n in names}


def of_row(s, row, names):
    return {**s, **{n: s[n].at[row] for n in names}}


def gelu_slope(z, half):
    return half + (z * half * (2.0 - 2.0 * half)) * (GELU + (0.134145 * GELU) * (z * z))


def forward(s, need, row, late):
    need("wq")
    hidden = s["h"][...]

    def vec(i):
        return s["vec"][i : i + 1, :]

    s["q"][...] = (nn(hidden, s["wq"][...]) + vec(BQ)).astype(BF)
    need("wk")
    s["k"][...] = nn(hidden, s["wk"][...]).astype(BF)
    need("wv")
    s["v"][...] = (nn(hidden, s["wv"][...]) + vec(BV)).astype(BF)
    seg = jnp.broadcast_to(s["seg"][row : row + 1, :].astype(F32), (L, L))
    same = seg == seg.T
    low, high, is_low = lane_masks()
    for head in range(HEADS):
        cols, rows = pair_lanes(head // 2), slice(head * L, head * L + L)
        scores = nt(s["q"][:, cols] * ((high if head % 2 else low) * SCALE), s["k"][:, cols])
        scores = jnp.where(same, scores, -1000000000.0)
        weight = jnp.exp(scores - jnp.max(scores, -1, keepdims=True))
        s["p"][rows, :] = (weight * (1.0 / jnp.sum(weight, -1, keepdims=True))).astype(BF)
    for pair in range(HEADS // 2):
        cols = pair_lanes(pair)
        both = nn(s["p"][pair * 2 * L : (pair + 1) * 2 * L, :], s["v"][:, cols])
        s["o"][:, cols] = jnp.where(is_low, both[:L], both[L:]).astype(BF)
    need("wo")
    resid = hidden.astype(F32) + nn(s["o"][...], s["wo"][...]) + vec(BO)
    unit, rstd, normed = norm_forward(resid, vec(G1), vec(S1))
    s["x1"][...] = unit
    s["rs"][:, :128] = jnp.broadcast_to(rstd, (L, 128))
    s["u"][...] = normed.astype(BF)
    need("w1")
    need("w2")
    total = normed + vec(C2)
    for j in range(FF // NARROW):
        cols = slice(j * NARROW, (j + 1) * NARROW)
        at = j * NARROW % BLK
        z = nn(s["u"][...], s["w1"][:, cols]) + vec(C1 + j * NARROW // BLK)[:, at : at + NARROW]
        square = z * z
        half = 0.5 + 0.5 * jnp.tanh(z * (GELU + (0.044715 * GELU) * square))
        if late:
            s["z"][:, cols] = z
            s["half"][:, cols] = half
        else:
            s["gp"][:, cols] = gelu_slope(z, half).astype(BF)
        active = (z * half).astype(BF)
        s["a"][:, cols] = active
        total = total + nn(active, s["w2"][cols, :])
    unit, rstd, out = norm_forward(total, vec(G2), vec(S2))
    s["y"][...] = out.astype(BF)
    s["x2"][...] = unit
    s["rs"][:, 128:] = jnp.broadcast_to(rstd, (L, 128))


BACK = dict(do=((L, D), BF), dsc=((HEADS * L, L), BF))


def backward_feed(s, late):
    gain1, gain2 = s["vec"][G1 : G1 + 1, :], s["vec"][G2 : G2 + 1, :]
    dout = s["dy"][...].astype(F32)
    unit = s["x2"][...]
    g_gain2 = jnp.sum(dout * unit, 0, keepdims=True)
    g_shift2 = jnp.sum(dout, 0, keepdims=True)
    dsecond = norm_backward(dout, unit, s["rs"][:, 128:129], gain2)
    s["e2"][...] = dsecond.astype(BF)
    for j in range(NBLK):
        cols = slice(j * BLK, j * BLK + BLK)
        dactive = nt(s["e2"][...], s["w2"][cols, :])
        slope = gelu_slope(s["z"][:, cols], s["half"][:, cols]) if late else s["gp"][:, cols].astype(F32)
        s["e1"][:, cols] = (slope * dactive).astype(BF)
    total = dsecond + nt(s["e1"][...], s["w1"][...])
    unit = s["x1"][...]
    g_gain1 = jnp.sum(total * unit, 0, keepdims=True)
    g_shift1 = jnp.sum(total, 0, keepdims=True)
    dresid = norm_backward(total, unit, s["rs"][:, 0:1], gain1)
    s["r1"][...] = dresid
    s["e0"][...] = dresid.astype(BF)
    s["ln"][...] = jnp.concatenate([g_gain2, g_shift2, g_gain1, g_shift1, jnp.zeros((4, D), F32)], 0)


def backward_attention(s):
    s["do"][...] = nt(s["e0"][...], s["wo"][...]).astype(BF)
    low, high, is_low = lane_masks()
    for pair in range(HEADS // 2):
        cols, rows = pair_lanes(pair), slice(pair * 2 * L, (pair + 1) * 2 * L)
        grad = s["do"][:, cols]
        dprobs = nt(jnp.concatenate([grad * low, grad * high], 0), s["v"][:, cols])
        probs = s["p"][rows, :].astype(F32)
        product = probs * dprobs
        s["dsc"][rows, :] = (product - probs * jnp.sum(product, -1, keepdims=True)).astype(BF)
    for pair in range(HEADS // 2):
        cols, rows = pair_lanes(pair), slice(pair * 2 * L, (pair + 1) * 2 * L)
        one, two = (slice((2 * pair + i) * L, (2 * pair + i + 1) * L) for i in range(2))
        both = nn(s["dsc"][rows, :], s["k"][:, cols])
        s["dq"][:, cols] = (jnp.where(is_low, both[:L], both[L:]) * SCALE).astype(BF)
        query, grad = s["q"][:, cols], s["do"][:, cols]
        s["dk"][:, cols] = (jnp.where(is_low, tn(s["dsc"][one, :], query), tn(s["dsc"][two, :], query)) * SCALE).astype(BF)
        s["dv"][:, cols] = jnp.where(is_low, tn(s["p"][one, :], grad), tn(s["p"][two, :], grad)).astype(BF)
    grad = s["r1"][...] + nt(s["dq"][...], s["wq"][...])
    grad = grad + nt(s["dk"][...], s["wk"][...]) + nt(s["dv"][...], s["wv"][...])
    s["ds"][...] = grad.astype(BF)
    s["dh"][...] = grad


VECTORS = (BQ, BV, BO, G1, S1, C2, G2, S2)


LOADED = {**WEIGHTS, "vec": ((VEC, D), F32), "seg": ((ROWS, L), jnp.int32), "cot": ((ROWS, L, D), BF)}


def first_forward(row, outside, state, here):
    if row == 0:
        reads, updates = {**outside, "here": here}, {}
        news = {**LOADED, **LATE, "pos": ((4,), jnp.int32), **both_rows(FORWARD)}
    else:
        reads = {**outside, "pos": state["pos"]}
        updates = {n: state[n] for n in (*LOADED, *FORWARD)}
        news = {}
    news["sent"] = ROW["y"]

    def body(s):
        copies, waiting = {}, []

        def start(n, source, target):
            copies[n] = pltpu.make_async_copy(source, target, s["sems"].at[len(copies)])
            copies[n].start()
            waiting.append(n)

        def rest():
            for m in ("wo", "w1", "w2"):
                start(m, s["in_" + m].at[0], s[m])
            start("cot", s["in_cot"], s["cot"])

        def need(n):
            if n in waiting:
                waiting.remove(n)
                copies[n].wait()
            if n == "wq" and row == 0:
                rest()

        def load():
            start("h", s["in_h"], s["h"])
            start("wq", s["in_wq"].at[0], s["wq"])
            for i in VECTORS:
                start(i, s[f"in_{i}"], s["vec"].at[pl.ds(i, 1), :])
            for n in ("wk", "wv"):
                start(n, s["in_" + n].at[0], s[n])
            start("seg", s["in_seg"], s["seg"])
            for j in range(NBLK):
                start(C1 + j, s[f"in_{C1}"].at[:, pl.ds(j * BLK, BLK)], s["vec"].at[pl.ds(C1 + j, 1), :])

        if row == 0:
            place = pltpu.make_async_copy(s["in_pos"], s["pos"], s["sems"].at[SEMS - 1])
            place.start()

        @pl.when((s["here"][0, 0] if row == 0 else s["pos"][SEC]) == 0)
        def _():
            if row == 0:
                load()
                for n in ("h", "seg", *VECTORS, *range(C1, C1 + NBLK)):
                    need(n)
            r = of_row(s, row, FORWARD)
            forward(r, need, row, row == 0)
            s["sent"][...] = r["y"][...]
            need("cot")

        if row == 0:
            place.wait()
        else:
            copies.clear()

            @pl.when(s["pos"][SEC] == 1)
            def _():
                load()
                rest()
                for n in list(waiting):
                    need(n)

    got = kernel(f"first_forward_{row}", body, reads, updates, news, sems=SEMS, outside=list(outside), flops=3 * 10**9, nbytes=8 * 10**6)
    return got.pop("sent"), {**state, **got}


SEMS = 32


def first_slopes(state):
    def body(s):
        @pl.when(s["pos"][SEC] == 0)
        def _():
            for j in range(FF // 128):
                cols = slice(j * 128, j * 128 + 128)
                s["gp"][0, :, cols] = gelu_slope(s["z"][:, cols], s["half"][:, cols]).astype(BF)

    return {**state, **kernel("first_slopes", body, {n: state[n] for n in ("pos", *LATE)}, {"gp": state["gp"]}, {})}


def second_both(row, arrived, state):
    reads = {n: state[n] for n in ("vec", "seg", "pos", "cot", *WEIGHTS)}
    reads["arrived"] = arrived
    updates = {n: state[n] for n in (*FORWARD, *LATE)}
    news = {"ds": ROW["y"]}
    if row == 0:
        news.update(both_rows(BACKWARD))
    else:
        updates.update({n: state[n] for n in BACKWARD})

    def body(s):
        r = of_row(s, row, FORWARD + BACKWARD)
        r["dy"] = s["cot"].at[row]

        @pl.when(s["pos"][SEC] == 1)
        def _():
            r["h"][...] = s["arrived"][...]
            forward(r, lambda n: None, row, True)
            backward_feed(r, True)
            backward_attention(r)

    got = kernel(f"second_both_{row}", body, reads, updates, news, {**BACK, "r1": ROW["dh"]}, flops=6 * 10**9, nbytes=8 * 10**6)
    return got.pop("ds"), {**state, **got}


def first_feed(row, arrived, state, after):
    reads = {n: state[n] for n in ("vec", "pos", "w1", "w2", "x1", "x2", "rs", "gp")}
    reads.update(dy=arrived, **after)
    keep = ("e2", "e1", "e0", "ln")

    def body(s):
        @pl.when(s["pos"][SEC] == 0)
        def _():
            backward_feed(of_row(s, row, ("x1", "x2", "rs", "gp", *keep)), False)

    got = kernel(f"first_feed_{row}", body, reads, {n: state[n] for n in keep}, {"r1": ROW["dh"]}, flops=10**9, nbytes=8 * 10**6)
    return got.pop("r1"), {**state, **got}


def first_attention(row, dresid, state, after):
    reads = {n: state[n] for n in ("pos", "wq", "wk", "wv", "wo", "e0", "q", "k", "v", "p")}
    reads.update(r1=dresid, **after)
    keep = ("dq", "dk", "dv", "dh")

    def body(s):
        @pl.when(s["pos"][SEC] == 0)
        def _():
            backward_attention(of_row(s, row, ("e0", "q", "k", "v", "p", *keep)))

    got = kernel(f"first_attention_{row}", body, reads, {n: state[n] for n in keep}, {}, {**BACK, "ds": ROW["y"]}, flops=2 * 10**9, nbytes=8 * 10**6)
    return {**state, **got}


T2 = ROWS * L
AQ = D // 2


def aligned(index, size):
    return pl.multiple_of(index * size, size)


def per_core(s, work):
    for core in range(2):
        pl.when(s["pos"][CORE] == core)(functools.partial(work, core))


def feed_block(s, up, j, rows):
    cols = pl.ds(aligned(j, BLK), BLK)
    if up:
        return tn(s["u"][rows, :], s["e1"][rows, cols])
    return tn(s["a"][rows, cols], s["e2"][rows, :])


def attention_block(s, out, i, rows):
    left, right = (("o", "e0"), ("h", "dq"))[i] if out else ("h", ("dk", "dv")[i])
    return tn(s[left][rows, :], s[right][rows, :])


def vector_rows(s, row, rows):
    ones = jnp.ones((8, L), BF)

    def total(value):
        return nn(ones, value)[0:1, :]

    ln = s["ln"][row]
    got = [total(s[n][rows, :]) for n in ("dq", "dv", "e0")] + [ln[2:3], ln[3:4], total(s["e2"][rows, :]), ln[0:1], ln[1:2]]
    got += [total(s["e1"][rows, j * BLK : j * BLK + BLK]) for j in range(NBLK)]
    return jnp.concatenate(got + [jnp.zeros((VEC - len(got), D), F32)], 0)


FIRST_ROW, LAST_ROW = slice(0, L), slice(L, 2 * L)


def first_products(pos, ops):
    def body(s):
        def work(core):
            for j in range(NBLK):
                rows = slice(j * BLK, j * BLK + BLK)
                s["fs"][rows, :] = feed_block(s, core == 0, j, FIRST_ROW).astype(BF)
                s["fk"][rows, :] = feed_block(s, core == 1, j, FIRST_ROW).astype(BF)
            for i in range(2):
                rows = slice(i * D, i * D + D)
                s["ts"][rows, :] = attention_block(s, core == 1, i, FIRST_ROW).astype(BF)
                s["tk"][rows, :] = attention_block(s, core == 0, i, FIRST_ROW).astype(BF)

        per_core(s, work)
        s["vec"][...] = vector_rows(s, 0, FIRST_ROW)

    news = {"fs": ((FF, D), BF), "fk": ((FF, D), BF), "ts": ((2 * D, D), BF), "tk": ((2 * D, D), BF), "vec": ((VEC, D), F32)}
    return kernel("first_products", body, {"pos": pos, **ops}, {}, news)


def feed_send(pos, ops, early, distances, after):
    def body(s):
        def work(core):
            for i, k in enumerate(distances):
                j = lax.rem(s["pos"][SECOND] + k, 4)
                more = s["early"][pl.ds(aligned(j, BLK), BLK), :].astype(F32)
                s["out"][i * BLK : i * BLK + BLK, :] = (feed_block(s, core == 0, j, LAST_ROW) + more).astype(BF)

        per_core(s, work)

    return kernel("feed_send", body, {"pos": pos, **ops, "early": early, **after}, {}, {"out": ((len(distances) * BLK, D), BF)})["out"]


def attention_send(pos, ops, early, early_vec, after):
    def body(s):
        def work(core):
            for i in range(2):
                rows = slice(i * D, i * D + D)
                s["out"][rows, :] = (attention_block(s, core == 1, i, LAST_ROW) + s["early"][rows, :].astype(F32)).astype(BF)

        per_core(s, work)
        s["vec"][...] = (s["early_vec"][...] + vector_rows(s, 1, LAST_ROW)).astype(BF)
        s["out"][2 * D :, :] = s["vec"][...]

    news = {"out": ((2 * D + VEC, D), BF), "vec": ((VEC, D), BF)}
    got = kernel("attention_send", body, {"pos": pos, **ops, "early": early, "early_vec": early_vec, **after}, {}, news)
    return got["out"], got["vec"]


def feed_keep(pos, ops, early, distances, got, after):
    def body(s):
        def work(core):
            for i, k in enumerate(distances):
                j = lax.rem(s["pos"][FIRST] + k, 4)
                more = s["got"][i * BLK : i * BLK + BLK, :].astype(F32) + s["early"][pl.ds(aligned(j, BLK), BLK), :].astype(F32)
                s[f"p{k}"][...] = (feed_block(s, core == 1, j, LAST_ROW) + more).astype(BF)

        per_core(s, work)

    news = {f"p{k}": ((BLK, D), BF) for k in distances}
    return kernel("feed_keep", body, {"pos": pos, **ops, "early": early, "got": got, **after}, {}, news)


def attention_keep(pos, ops, early, vec, got):
    def body(s):
        def work(core):
            for i in range(2):
                rows = slice(i * D, i * D + D)
                more = s["got"][rows, :].astype(F32) + s["early"][rows, :].astype(F32)
                s["acc"][rows, :] = (attention_block(s, core == 0, i, LAST_ROW) + more).astype(BF)

        per_core(s, work)
        shared = (s["vec"][...].astype(F32) + s["got"][2 * D :, :].astype(F32)).astype(BF)
        for k in range(4):
            j = lax.rem(s["pos"][FIRST] + k, 4)
            s[f"p{k}"][:AQ, :] = s["acc"][pl.ds(aligned(j, AQ), AQ), :]
            s[f"p{k}"][AQ:, :] = shared

    news = {f"p{k}": ((AQ + VEC, D), BF) for k in range(4)}
    reads = {"pos": pos, **ops, "early": early, "vec": vec, "got": got}
    return list(kernel("attention_keep", body, reads, {}, news, {"acc": ((2 * D, D), BF)}).values())


def total_of(s, tag):
    wide = [s[f"{tag}{k}"][...].astype(F32) for k in range(4)]
    return ((wide[0] + wide[2]) + (wide[1] + wide[3])).astype(BF)


def by_distance(tag, values):
    return {f"{tag}{k}": v for k, v in enumerate(values)}


FQ, TQ = BLK // 4, AQ // 4
SHARD = FQ + TQ


def sum_split(pos, feed, atts):
    def body(s):
        s["att"][...] = total_of(s, "t")
        for k in range(4):
            j = lax.rem(s["pos"][SECOND] + k, 4)
            s[f"p{k}"][:FQ, :] = s["feed"][pl.ds(aligned(j, FQ), FQ), :]
            s[f"p{k}"][FQ:SHARD, :] = s["att"][pl.ds(aligned(j, TQ), TQ), :]
            s[f"p{k}"][SHARD:, :] = s["att"][AQ:, :]

    reads = {"pos": pos, "feed": feed, **by_distance("t", atts)}
    news = {f"p{k}": ((SHARD + VEC, D), BF) for k in range(4)}
    scratch = {"att": ((AQ + VEC, D), BF)}
    return list(kernel("sum_split", body, reads, {}, news, scratch).values())


def sum_four(got):
    def body(s):
        s["out"][...] = total_of(s, "g")

    return kernel("sum_four", body, by_distance("g", got), {}, {"out": (got[0].shape, BF)})["out"]


def sum_two(own, got):
    def body(s):
        total = (s["a"][...].astype(F32) + s["b"][...].astype(F32)).astype(BF)
        s["out"][...] = total[:SHARD]
        s["vec"][...] = total[SHARD:]

    got = kernel("sum_two", body, {"a": own, "b": got}, {}, {"out": ((SHARD, D), BF), "vec": ((VEC, D), BF)})
    return got["out"], got["vec"]


HALF = (BLK + AQ) // 2


def join(pos, got, vec):
    def body(s):
        for k in range(4):
            j = lax.rem(s["pos"][SECOND] + (4 - k), 4)
            s["out"][pl.ds(aligned(j, FQ), FQ), :] = s[f"g{k}"][:FQ, :]
            s["out"][pl.ds(aligned(j, TQ) + BLK, TQ), :] = s[f"g{k}"][FQ:, :]
        s["out"][2 * HALF :, :] = s["vec"][...]
        s["up"][...] = s["out"][:HALF, :]
        s["low"][...] = s["out"][HALF : 2 * HALF, :]

    news = {"out": ((2 * HALF + VEC, D), BF), "up": ((HALF, D), BF), "low": ((HALF, D), BF)}
    return kernel("join", body, {"pos": pos, **by_distance("g", got), "vec": vec}, {}, news).values()


MATRICES = ("o", "q", "k", "v")


def pair(one, two):
    def body(s):
        s["out"][:HALF, :] = s["one"][...]
        s["out"][HALF:, :] = s["two"][...]

    return kernel("pair", body, {"one": one, "two": two}, {}, {"out": ((2 * HALF, D), BF)})["out"]


def finish(pos, name, halves, done):
    arrays = []
    for array, *_ in halves:
        arrays += [] if any(array is a for a in arrays) else [array]

    def named(array):
        return "b%d" % [array is a for a in arrays].index(True)

    def body(s):
        started = []

        def move(source, target, sem):
            pltpu.make_async_copy(source, target, s["sems"].at[sem]).start()

        for i, (array, row, mine, k, lower) in enumerate(halves):
            s["wide"][i] = s[named(array)][row : row + HALF, :].astype(F32)
            rest = BLK - HALF if lower else HALF
            feed = s["wide"].at[i, pl.ds(0, rest)]
            piece = lax.rem(s["pos"][FIRST if mine else SECOND] + (4 - k), 4)
            down = (s["pos"][CORE] == 0) if mine else (s["pos"][CORE] == 1)
            at, cols = pl.ds(pl.multiple_of(piece * BLK + lower * HALF, 128), rest), pl.ds(aligned(piece, BLK), BLK)
            pl.when(down)(functools.partial(move, feed, s["down"].at[0, at, :], 2 * i))
            pl.when(jnp.logical_not(down))(functools.partial(move, feed, s["up"].at[0, pl.ds(lower * HALF, rest), cols], 2 * i))
            started.append((feed, s["down"].at[0, pl.ds(0, rest), :], 2 * i))
            if lower:
                att = s["wide"].at[i, pl.ds(rest, AQ)]
                kind = jnp.where(down, 0, 2) + lax.div(piece, 2)
                at = pl.ds(aligned(lax.rem(piece, 2), AQ), AQ)
                for which, n in enumerate(MATRICES):
                    pl.when(kind == which)(functools.partial(move, att, s[n].at[0, at, :], 2 * i + 1))
                started.append((att, s["o"].at[0, pl.ds(0, AQ), :], 2 * i + 1))
        for source, target, sem in started:
            pltpu.make_async_copy(source, target, s["sems"].at[sem]).wait()

    reads = {"pos": pos, **{named(v): v for v in arrays}}
    news = {} if done else {"up": ((1, D, FF), F32), "down": ((1, FF, D), F32), **{n: ((1, D, D), F32) for n in MATRICES}}
    scratch = {"wide": ((len(halves), HALF, D), F32)}
    return kernel(name, body, reads, done, news, scratch, sems=2 * len(halves), outside=("up", "down", *MATRICES))


def hold(values, stored=(), near=()):
    updates = {f"x{i}": v for i, v in enumerate(values)}
    outside = {f"a{i}": v for i, v in enumerate(stored)}
    reads = {**outside, **{f"b{i}": v for i, v in enumerate(near)}}
    return list(kernel("hold", lambda s: None, reads, updates, {}, outside=outside).values())


def store(y, dh):
    def body(s):
        moves = [pltpu.make_async_copy(s[n], s["out_" + n].at[0], s["sems"].at[i]) for i, n in enumerate(("y", "dh"))]
        for move in moves:
            move.start()
        for move in moves:
            move.wait()

    news = {"out_y": ((1, *y.shape), BF), "out_dh": ((1, *dh.shape), F32)}
    got = kernel("store", body, {"y": y, "dh": dh}, {}, news, sems=2, outside=news)
    return got["out_y"], got["out_dh"]


def vector_finish(pos, mine, other):
    def body(s):
        own = (s["pos"][CORE] == 0).astype(F32)
        values = jnp.where(own > 0.5, s["mine"][2 * HALF :, :].astype(F32), s["other"][2 * HALF :, :].astype(F32))
        for i in VECTORS:
            s[str(i)][...] = values[i : i + 1, :]
        for j in range(NBLK):
            s[str(C1)][:, j * BLK : j * BLK + BLK] = values[C1 + j : C1 + j + 1, :]

    news = {**{str(i): ((1, D), F32) for i in VECTORS}, str(C1): ((1, FF), F32)}
    return kernel("vector_finish", body, {"pos": pos, "mine": mine, "other": other}, {}, news, free=news)


def spot(y, z, x, core):
    return ((y * 2 + z) * 4 + x) * 2 + core


def everywhere(move):
    return [(spot(y, z, x, c), spot(*move(y, z, x, c))) for y in range(4) for z in range(2) for x in range(4) for c in range(2)]


def along(stage, distance):
    def move(y, z, x, core):
        if (core == 0) == (stage == 0):
            return y, z, (x + distance) % 4, core
        return (y + distance) % 4, z, x, core

    return everywhere(move)


def send(value, route):
    return lax.ppermute(value, "dp", route)


def to_core(value):
    return send(value, everywhere(lambda y, z, x, core: (y, z, x, 1 - core)))


def to_z(value):
    return send(value, everywhere(lambda y, z, x, core: (y, 1 - z, x, core)))


def spread(pieces, stage):
    sent = {k: send(pieces[k], along(stage, k)) for k in (1, 3, 2)}
    return [pieces[0]] + [sent[k] for k in (1, 2, 3)]


def shards(tokens, segments, cotangent, w_query, q_bias, w_key, w_value, v_bias, w_out, out_bias, ln1_gain, ln1_shift, w_up, up_bias, w_down, down_bias, ln2_gain, ln2_shift):
    dp = lax.axis_index("dp")
    core, x, y = dp % 2, (dp // 2) % 4, dp // 16
    first, second = jnp.where(core == 0, x, y), jnp.where(core == 0, y, x)
    here = jnp.stack([lax.axis_index("section"), core, first, second]).astype(jnp.int32)
    outside = {"in_pos": here, "in_h": tokens, "in_seg": segments, "in_cot": cotangent}
    outside.update(in_wq=w_query, in_wk=w_key, in_wv=w_value, in_wo=w_out, in_w1=w_up, in_w2=w_down)
    vectors = {BQ: q_bias, BV: v_bias, BO: out_bias, G1: ln1_gain, S1: ln1_shift, C2: down_bias, G2: ln2_gain, S2: ln2_shift, C1: up_bias}
    outside.update({f"in_{i}": v for i, v in vectors.items()})

    def forth(value):
        return lax.ppermute(value, "section", [(0, 1)])

    def back(value):
        return lax.ppermute(value, "section", [(1, 0)])

    state = {}
    came, dcame = [], []
    for row in range(ROWS):
        sent, state = first_forward(row, outside, state, jnp.broadcast_to(here[:1], (8, 128)))
        came.append(forth(sent))
    state = first_slopes(state)
    for row in range(ROWS):
        sent, state = second_both(row, came[row], state)
        dcame.append(back(sent))
    pos = state["pos"]

    def flat(*names):
        return {n: state[n].reshape((T2, state[n].shape[-1])) for n in names}

    dresid, state = first_feed(0, dcame[0], state, {})
    state = first_attention(0, dresid, state, {})
    names = ("u", "a", "o", "h", "e1", "e2", "e0", "dq", "dk", "dv")
    early = first_products(pos, {**flat(*names), "ln": state["ln"]})
    dresid, state = first_feed(1, dcame[1], state, {"after": early["vec"]})
    near, far = (1, 3), (2, 0)
    feed_ops = flat("u", "a", "e1", "e2")
    near_out = feed_send(pos, feed_ops, early["fs"], near, {})
    far_out = feed_send(pos, feed_ops, early["fs"], far, {"after": near_out})
    state = first_attention(1, dresid, state, {"after": far_out})
    feeds = feed_keep(pos, feed_ops, early["fk"], near, to_core(near_out), {})
    ops = flat(*names)
    att_out, vec = attention_send(pos, {**ops, "ln": state["ln"]}, early["ts"], early["vec"], {"after": feeds["p3"]})
    atts = attention_keep(pos, flat("o", "h", "e0", "dq", "dk", "dv"), early["tk"], vec, to_core(att_out))
    feeds.update(feed_keep(pos, feed_ops, early["fk"], far, to_core(far_out), {"after": atts[0]}))
    pieces = sum_split(pos, sum_four(spread([feeds[f"p{k}"] for k in range(4)], 0)), spread(atts, 0))
    mine = sum_four(spread(pieces, 1))
    shard, vec = sum_two(mine, to_z(mine))
    block, up, low = join(pos, spread([shard] * 4, 1), vec)
    up_behind, low_ahead = send(up, along(0, 1)), send(low, along(0, 3))
    low_behind, up_ahead = send(low, along(0, 1)), send(up, along(0, 3))
    other = to_core(block)
    y, dh = store(state["y"], state["dh"])
    g = vector_finish(pos, block, other)
    own = [(v, h * HALF, mine, 0, h) for v, mine in ((block, True), (other, False)) for h in range(2)]
    full = finish(pos, "finish_own", own, {})
    up_behind, low_ahead = hold([up_behind, low_ahead], [y, dh, g[str(BQ)], full["up"]])
    opposite = [send(up_behind, along(0, 1)), send(low_ahead, along(0, 3))]
    first = pair(up_behind, low_ahead)
    low_behind, up_ahead = hold([low_behind, up_ahead], near=[up_behind, low_ahead])
    sides = [(up_behind, 0, True, 1, 0), (low_behind, 0, True, 1, 1), (up_ahead, 0, True, 3, 0), (low_ahead, 0, True, 3, 1)]
    full = finish(pos, "finish_sides", sides, full)
    opposite = hold(opposite, [full["up"]])
    others = [to_core(b) for b in opposite]
    first = to_core(first)
    second = [(first, 0, False, 1, 0), (first, HALF, False, 3, 1), (to_core(low_behind), 0, False, 1, 1), (to_core(up_ahead), 0, False, 3, 0)]
    full = finish(pos, "finish_second", second + [(b, 0, True, 2, h) for h, b in enumerate(opposite)], full)
    full = finish(pos, "finish_last", [(b, 0, False, 2, h) for h, b in enumerate(others)], full)

    def vector(i):
        return g[str(i)]

    return (
        y,
        dh,
        full["q"],
        vector(BQ),
        full["k"],
        full["v"],
        vector(BV),
        full["o"],
        vector(BO),
        vector(G1),
        vector(S1),
        full["up"],
        vector(C1),
        full["down"],
        vector(C2),
        vector(G2),
        vector(S2),
    )


def solution(mesh):
    row, matrix, vector = P("dp", None, None), P("section", None, None), P("section", None)
    in_specs = (row, P("dp", None), row, matrix, vector, matrix, matrix, vector, matrix, vector, vector, vector, matrix, vector, matrix, vector, vector, vector)
    big = P("section", "dp", None, None)
    out_specs = (big, big, matrix, vector, matrix, matrix, vector, matrix, vector, vector, vector, matrix, vector, matrix, vector, vector, vector)
    return jax.shard_map(shards, mesh=mesh, in_specs=in_specs, out_specs=out_specs, check_vma=False)
```

```python
import functools

import jax
import jax.numpy as jnp
from jax import lax
from jax.experimental import pallas as pl
from jax.experimental.pallas import tpu as pltpu
from jax.sharding import PartitionSpec as P

BF, F32 = jnp.bfloat16, jnp.float32
ROWS, L, D, FF, HEADS, HEAD = 2, 256, 512, 2048, 8, 64
BLK = 512
NBLK = FF // BLK
NARROW = 256
GELU = 0.7978845608028654
VEC = 16
MiB = 1 << 20
SCALE = HEAD ** (-0.5)
BQ, BV, BO, G1, S1, C2, G2, S2, C1 = 0, 1, 2, 3, 4, 5, 6, 7, 8
SEC, CORE, FIRST, SECOND = 0, 1, 2, 3


def nn(a, b):
    return jnp.dot(a, b, preferred_element_type=F32)


def nt(a, b):
    return lax.dot_general(a, b, (((1,), (1,)), ((), ())), preferred_element_type=F32)


def tn(a, b):
    return lax.dot_general(a, b, (((0,), (0,)), ((), ())), preferred_element_type=F32)


def kernel(name, body, reads, updates, news, scratch=None, sems=0, outside=(), free=(), vmem=12, flops=1000, nbytes=1000):
    scratch = scratch or {}
    outs = {**updates, **news}
    names = list(reads) + list(updates)

    def spec(n):
        if n == "in_pos":
            return pl.BlockSpec(memory_space=pl.ANY)
        if n in outside:
            return pl.BlockSpec(memory_space=pltpu.HBM)
        if n == "pos":
            return pl.BlockSpec(memory_space=pltpu.SMEM)
        return pl.BlockSpec(memory_space=pltpu.VMEM)

    def shape(n):
        if n == "pos":
            return pltpu.SMEM(*news[n])
        space = pltpu.HBM if n in outside else jax.ShapeDtypeStruct if n in free else pltpu.VMEM
        return space(*news[n]) if n in news else space(updates[n].shape, updates[n].dtype)

    reads = {n: pltpu.with_memory_space_constraint(v, pltpu.HBM) if n in outside and n != "in_pos" else v for n, v in reads.items()}

    def whole(*refs):
        s = dict(zip(reads, refs))
        rest = refs[len(names) :]
        s.update(zip(outs, rest))
        s.update(zip(list(scratch) + ["sems"], rest[len(outs) :]))
        body(s)

    got = pl.pallas_call(
        whole,
        out_shape=[shape(n) for n in outs],
        in_specs=[spec(n) for n in names],
        out_specs=[spec(n) for n in outs],
        scratch_shapes=[pltpu.VMEM(*v) for v in scratch.values()] + ([pltpu.SemaphoreType.DMA((sems,))] if sems else []),
        input_output_aliases={len(reads) + i: i for i in range(len(updates))},
        compiler_params=pltpu.CompilerParams(vmem_limit_bytes=vmem * MiB),
        cost_estimate=pl.CostEstimate(flops=flops, bytes_accessed=nbytes, transcendentals=0),
        name=name,
    )(*reads.values(), *updates.values())
    return dict(zip(outs, got))


def norm_forward(resid, gain, shift):
    centre = resid - jnp.mean(resid, -1, keepdims=True)
    rstd = lax.rsqrt(jnp.mean(centre * centre, -1, keepdims=True) + 1e-05)
    unit = centre * rstd
    return unit, rstd, unit * gain + shift


def norm_backward(grad, unit, rstd, gain):
    scaled = grad * gain
    inner = scaled - jnp.mean(scaled, -1, keepdims=True)
    return rstd * (inner - unit * jnp.mean(scaled * unit, -1, keepdims=True))


def pair_lanes(pair):
    return slice(pair * 2 * HEAD, (pair + 1) * 2 * HEAD)


def lane_masks():
    lane = lax.broadcasted_iota(jnp.int32, (L, 128), 1)
    low = (lane < HEAD).astype(F32)
    return low.astype(BF), (1.0 - low).astype(BF), lane < HEAD


ROW = dict(
    h=((L, D), BF),
    y=((L, D), BF),
    o=((L, D), BF),
    u=((L, D), BF),
    a=((L, FF), BF),
    q=((L, D), BF),
    k=((L, D), BF),
    v=((L, D), BF),
    p=((HEADS * L, L), BF),
    gp=((L, FF), BF),
    x1=((L, D), F32),
    x2=((L, D), F32),
    rs=((L, 256), F32),
    e2=((L, D), BF),
    e1=((L, FF), BF),
    e0=((L, D), BF),
    dq=((L, D), BF),
    dk=((L, D), BF),
    dv=((L, D), BF),
    ln=((8, D), F32),
    dh=((L, D), F32),
)
FORWARD = ("h", "y", "o", "u", "a", "q", "k", "v", "p", "gp", "x1", "x2", "rs")
BACKWARD = ("e2", "e1", "e0", "dq", "dk", "dv", "ln", "dh")
WEIGHTS = dict(wq=((D, D), BF), wk=((D, D), BF), wv=((D, D), BF), wo=((D, D), BF), w1=((D, FF), BF), w2=((FF, D), BF))


LATE = dict(z=((L, FF), F32), half=((L, FF), F32))


def both_rows(names):
    return {n: ((ROWS,) + ROW[n][0], ROW[n][1]) for n in names}


def of_row(s, row, names):
    return {**s, **{n: s[n].at[row] for n in names}}


def gelu_slope(z, half):
    return half + (z * half * (2.0 - 2.0 * half)) * (GELU + (0.134145 * GELU) * (z * z))


def forward(s, need, row, late):
    need("wq")
    hidden = s["h"][...]

    def vec(i):
        return s["vec"][i : i + 1, :]

    s["q"][...] = (nn(hidden, s["wq"][...]) + vec(BQ)).astype(BF)
    need("wk")
    s["k"][...] = nn(hidden, s["wk"][...]).astype(BF)
    need("wv")
    s["v"][...] = (nn(hidden, s["wv"][...]) + vec(BV)).astype(BF)
    seg = jnp.broadcast_to(s["seg"][row : row + 1, :].astype(F32), (L, L))
    same = seg == seg.T
    low, high, is_low = lane_masks()
    for head in range(HEADS):
        cols, rows = pair_lanes(head // 2), slice(head * L, head * L + L)
        scores = nt(s["q"][:, cols] * ((high if head % 2 else low) * SCALE), s["k"][:, cols])
        scores = jnp.where(same, scores, -1000000000.0)
        weight = jnp.exp(scores - jnp.max(scores, -1, keepdims=True))
        s["p"][rows, :] = (weight * (1.0 / jnp.sum(weight, -1, keepdims=True))).astype(BF)
    for pair in range(HEADS // 2):
        cols = pair_lanes(pair)
        both = nn(s["p"][pair * 2 * L : (pair + 1) * 2 * L, :], s["v"][:, cols])
        s["o"][:, cols] = jnp.where(is_low, both[:L], both[L:]).astype(BF)
    need("wo")
    resid = hidden.astype(F32) + nn(s["o"][...], s["wo"][...]) + vec(BO)
    unit, rstd, normed = norm_forward(resid, vec(G1), vec(S1))
    s["x1"][...] = unit
    s["rs"][:, :128] = jnp.broadcast_to(rstd, (L, 128))
    s["u"][...] = normed.astype(BF)
    need("w1")
    need("w2")
    total = normed + vec(C2)
    for j in range(FF // NARROW):
        cols = slice(j * NARROW, (j + 1) * NARROW)
        at = j * NARROW % BLK
        z = nn(s["u"][...], s["w1"][:, cols]) + vec(C1 + j * NARROW // BLK)[:, at : at + NARROW]
        square = z * z
        half = 0.5 + 0.5 * jnp.tanh(z * (GELU + (0.044715 * GELU) * square))
        if late:
            s["z"][:, cols] = z
            s["half"][:, cols] = half
        else:
            s["gp"][:, cols] = gelu_slope(z, half).astype(BF)
        active = (z * half).astype(BF)
        s["a"][:, cols] = active
        total = total + nn(active, s["w2"][cols, :])
    unit, rstd, out = norm_forward(total, vec(G2), vec(S2))
    s["y"][...] = out.astype(BF)
    s["x2"][...] = unit
    s["rs"][:, 128:] = jnp.broadcast_to(rstd, (L, 128))


BACK = dict(do=((L, D), BF), dsc=((HEADS * L, L), BF))


def backward_feed(s, late):
    gain1, gain2 = s["vec"][G1 : G1 + 1, :], s["vec"][G2 : G2 + 1, :]
    dout = s["dy"][...].astype(F32)
    unit = s["x2"][...]
    g_gain2 = jnp.sum(dout * unit, 0, keepdims=True)
    g_shift2 = jnp.sum(dout, 0, keepdims=True)
    dsecond = norm_backward(dout, unit, s["rs"][:, 128:129], gain2)
    s["e2"][...] = dsecond.astype(BF)
    for j in range(NBLK):
        cols = slice(j * BLK, j * BLK + BLK)
        dactive = nt(s["e2"][...], s["w2"][cols, :])
        slope = gelu_slope(s["z"][:, cols], s["half"][:, cols]) if late else s["gp"][:, cols].astype(F32)
        s["e1"][:, cols] = (slope * dactive).astype(BF)
    total = dsecond + nt(s["e1"][...], s["w1"][...])
    unit = s["x1"][...]
    g_gain1 = jnp.sum(total * unit, 0, keepdims=True)
    g_shift1 = jnp.sum(total, 0, keepdims=True)
    dresid = norm_backward(total, unit, s["rs"][:, 0:1], gain1)
    s["r1"][...] = dresid
    s["e0"][...] = dresid.astype(BF)
    s["ln"][...] = jnp.concatenate([g_gain2, g_shift2, g_gain1, g_shift1, jnp.zeros((4, D), F32)], 0)


def backward_attention(s):
    s["do"][...] = nt(s["e0"][...], s["wo"][...]).astype(BF)
    low, high, is_low = lane_masks()
    for pair in range(HEADS // 2):
        cols, rows = pair_lanes(pair), slice(pair * 2 * L, (pair + 1) * 2 * L)
        grad = s["do"][:, cols]
        dprobs = nt(jnp.concatenate([grad * low, grad * high], 0), s["v"][:, cols])
        probs = s["p"][rows, :].astype(F32)
        product = probs * dprobs
        s["dsc"][rows, :] = (product - probs * jnp.sum(product, -1, keepdims=True)).astype(BF)
    for pair in range(HEADS // 2):
        cols, rows = pair_lanes(pair), slice(pair * 2 * L, (pair + 1) * 2 * L)
        one, two = (slice((2 * pair + i) * L, (2 * pair + i + 1) * L) for i in range(2))
        both = nn(s["dsc"][rows, :], s["k"][:, cols])
        s["dq"][:, cols] = (jnp.where(is_low, both[:L], both[L:]) * SCALE).astype(BF)
        query, grad = s["q"][:, cols], s["do"][:, cols]
        s["dk"][:, cols] = (jnp.where(is_low, tn(s["dsc"][one, :], query), tn(s["dsc"][two, :], query)) * SCALE).astype(BF)
        s["dv"][:, cols] = jnp.where(is_low, tn(s["p"][one, :], grad), tn(s["p"][two, :], grad)).astype(BF)


def backward_input(s):
    grad = s["r1"][...] + nt(s["dq"][...], s["wq"][...])
    grad = grad + nt(s["dk"][...], s["wk"][...]) + nt(s["dv"][...], s["wv"][...])
    s["ds"][...] = grad.astype(BF)
    s["dh"][...] = grad


VECTORS = (BQ, BV, BO, G1, S1, C2, G2, S2)


LOADED = {**WEIGHTS, "vec": ((VEC, D), F32), "seg": ((ROWS, L), jnp.int32), "cot": ((ROWS, L, D), BF)}


def first_forward(row, outside, state, here):
    if row == 0:
        reads, updates = {**outside, "here": here}, {}
        news = {**LOADED, **LATE, "pos": ((4,), jnp.int32), **both_rows(FORWARD)}
    else:
        reads = {**outside, "pos": state["pos"]}
        updates = {n: state[n] for n in (*LOADED, *FORWARD)}
        news = {}
    news["sent"] = ROW["y"]

    def body(s):
        copies, waiting = {}, []

        def start(n, source, target):
            copies[n] = pltpu.make_async_copy(source, target, s["sems"].at[len(copies)])
            copies[n].start()
            waiting.append(n)

        def rest():
            for m in ("wo", "w1", "w2"):
                start(m, s["in_" + m].at[0], s[m])
            start("cot", s["in_cot"], s["cot"])

        def need(n):
            if n in waiting:
                waiting.remove(n)
                copies[n].wait()
            if n == "wq" and row == 0:
                rest()

        def load():
            start("h", s["in_h"], s["h"])
            start("wq", s["in_wq"].at[0], s["wq"])
            for i in VECTORS:
                start(i, s[f"in_{i}"], s["vec"].at[pl.ds(i, 1), :])
            for n in ("wk", "wv"):
                start(n, s["in_" + n].at[0], s[n])
            start("seg", s["in_seg"], s["seg"])
            for j in range(NBLK):
                start(C1 + j, s[f"in_{C1}"].at[:, pl.ds(j * BLK, BLK)], s["vec"].at[pl.ds(C1 + j, 1), :])

        if row == 0:
            place = pltpu.make_async_copy(s["in_pos"], s["pos"], s["sems"].at[SEMS - 1])
            place.start()

        @pl.when((s["here"][0, 0] if row == 0 else s["pos"][SEC]) == 0)
        def _():
            if row == 0:
                load()
                for n in ("h", "seg", *VECTORS, *range(C1, C1 + NBLK)):
                    need(n)
            r = of_row(s, row, FORWARD)
            forward(r, need, row, row == 0)
            s["sent"][...] = r["y"][...]
            need("cot")

        if row == 0:
            place.wait()
        else:
            copies.clear()

            @pl.when(s["pos"][SEC] == 1)
            def _():
                load()
                rest()
                for n in list(waiting):
                    need(n)

    got = kernel(f"first_forward_{row}", body, reads, updates, news, sems=SEMS, outside=list(outside), flops=3 * 10**9, nbytes=8 * 10**6)
    return got.pop("sent"), {**state, **got}


SEMS = 32


def first_slopes(state):
    def body(s):
        @pl.when(s["pos"][SEC] == 0)
        def _():
            for j in range(FF // 128):
                cols = slice(j * 128, j * 128 + 128)
                s["gp"][0, :, cols] = gelu_slope(s["z"][:, cols], s["half"][:, cols]).astype(BF)

    return {**state, **kernel("first_slopes", body, {n: state[n] for n in ("pos", *LATE)}, {"gp": state["gp"]}, {})}


def second_both(row, arrived, state):
    reads = {n: state[n] for n in ("vec", "seg", "pos", "cot", *WEIGHTS)}
    reads["arrived"] = arrived
    updates = {n: state[n] for n in (*FORWARD, *LATE)}
    news = {"ds": ROW["y"]}
    if row == 0:
        news.update(both_rows(BACKWARD))
    else:
        updates.update({n: state[n] for n in BACKWARD})

    def body(s):
        r = of_row(s, row, FORWARD + BACKWARD)
        r["dy"] = s["cot"].at[row]

        @pl.when(s["pos"][SEC] == 1)
        def _():
            r["h"][...] = s["arrived"][...]
            forward(r, lambda n: None, row, True)
            backward_feed(r, True)
            backward_attention(r)
            backward_input(r)

    got = kernel(f"second_both_{row}", body, reads, updates, news, {**BACK, "r1": ROW["dh"]}, flops=6 * 10**9, nbytes=8 * 10**6)
    return got.pop("ds"), {**state, **got}


def first_feed(row, arrived, state, after):
    reads = {n: state[n] for n in ("vec", "pos", "w1", "w2", "x1", "x2", "rs", "gp")}
    reads.update(dy=arrived, **after)
    keep = ("e2", "e1", "e0", "ln")

    def body(s):
        @pl.when(s["pos"][SEC] == 0)
        def _():
            backward_feed(of_row(s, row, ("x1", "x2", "rs", "gp", *keep)), False)

    got = kernel(f"first_feed_{row}", body, reads, {n: state[n] for n in keep}, {"r1": ROW["dh"]}, flops=10**9, nbytes=8 * 10**6)
    return got.pop("r1"), {**state, **got}


def first_attention(row, state, after):
    reads = {**{n: state[n] for n in ("pos", "wo", "e0", "q", "k", "v", "p")}, **after}
    keep = ("dq", "dk", "dv")

    def body(s):
        @pl.when(s["pos"][SEC] == 0)
        def _():
            backward_attention(of_row(s, row, ("e0", "q", "k", "v", "p", *keep)))

    got = kernel(f"first_attention_{row}", body, reads, {n: state[n] for n in keep}, {}, BACK, flops=2 * 10**9, nbytes=8 * 10**6)
    return {**state, **got}


def first_input(row, dresid, state):
    reads = {**{n: state[n] for n in ("pos", "wq", "wk", "wv", "dq", "dk", "dv")}, "r1": dresid}

    def body(s):
        @pl.when(s["pos"][SEC] == 0)
        def _():
            backward_input(of_row(s, row, ("dq", "dk", "dv", "dh")))

    return {**state, **kernel(f"first_input_{row}", body, reads, {"dh": state["dh"]}, {}, {"ds": ROW["y"]})}


T2 = ROWS * L
AQ = D // 2


def aligned(index, size):
    return pl.multiple_of(index * size, size)


def per_core(s, work):
    for core in range(2):
        pl.when(s["pos"][CORE] == core)(functools.partial(work, core))


def feed_block(s, up, j, rows):
    cols = pl.ds(aligned(j, BLK), BLK)
    if up:
        return tn(s["u"][rows, :], s["e1"][rows, cols])
    return tn(s["a"][rows, cols], s["e2"][rows, :])


def attention_block(s, out, i, rows):
    left, right = (("o", "e0"), ("h", "dq"))[i] if out else ("h", ("dk", "dv")[i])
    return tn(s[left][rows, :], s[right][rows, :])


def vector_rows(s, row, rows):
    ones = jnp.ones((8, L), BF)

    def total(value):
        return nn(ones, value)[0:1, :]

    ln = s["ln"][row]
    got = [total(s[n][rows, :]) for n in ("dq", "dv", "e0")] + [ln[2:3], ln[3:4], total(s["e2"][rows, :]), ln[0:1], ln[1:2]]
    got += [total(s["e1"][rows, j * BLK : j * BLK + BLK]) for j in range(NBLK)]
    return jnp.concatenate(got + [jnp.zeros((VEC - len(got), D), F32)], 0)


FIRST_ROW, LAST_ROW = slice(0, L), slice(L, 2 * L)


def first_products(pos, ops):
    def body(s):
        def work(core):
            for j in range(NBLK):
                rows = slice(j * BLK, j * BLK + BLK)
                s["fs"][rows, :] = feed_block(s, core == 0, j, FIRST_ROW).astype(BF)
                s["fk"][rows, :] = feed_block(s, core == 1, j, FIRST_ROW).astype(BF)
            for i in range(2):
                rows = slice(i * D, i * D + D)
                s["ts"][rows, :] = attention_block(s, core == 1, i, FIRST_ROW).astype(BF)
                s["tk"][rows, :] = attention_block(s, core == 0, i, FIRST_ROW).astype(BF)

        per_core(s, work)
        s["vec"][...] = vector_rows(s, 0, FIRST_ROW)

    news = {"fs": ((FF, D), BF), "fk": ((FF, D), BF), "ts": ((2 * D, D), BF), "tk": ((2 * D, D), BF), "vec": ((VEC, D), F32)}
    return kernel("first_products", body, {"pos": pos, **ops}, {}, news)


def feed_send(pos, ops, early, distances, after):
    def body(s):
        def work(core):
            for i, k in enumerate(distances):
                j = lax.rem(s["pos"][SECOND] + k, 4)
                more = s["early"][pl.ds(aligned(j, BLK), BLK), :].astype(F32)
                s["out"][i * BLK : i * BLK + BLK, :] = (feed_block(s, core == 0, j, LAST_ROW) + more).astype(BF)

        per_core(s, work)

    return kernel("feed_send", body, {"pos": pos, **ops, "early": early, **after}, {}, {"out": ((len(distances) * BLK, D), BF)})["out"]


def attention_send(pos, ops, early, early_vec, after):
    def body(s):
        def work(core):
            for i in range(2):
                rows = slice(i * D, i * D + D)
                s["out"][rows, :] = (attention_block(s, core == 1, i, LAST_ROW) + s["early"][rows, :].astype(F32)).astype(BF)

        per_core(s, work)
        s["vec"][...] = (s["early_vec"][...] + vector_rows(s, 1, LAST_ROW)).astype(BF)
        s["out"][2 * D :, :] = s["vec"][...]

    news = {"out": ((2 * D + VEC, D), BF), "vec": ((VEC, D), BF)}
    got = kernel("attention_send", body, {"pos": pos, **ops, "early": early, "early_vec": early_vec, **after}, {}, news)
    return got["out"], got["vec"]


def feed_keep(pos, ops, early, distances, got, after):
    def body(s):
        def work(core):
            for i, k in enumerate(distances):
                j = lax.rem(s["pos"][FIRST] + k, 4)
                more = s["got"][i * BLK : i * BLK + BLK, :].astype(F32) + s["early"][pl.ds(aligned(j, BLK), BLK), :].astype(F32)
                s[f"p{k}"][...] = (feed_block(s, core == 1, j, LAST_ROW) + more).astype(BF)

        per_core(s, work)

    news = {f"p{k}": ((BLK, D), BF) for k in distances}
    return kernel("feed_keep", body, {"pos": pos, **ops, "early": early, "got": got, **after}, {}, news)


def attention_keep(pos, ops, early, vec, got):
    def body(s):
        def work(core):
            for i in range(2):
                rows = slice(i * D, i * D + D)
                more = s["got"][rows, :].astype(F32) + s["early"][rows, :].astype(F32)
                s["acc"][rows, :] = (attention_block(s, core == 0, i, LAST_ROW) + more).astype(BF)

        per_core(s, work)
        shared = (s["vec"][...].astype(F32) + s["got"][2 * D :, :].astype(F32)).astype(BF)
        for k in range(4):
            j = lax.rem(s["pos"][FIRST] + k, 4)
            s[f"p{k}"][:AQ, :] = s["acc"][pl.ds(aligned(j, AQ), AQ), :]
            s[f"p{k}"][AQ:, :] = shared

    news = {f"p{k}": ((AQ + VEC, D), BF) for k in range(4)}
    reads = {"pos": pos, **ops, "early": early, "vec": vec, "got": got}
    return list(kernel("attention_keep", body, reads, {}, news, {"acc": ((2 * D, D), BF)}).values())


def total_of(s, tag):
    wide = [s[f"{tag}{k}"][...].astype(F32) for k in range(4)]
    return ((wide[0] + wide[2]) + (wide[1] + wide[3])).astype(BF)


def by_distance(tag, values):
    return {f"{tag}{k}": v for k, v in enumerate(values)}


FQ, TQ = BLK // 4, AQ // 4
SHARD = FQ + TQ


def sum_split(pos, feed, atts):
    def body(s):
        s["att"][...] = total_of(s, "t")
        for k in range(4):
            j = lax.rem(s["pos"][SECOND] + k, 4)
            s[f"p{k}"][:FQ, :] = s["feed"][pl.ds(aligned(j, FQ), FQ), :]
            s[f"p{k}"][FQ:SHARD, :] = s["att"][pl.ds(aligned(j, TQ), TQ), :]
            s[f"p{k}"][SHARD:, :] = s["att"][AQ:, :]

    reads = {"pos": pos, "feed": feed, **by_distance("t", atts)}
    news = {f"p{k}": ((SHARD + VEC, D), BF) for k in range(4)}
    scratch = {"att": ((AQ + VEC, D), BF)}
    return list(kernel("sum_split", body, reads, {}, news, scratch).values())


def sum_four(got, stored=()):
    def body(s):
        s["out"][...] = total_of(s, "g")

    outside = {f"a{i}": v for i, v in enumerate(stored)}
    return kernel("sum_four", body, {**by_distance("g", got), **outside}, {}, {"out": (got[0].shape, BF)}, outside=outside)["out"]


def sum_two(own, got):
    def body(s):
        total = (s["a"][...].astype(F32) + s["b"][...].astype(F32)).astype(BF)
        s["out"][...] = total[:SHARD]
        s["vec"][...] = total[SHARD:]

    got = kernel("sum_two", body, {"a": own, "b": got}, {}, {"out": ((SHARD, D), BF), "vec": ((VEC, D), BF)})
    return got["out"], got["vec"]


HALF = (BLK + AQ) // 2


def join(pos, got, vec):
    def body(s):
        for k in range(4):
            j = lax.rem(s["pos"][SECOND] + (4 - k), 4)
            s["out"][pl.ds(aligned(j, FQ), FQ), :] = s[f"g{k}"][:FQ, :]
            s["out"][pl.ds(aligned(j, TQ) + BLK, TQ), :] = s[f"g{k}"][FQ:, :]
        s["out"][2 * HALF :, :] = s["vec"][...]
        s["up"][...] = s["out"][:HALF, :]
        s["low"][...] = s["out"][HALF : 2 * HALF, :]

    news = {"out": ((2 * HALF + VEC, D), BF), "up": ((HALF, D), BF), "low": ((HALF, D), BF)}
    return kernel("join", body, {"pos": pos, **by_distance("g", got), "vec": vec}, {}, news).values()


MATRICES = ("o", "q", "k", "v")


def pair(one, two):
    def body(s):
        s["out"][:HALF, :] = s["one"][...]
        s["out"][HALF:, :] = s["two"][...]

    return kernel("pair", body, {"one": one, "two": two}, {}, {"out": ((2 * HALF, D), BF)})["out"]


def finish(pos, name, halves, done):
    arrays = []
    for array, *_ in halves:
        arrays += [] if any(array is a for a in arrays) else [array]

    def named(array):
        return "b%d" % [array is a for a in arrays].index(True)

    def body(s):
        started = []

        def move(source, target, sem):
            pltpu.make_async_copy(source, target, s["sems"].at[sem]).start()

        for i, (array, row, mine, k, lower) in enumerate(halves):
            s["wide"][i] = s[named(array)][row : row + HALF, :].astype(F32)
            rest = BLK - HALF if lower else HALF
            feed = s["wide"].at[i, pl.ds(0, rest)]
            piece = lax.rem(s["pos"][FIRST if mine else SECOND] + (4 - k), 4)
            down = (s["pos"][CORE] == 0) if mine else (s["pos"][CORE] == 1)
            at, cols = pl.ds(pl.multiple_of(piece * BLK + lower * HALF, 128), rest), pl.ds(aligned(piece, BLK), BLK)
            pl.when(down)(functools.partial(move, feed, s["down"].at[0, at, :], 2 * i))
            pl.when(jnp.logical_not(down))(functools.partial(move, feed, s["up"].at[0, pl.ds(lower * HALF, rest), cols], 2 * i))
            started.append((feed, s["down"].at[0, pl.ds(0, rest), :], 2 * i))
            if lower:
                att = s["wide"].at[i, pl.ds(rest, AQ)]
                kind = jnp.where(down, 0, 2) + lax.div(piece, 2)
                at = pl.ds(aligned(lax.rem(piece, 2), AQ), AQ)
                for which, n in enumerate(MATRICES):
                    pl.when(kind == which)(functools.partial(move, att, s[n].at[0, at, :], 2 * i + 1))
                started.append((att, s["o"].at[0, pl.ds(0, AQ), :], 2 * i + 1))
        for source, target, sem in started:
            pltpu.make_async_copy(source, target, s["sems"].at[sem]).wait()

    reads = {"pos": pos, **{named(v): v for v in arrays}}
    news = {} if done else {"up": ((1, D, FF), F32), "down": ((1, FF, D), F32), **{n: ((1, D, D), F32) for n in MATRICES}}
    scratch = {"wide": ((len(halves), HALF, D), F32)}
    return kernel(name, body, reads, done, news, scratch, sems=2 * len(halves), outside=("up", "down", *MATRICES))


def hold(values, stored=(), near=()):
    updates = {f"x{i}": v for i, v in enumerate(values)}
    outside = {f"a{i}": v for i, v in enumerate(stored)}
    reads = {**outside, **{f"b{i}": v for i, v in enumerate(near)}}
    return list(kernel("hold", lambda s: None, reads, updates, {}, outside=outside).values())


def store(y, dh):
    def body(s):
        moves = [pltpu.make_async_copy(s[n], s["out_" + n].at[0], s["sems"].at[i]) for i, n in enumerate(("y", "dh"))]
        for move in moves:
            move.start()
        for move in moves:
            move.wait()

    news = {"out_y": ((1, *y.shape), BF), "out_dh": ((1, *dh.shape), F32)}
    got = kernel("store", body, {"y": y, "dh": dh}, {}, news, sems=2, outside=news)
    return got["out_y"], got["out_dh"]


def vector_finish(pos, mine, other):
    def body(s):
        own = (s["pos"][CORE] == 0).astype(F32)
        values = jnp.where(own > 0.5, s["mine"][2 * HALF :, :].astype(F32), s["other"][2 * HALF :, :].astype(F32))
        for i in VECTORS:
            s[str(i)][...] = values[i : i + 1, :]
        for j in range(NBLK):
            s[str(C1)][:, j * BLK : j * BLK + BLK] = values[C1 + j : C1 + j + 1, :]

    news = {**{str(i): ((1, D), F32) for i in VECTORS}, str(C1): ((1, FF), F32)}
    return kernel("vector_finish", body, {"pos": pos, "mine": mine, "other": other}, {}, news, free=news)


def spot(y, z, x, core):
    return ((y * 2 + z) * 4 + x) * 2 + core


def everywhere(move):
    return [(spot(y, z, x, c), spot(*move(y, z, x, c))) for y in range(4) for z in range(2) for x in range(4) for c in range(2)]


def along(stage, distance):
    def move(y, z, x, core):
        if (core == 0) == (stage == 0):
            return y, z, (x + distance) % 4, core
        return (y + distance) % 4, z, x, core

    return everywhere(move)


def send(value, route):
    return lax.ppermute(value, "dp", route)


def to_core(value):
    return send(value, everywhere(lambda y, z, x, core: (y, z, x, 1 - core)))


def to_z(value):
    return send(value, everywhere(lambda y, z, x, core: (y, 1 - z, x, core)))


def spread(pieces, stage):
    sent = {k: send(pieces[k], along(stage, k)) for k in (1, 3, 2)}
    return [pieces[0]] + [sent[k] for k in (1, 2, 3)]


def shards(tokens, segments, cotangent, w_query, q_bias, w_key, w_value, v_bias, w_out, out_bias, ln1_gain, ln1_shift, w_up, up_bias, w_down, down_bias, ln2_gain, ln2_shift):
    dp = lax.axis_index("dp")
    core, x, y = dp % 2, (dp // 2) % 4, dp // 16
    first, second = jnp.where(core == 0, x, y), jnp.where(core == 0, y, x)
    here = jnp.stack([lax.axis_index("section"), core, first, second]).astype(jnp.int32)
    outside = {"in_pos": here, "in_h": tokens, "in_seg": segments, "in_cot": cotangent}
    outside.update(in_wq=w_query, in_wk=w_key, in_wv=w_value, in_wo=w_out, in_w1=w_up, in_w2=w_down)
    vectors = {BQ: q_bias, BV: v_bias, BO: out_bias, G1: ln1_gain, S1: ln1_shift, C2: down_bias, G2: ln2_gain, S2: ln2_shift, C1: up_bias}
    outside.update({f"in_{i}": v for i, v in vectors.items()})

    def forth(value):
        return lax.ppermute(value, "section", [(0, 1)])

    def back(value):
        return lax.ppermute(value, "section", [(1, 0)])

    state = {}
    came, dcame = [], []
    for row in range(ROWS):
        sent, state = first_forward(row, outside, state, jnp.broadcast_to(here[:1], (8, 128)))
        came.append(forth(sent))
    state = first_slopes(state)
    for row in range(ROWS):
        sent, state = second_both(row, came[row], state)
        dcame.append(back(sent))
    pos = state["pos"]

    def flat(*names):
        return {n: state[n].reshape((T2, state[n].shape[-1])) for n in names}

    dresid, state = first_feed(0, dcame[0], state, {})
    state = first_input(0, dresid, first_attention(0, state, {}))
    names = ("u", "a", "o", "h", "e1", "e2", "e0", "dq", "dk", "dv")
    early = first_products(pos, {**flat(*names), "ln": state["ln"], "after": state["dh"]})
    dresid, state = first_feed(1, dcame[1], state, {"after": early["vec"]})
    near, far = (1, 3), (2, 0)
    feed_ops = flat("u", "a", "e1", "e2")
    near_out = feed_send(pos, feed_ops, early["fs"], near, {})
    far_out = feed_send(pos, feed_ops, early["fs"], far, {"after": near_out})
    state = first_attention(1, state, {"after": far_out})
    ops = flat(*names)
    att_out, vec = attention_send(pos, {**ops, "ln": state["ln"]}, early["ts"], early["vec"], {})
    feeds = feed_keep(pos, feed_ops, early["fk"], near, to_core(near_out), {"after": att_out})
    atts = attention_keep(pos, flat("o", "h", "e0", "dq", "dk", "dv"), early["tk"], vec, to_core(att_out))
    feeds.update(feed_keep(pos, feed_ops, early["fk"], far, to_core(far_out), {"after": atts[0]}))
    state = first_input(1, dresid, state)
    y, dh = store(state["y"], state["dh"])
    pieces = sum_split(pos, sum_four(spread([feeds[f"p{k}"] for k in range(4)], 0), [y, dh]), spread(atts, 0))
    mine = sum_four(spread(pieces, 1))
    shard, vec = sum_two(mine, to_z(mine))
    block, up, low = join(pos, spread([shard] * 4, 1), vec)
    up_behind, low_ahead = send(up, along(0, 1)), send(low, along(0, 3))
    low_behind, up_ahead = send(low, along(0, 1)), send(up, along(0, 3))
    other = to_core(block)
    g = vector_finish(pos, block, other)
    own = [(v, h * HALF, mine, 0, h) for v, mine in ((block, True), (other, False)) for h in range(2)]
    full = finish(pos, "finish_own", own, {})
    up_behind, low_ahead = hold([up_behind, low_ahead], [g[str(BQ)], full["up"]])
    opposite = [send(up_behind, along(0, 1)), send(low_ahead, along(0, 3))]
    first = pair(up_behind, low_ahead)
    low_behind, up_ahead = hold([low_behind, up_ahead], near=[up_behind, low_ahead])
    sides = [(up_behind, 0, True, 1, 0), (low_behind, 0, True, 1, 1), (up_ahead, 0, True, 3, 0), (low_ahead, 0, True, 3, 1)]
    full = finish(pos, "finish_sides", sides, full)
    opposite = hold(opposite, [full["up"]])
    others = [to_core(b) for b in opposite]
    first = to_core(first)
    second = [(first, 0, False, 1, 0), (first, HALF, False, 3, 1), (to_core(low_behind), 0, False, 1, 1), (to_core(up_ahead), 0, False, 3, 0)]
    full = finish(pos, "finish_second", second + [(b, 0, True, 2, h) for h, b in enumerate(opposite)], full)
    full = finish(pos, "finish_last", [(b, 0, False, 2, h) for h, b in enumerate(others)], full)

    def vector(i):
        return g[str(i)]

    return (
        y,
        dh,
        full["q"],
        vector(BQ),
        full["k"],
        full["v"],
        vector(BV),
        full["o"],
        vector(BO),
        vector(G1),
        vector(S1),
        full["up"],
        vector(C1),
        full["down"],
        vector(C2),
        vector(G2),
        vector(S2),
    )


def solution(mesh):
    row, matrix, vector = P("dp", None, None), P("section", None, None), P("section", None)
    in_specs = (row, P("dp", None), row, matrix, vector, matrix, matrix, vector, matrix, vector, vector, vector, matrix, vector, matrix, vector, vector, vector)
    big = P("section", "dp", None, None)
    out_specs = (big, big, matrix, vector, matrix, matrix, vector, matrix, vector, vector, vector, matrix, vector, matrix, vector, vector, vector)
    return jax.shard_map(shards, mesh=mesh, in_specs=in_specs, out_specs=out_specs, check_vma=False)
```
